32 devices in a mesh: grp: 16 (over z, y, x), row: 2 (over core).
Axes of the slice: x: 2, y: 2, z: 4, core: 2. Of those that a mesh axis runs over, the one named last changes fastest.
Arguments:
- latents: bfloat16 [16, 4096], P('grp'), may hold values from -6 to 6
- frames: int32 [16], replicated, may hold values from 1 to 4, as said below
- offsets: int32 [16], replicated, may hold values from 0 to 240, as said below
- assign: int32 [16], replicated, may hold values from 0 to 15, each once
- w_in: bfloat16 [16, 27, 384], replicated, may hold values from -0.3125 to 0.3125
- w_mid: bfloat16 [384, 27, 192], P('grp'), may hold values from -0.0625 to 0.0625
- w_out: bfloat16 [192, 27, 96], P('grp'), may hold values from -0.078125 to 0.078125
- gain_in: float32 [384], replicated, may hold values from 0.25 to 1.75
- gain_mid: float32 [192], replicated, may hold values from 0.25 to 1.75
- gain_out: float32 [96], replicated, may hold values from 0.25 to 1.75
Outputs:
- decoded: bfloat16 [16, 4, 16, 6144], P('grp', None, 'row')
The draws below stay inside these ranges and needn't reach their ends.
Inputs may be any that keep to these rules, and one draw needn't show every extreme that they name: Some request has exactly 4 frames. The blocks of different requests do not intersect, and offsets[r] + 16 <= 256 for every request; some request starts at 240. `assign`: every request is decoded by exactly one group.
All inputs are finite; a program needn't handle non-finite values.
Results may differ from the reference program's by a relative error of at most 0.006.
Values may be sent and summed in bfloat16 or wider, within the bound.
No kernel may reach another device: no remote copies, remote signals or barrier semaphores. Data moves between devices by JAX's collectives and lax.ppermute only.
A program may use at most 128 MiB of HBM per device.

```python
import jax
import jax.numpy as jnp
from jax import lax

ZC = 16
C1 = 384
C2 = 192
C3 = 96
WL = 16
FMAX = 4
HL = 4
REQS = 16
SPAN = 4
CAP = 16
BUF = 256
N_GRP = 16


def shared_plan(key):
    plan_key = jax.random.fold_in(key, 11)
    key_base, key_large, key_order = jax.random.split(plan_key, 3)
    base = jax.random.randint(key_base, (REQS,), 1, min(FMAX // 2 + 1, FMAX) + 1, dtype=jnp.int32)
    largest = jax.random.randint(key_large, (), 0, REQS, dtype=jnp.int32)
    counts = jnp.where(jnp.arange(REQS, dtype=jnp.int32) == largest, FMAX, base).astype(jnp.int32)
    order = jax.random.permutation(key_order, REQS)
    lengths = counts[order] * SPAN
    starts = (jnp.cumsum(lengths) - lengths).astype(jnp.int32)
    last = jnp.arange(REQS, dtype=jnp.int32) == REQS - 1
    starts = jnp.where(last, BUF - CAP, starts).astype(jnp.int32)
    placed = jnp.zeros((REQS,), jnp.int32).at[order].set(starts)
    return (counts, placed)


def draw_frames(key, part):
    return shared_plan(key)[0]


def draw_offsets(key, part):
    return shared_plan(key)[1]


def block_levels(key, shape, pieces, smallest, high):
    factor_of, own = 1.0, jax.random.fold_in(key, 6)
    for axis_at, blocks in pieces:
        heights = jnp.exp(jax.random.uniform(jax.random.fold_in(own, axis_at), (blocks,), jnp.float32, smallest / len(pieces), high / len(pieces)))
        factor_of = factor_of * jnp.repeat(heights, shape[axis_at] // blocks).reshape([-1 if axis == axis_at else 1 for axis in range(len(shape))])
    return factor_of


def bell_draw(rng, extent, spread, limit, pieces=(), held_as=jnp.bfloat16):
    loudness = block_levels(rng, extent, pieces, -0.22, 0.18) if pieces else 1.0
    drawn = jax.random.normal(rng, extent, jnp.float32) * spread * loudness
    return jnp.minimum(jnp.maximum(drawn, -limit), limit).astype(held_as)


def setup_inputs(seed: int = 0) -> dict:
    seeds = jax.random.split(jax.random.key(seed), 11)
    return {
        "latents": bell_draw(seeds[0], (N_GRP, BUF * ZC), 1.0, 6.0, ((0, 16),)),
        "frames": draw_frames(jax.random.fold_in(seeds[10], 71), 0),
        "offsets": draw_offsets(jax.random.fold_in(seeds[10], 71), 0),
        "assign": jax.random.permutation(seeds[3], REQS).astype(jnp.int32),
        "w_in": bell_draw(seeds[4], (ZC, 27, C1), (27 * ZC) ** -0.5, 0.3125),
        "w_mid": bell_draw(seeds[5], (C1, 27, C2), (27 * C1) ** -0.5, 0.0625, ((0, 16),)),
        "w_out": bell_draw(seeds[6], (C2, 27, C3), (27 * C2) ** -0.5, 0.078125, ((0, 16),)),
        "gain_in": jnp.clip(1.0 + 0.15 * jax.random.normal(seeds[7], (C1,), jnp.float32), 0.25, 1.75),
        "gain_mid": jnp.clip(1.0 + 0.15 * jax.random.normal(seeds[8], (C2,), jnp.float32), 0.25, 1.75),
        "gain_out": jnp.clip(1.0 + 0.15 * jax.random.normal(seeds[9], (C3,), jnp.float32), 0.25, 1.75),
    }


def rms_silu(hidden, gain):
    mean_sq = lax.optimization_barrier(jnp.mean(hidden * hidden, axis=-1, keepdims=True))
    scaled = hidden * lax.rsqrt(mean_sq + 1e-06) * gain
    return jax.nn.silu(scaled)

def causal_conv(extended, weight):
    count_t = extended.shape[0]
    count_r = extended.shape[1] - 2
    count_c = extended.shape[2]
    width_in = extended.shape[3]
    width_out = weight.shape[2]
    padded = jnp.pad(extended, ((2, 0), (0, 0), (1, 1), (0, 0)))
    total = jnp.zeros((count_t * count_r * count_c, width_out), jnp.float32)
    for time_tap in range(3):
        for row_tap in range(3):
            for col_tap in range(3):
                window = padded[time_tap:time_tap + count_t, row_tap:row_tap + count_r, col_tap:col_tap + count_c]
                window = window.reshape(count_t * count_r * count_c, width_in)
                tap_index = 9 * time_tap + 3 * row_tap + col_tap
                total = total + jnp.dot(window, weight[:, tap_index, :], preferred_element_type=jnp.float32)
    return total.reshape(count_t, count_r, count_c, width_out)

def upsample(values):
    return jnp.repeat(jnp.repeat(values, 2, axis=1), 2, axis=2)

def pad_rows(values):
    return jnp.pad(values, ((0, 0), (1, 1), (0, 0), (0, 0)))

def reference(latents, frames, offsets, assign, w_in, w_mid, w_out, gain_in, gain_mid, gain_out):
    table = latents.reshape(N_GRP, BUF, ZC)
    frame_ids = jnp.arange(FMAX, dtype=jnp.int32)[:, None, None]
    row_ids = jnp.arange(HL, dtype=jnp.int32)[None, :, None]
    col_ids = jnp.arange(WL, dtype=jnp.int32)[None, None, :]
    position = (frame_ids * HL + row_ids) * WL + col_ids

    def decode(group):
        request = assign[group]
        count = frames[request]
        fill_len = count * SPAN
        shard = jnp.minimum(position // fill_len, N_GRP - 1).astype(jnp.int32)
        within = (position % fill_len).astype(jnp.int32)
        tokens = table[shard, offsets[request] + within]
        valid = (frame_ids < count)[..., None]
        latent_in = jnp.where(valid, tokens, jnp.zeros((), jnp.bfloat16)).astype(jnp.bfloat16)
        act_in = rms_silu(causal_conv(pad_rows(latent_in), w_in), gain_in).astype(jnp.bfloat16)
        act_mid = rms_silu(causal_conv(pad_rows(upsample(act_in)), w_mid), gain_mid).astype(jnp.bfloat16)
        final = rms_silu(causal_conv(pad_rows(upsample(act_mid)), w_out), gain_out)
        final = jnp.where(valid, final, jnp.zeros((), jnp.float32))
        return final.astype(jnp.bfloat16).reshape(FMAX, 4 * HL, 4 * WL * C3)
    return lax.map(decode, jnp.arange(N_GRP, dtype=jnp.int32))
```

```python
import functools

import jax
import jax.numpy as jnp
from jax import lax
from jax.experimental import pallas as pl
from jax.experimental.pallas import tpu as pltpu
from jax.sharding import PartitionSpec as P

RL = 2
WL = 16
FMAX = 4


def extended_2(cells, sides, width):
    for axis, dim in sides:
        count = lax.axis_size(axis)
        ends = count - 1
        head = lax.slice_in_dim(cells, 0, width, axis=dim)
        tail = lax.slice_in_dim(cells, cells.shape[dim] - width, cells.shape[dim], axis=dim)
        cells = jnp.concatenate(
            [
                lax.ppermute(tail, axis, [(i, (i + 1) % count) for i in range(ends)]),
                cells,
                lax.ppermute(head, axis, [((i + 1) % count, i) for i in range(ends)]),
            ],
            axis=dim,
        )
    return cells


def rms_silu(hidden, gain):
    mean_sq = jnp.mean(hidden * hidden, axis=-1, keepdims=True)
    scaled = hidden * lax.rsqrt(mean_sq + 1e-06) * gain
    return jax.nn.silu(scaled)


def causal_conv(extended, weight):
    count_t = extended.shape[0]
    count_r = extended.shape[1] - 2
    count_c = extended.shape[2]
    width_in = extended.shape[3]
    width_out = weight.shape[2]
    padded = jnp.pad(extended, ((2, 0), (0, 0), (1, 1), (0, 0)))
    total = jnp.zeros((count_t * count_r * count_c, width_out), jnp.float32)
    for time_tap in range(3):
        for row_tap in range(3):
            for col_tap in range(3):
                window = padded[
                    time_tap : time_tap + count_t,
                    row_tap : row_tap + count_r,
                    col_tap : col_tap + count_c,
                ]
                window = window.reshape(count_t * count_r * count_c, width_in)
                tap_index = 9 * time_tap + 3 * row_tap + col_tap
                total = total + jnp.dot(
                    window, weight[:, tap_index, :], preferred_element_type=jnp.float32
                )
    return total.reshape(count_t, count_r, count_c, width_out)


def upsample(values):
    return jnp.repeat(jnp.repeat(values, 2, axis=1), 2, axis=2)


def per_device_general(latents, frames, offsets, assign, w_in, w_mid, w_out, gain_in, gain_mid, gain_out):
    groups = lax.axis_size("grp")
    row_count = lax.axis_size("row")
    row_index = lax.axis_index("row")
    group_index = lax.axis_index("grp")
    channels = w_in.shape[0]
    cap_vals = latents.shape[1] // groups
    cap_tokens = cap_vals // channels
    span_len = cap_tokens // FMAX
    flat = latents[0]
    slot_ids = jnp.arange(cap_vals, dtype=jnp.int32)

    def select_span(request):
        start = offsets[request] * channels
        block = lax.dynamic_slice_in_dim(flat, start, cap_vals)
        keep = slot_ids < frames[request] * span_len * channels
        return jnp.where(keep, block, jnp.zeros((), block.dtype))

    outgoing = jax.vmap(select_span)(assign)
    incoming = lax.all_to_all(outgoing, "grp", split_axis=0, concat_axis=0, tiled=True)
    table = incoming.reshape(groups * cap_tokens, channels)
    request = assign[group_index]
    count = frames[request]
    fill_len = count * span_len
    image_rows = RL * row_count
    frame_ids = jnp.arange(FMAX, dtype=jnp.int32)[:, None, None]
    row_ids = row_index * RL + jnp.arange(RL, dtype=jnp.int32)[None, :, None]
    col_ids = jnp.arange(WL, dtype=jnp.int32)[None, None, :]
    position = (frame_ids * image_rows + row_ids) * WL + col_ids
    shard = jnp.minimum(position // fill_len, groups - 1)
    within = position % fill_len
    tokens = table[shard * cap_tokens + within]
    valid = (frame_ids < count)[..., None]
    latent_in = jnp.where(valid, tokens, jnp.zeros((), tokens.dtype))
    full_mid, full_out = (
        lax.all_gather(w_mid, "grp", axis=0, tiled=True),
        lax.all_gather(w_out, "grp", axis=0, tiled=True),
    )
    latent_ext = extended_2(latent_in, (("row", 1),), 1)
    act_in = rms_silu(causal_conv(latent_ext, w_in), gain_in).astype(jnp.bfloat16)
    mid_ext = extended_2(upsample(act_in), (("row", 1),), 1)
    act_mid = rms_silu(causal_conv(mid_ext, full_mid), gain_mid).astype(jnp.bfloat16)
    out_ext = extended_2(upsample(act_mid), (("row", 1),), 1)
    final = rms_silu(causal_conv(out_ext, full_out), gain_out)
    final = jnp.where(valid, final, jnp.zeros((), jnp.float32)).astype(jnp.bfloat16)
    return final.reshape(1, FMAX, 4 * RL, 4 * WL * final.shape[3])


LINE = 4
PLANE = 4
ZC, C1, C2, C3 = 16, 384, 192, 96
TOK = 16
IN_SH = C1 // 16
MID_SH = C2 // 16
OUT_BLK = C2 // (2 * LINE)
PIECE_ROWS = 96
W_ROWS = 3 * IN_SH
B_ROWS = LINE * W_ROWS + LINE * LINE
WOUT_LANES = 896
F32, BF16 = jnp.float32, jnp.bfloat16
VMEM = functools.partial(pl.BlockSpec, memory_space=pltpu.VMEM)
SMEM = functools.partial(pl.BlockSpec, memory_space=pltpu.SMEM)


def iota(shape, dim):
    return lax.broadcasted_iota(jnp.int32, shape, dim)


def place():
    group = lax.axis_index("grp")
    return lax.div(group, PLANE), lax.rem(group, PLANE), lax.axis_index("row")


def silu(v):
    return v / (1.0 + jnp.exp(-v))


def dot_nt(lhs, rhs):
    return lax.dot_general(lhs, rhs, (((1,), (1,)), ((), ())), preferred_element_type=F32)


def pack_kernel(offsets, assign, w_ref, lat_ref, *refs):
    outs, (wf, lf, pf) = refs[:LINE], refs[LINE:]
    z, _, c = place()
    wf[:, :, :C2] = w_ref[...].astype(F32)
    lat = lat_ref[...].astype(F32)
    lf[32:40, :] = jnp.zeros((8, 128), F32)
    for j in range(32):
        lf[j : j + 1, :] = lat[:, 128 * j : 128 * j + 128]
    lane1 = iota((1, 128), 1)
    pf[PIECE_ROWS - 8 :, :] = jnp.zeros((8, 256), F32)
    for g in range(16):
        off = offsets[assign[g]]
        row, rem = lax.div(off, 8), lax.rem(off, 8)
        x = pltpu.roll(lf[pl.ds(row, 8), :], lax.rem(128 - ZC * rem, 128), 1)
        keep = lane1 < 128 - ZC * rem
        pf[g : g + 1, 0:128] = jnp.where(keep, x[0:1], x[1:2])
        pf[g : g + 1, 128:256] = jnp.where(keep, x[1:2], x[2:3])
    lane = iota((IN_SH, 256), 1)
    for k in range(LINE):
        first = (lax.rem(z + k, LINE) * 2 + c) * OUT_BLK
        for b in range(3):
            acc = jnp.zeros((IN_SH, 256), F32)
            for j in range(9):
                tap = 9 * (j // 3) + 3 * b + j % 3
                at = OUT_BLK * j
                moved = pltpu.roll(wf[tap], lax.rem(at - first + 256, 256), 1)
                acc = jnp.where((lane >= at) & (lane < at + OUT_BLK), moved, acc)
            pf[TOK + IN_SH * b : TOK + IN_SH * (b + 1), :] = acc
        outs[k][...] = pf[...].astype(BF16)


def pack(offsets, assign, w_mid, latents):
    piece = jax.ShapeDtypeStruct((PIECE_ROWS, 256), BF16)
    return pl.pallas_call(
        pack_kernel,
        out_shape=[piece] * LINE,
        in_specs=[SMEM(), SMEM(), VMEM(), VMEM()],
        out_specs=[VMEM()] * LINE,
        scratch_shapes=[
            pltpu.VMEM((27, IN_SH, 256), F32),
            pltpu.VMEM((40, 128), F32),
            pltpu.VMEM((PIECE_ROWS, 256), F32),
        ],
        compiler_params=pltpu.CompilerParams(vmem_limit_bytes=32 << 20),
        name="pack",
    )(offsets, assign, w_mid, latents)


def join_kernel(*refs):
    pieces, outs, (pf, bf) = refs[:LINE], refs[LINE : LINE + PLANE], refs[LINE + PLANE :]
    _, q, _ = place()
    for k in range(LINE):
        whole = pieces[k][...].astype(F32)
        pf[TOK * k : TOK * (k + 1), :] = whole[:TOK]
        bf[W_ROWS * k : W_ROWS * (k + 1), :] = whole[TOK : TOK + W_ROWS]
    base = LINE * W_ROWS
    for d in range(PLANE):
        for k in range(LINE):
            for line in range(LINE):
                at = base + LINE * k + line
                bf[at : at + 1, :] = pf[pl.ds(TOK * k + PLANE * line + (q ^ d), 1), :]
        outs[d][...] = bf[...].astype(BF16)


def join(pieces):
    out = jax.ShapeDtypeStruct((B_ROWS, 256), BF16)
    return pl.pallas_call(
        join_kernel,
        out_shape=[out] * PLANE,
        in_specs=[VMEM()] * LINE,
        out_specs=[VMEM()] * PLANE,
        scratch_shapes=[pltpu.VMEM((LINE * TOK, 256), F32), pltpu.VMEM((B_ROWS, 256), F32)],
        compiler_params=pltpu.CompilerParams(vmem_limit_bytes=32 << 20),
        name="join",
    )(*pieces)


def mid_kernel(frames, assign, *refs):
    parts, (win_ref, gain_ref), outs = refs[:PLANE], refs[PLANE : PLANE + 2], refs[PLANE + 2 : PLANE + 2 + LINE]
    lt, xs, zlo, zhi, w1, act, wf = refs[PLANE + 2 + LINE :]
    z, q, _ = place()
    base = LINE * W_ROWS
    for d in range(PLANE):
        part = parts[d][...].astype(F32)
        lt[...] = part[base:]
        for k in range(LINE):
            shard = lax.rem(z - k + LINE, LINE) * PLANE + (q ^ d)
            for b in range(3):
                at = W_ROWS * k + IN_SH * b
                wf[b, pl.ds(pl.multiple_of(shard * IN_SH, 8), IN_SH), :] = part[at : at + IN_SH]
            for i in range(LINE):
                xs[i, pl.ds(shard, 1), :] = lt[pl.ds(LINE * k + lax.rem(z + i, LINE), 1), :]
    zero_rows = jnp.zeros((1, 6, WL, 640), BF16)
    zero_cols = jnp.zeros((4, 1, WL, 640), BF16)
    for ref in (zlo, zhi):
        for i in range(LINE):
            ref[i, 0:1] = zero_rows
            ref[i, 1:2] = zero_rows
            ref[i, 2:6, 0:1] = zero_cols
            ref[i, 2:6, 5:6] = zero_cols
    w1[...] = jnp.zeros((640, C1), BF16)
    for n in range(9):
        w1[64 * n : 64 * n + 48, :] = win_ref[48 * n : 48 * n + 48, :]
    lane_n, row_l = iota((256, 640), 1), iota((256, 640), 0)
    spread = ((row_l % ZC == lane_n % ZC) & (lane_n % 64 < 48) & (lane_n < 576)).astype(F32).astype(BF16)
    tap_e = (lane_n % 64) // ZC
    col = row_l % WL
    from_left = (tap_e == 0) & (col > 0)
    from_right = (tap_e == 2) & (col < WL - 1)
    is_mid = tap_e == 1
    low = lane_n % 128 < 64
    pos16, shard16 = iota((256, 16), 0), iota((256, 16), 1)
    pos, tok_l = iota((256, 256), 0).astype(F32), (iota((256, 256), 1) // ZC).astype(F32)
    for i in range(LINE):
        group = lax.rem(z + i, LINE) * PLANE + q
        fill = frames[assign[group]] * (TOK // FMAX)
        hit = (pos16 >= fill * shard16) & (pos16 < fill * (shard16 + 1))
        first = jnp.sum(jnp.where(hit, (fill * shard16).astype(F32), 0.0), axis=1, keepdims=True)
        rows = jnp.dot(hit.astype(F32).astype(BF16), xs[i].astype(BF16), preferred_element_type=F32)
        own = jnp.where(pos - first == tok_l, rows, 0.0).astype(BF16)
        wide = jnp.dot(own, spread, preferred_element_type=F32)
        left, right = pltpu.roll(wide, 1, 0), pltpu.roll(wide, 255, 0)
        cols = jnp.where(is_mid, wide, jnp.where(from_left, left, jnp.where(from_right, right, 0.0)))
        zlo[i, 2:6, 1:5] = jnp.where(low, cols, 0.0).astype(BF16).reshape(4, 4, WL, 640)
        zhi[i, 2:6, 1:5] = jnp.where(low, 0.0, cols).astype(BF16).reshape(4, 4, WL, 640)
        taps = []
        for j in range(5):
            a0, b0 = divmod(2 * j, 3)
            a1, b1 = divmod(min(2 * j + 1, 8), 3)
            at = slice(128 * j, 128 * j + 128)
            tile = zlo[i, a0 : a0 + 4, b0 : b0 + 4, :, at] + zhi[i, a1 : a1 + 4, b1 : b1 + 4, :, at]
            taps.append(tile.reshape(256, 128))
        h = jnp.dot(jnp.concatenate(taps, axis=1), w1[...], preferred_element_type=F32)
        scale = lax.rsqrt(jnp.mean(h * h, axis=1, keepdims=True) + 1e-6)
        act[256 * i : 256 * i + 256, :] = silu(h * scale * gain_ref[...]).astype(BF16)
    lanes = LINE * 256
    at = iota((OUT_BLK, lanes), 1)
    frame, row, column = (at // 64) % FMAX, (at // WL) % 4, at % WL
    summed = []
    for b in range(3):
        prod = dot_nt(wf[b].T.astype(BF16), act[...])
        for e in range(3):
            now, before, two = (prod[OUT_BLK * (3 * a + e) : OUT_BLK * (3 * a + e + 1)] for a in (2, 1, 0))
            summed.append(
                now
                + jnp.where(frame >= 1, pltpu.roll(before, 64, 1), 0.0)
                + jnp.where(frame >= 2, pltpu.roll(two, 128, 1), 0.0)
            )
    halves = [[], []]
    for b in range(3):
        e0, e1, e2 = summed[3 * b : 3 * b + 3]
        halves[0].append(jnp.where(column > 0, pltpu.roll(e0, 1, 1), 0.0) + e1 + e2)
        halves[1].append(e0 + e1 + jnp.where(column < WL - 1, pltpu.roll(e2, lanes - 1, 1), 0.0))
    phases = [None] * 4
    for px in range(2):
        b0, b1, b2 = halves[px]
        phases[px] = jnp.where(row > 0, pltpu.roll(b0, WL, 1), 0.0) + b1 + b2
        phases[2 + px] = b0 + b1 + jnp.where(row < 3, pltpu.roll(b2, lanes - WL, 1), 0.0)
    for i in range(LINE):
        outs[i][...] = jnp.concatenate([p[:, 256 * i : 256 * i + 256] for p in phases], axis=0).astype(BF16)


def mid(frames, assign, parts, w_in, gain_in):
    out = jax.ShapeDtypeStruct((4 * OUT_BLK, 256), BF16)
    return pl.pallas_call(
        mid_kernel,
        out_shape=[out] * LINE,
        in_specs=[SMEM(), SMEM()] + [VMEM()] * (PLANE + 2),
        out_specs=[VMEM()] * LINE,
        scratch_shapes=[
            pltpu.VMEM((LINE * LINE, 256), F32),
            pltpu.VMEM((LINE, 16, 256), F32),
            pltpu.VMEM((LINE, 6, 6, WL, 640), BF16),
            pltpu.VMEM((LINE, 6, 6, WL, 640), BF16),
            pltpu.VMEM((640, C1), BF16),
            pltpu.VMEM((LINE * 256, C1), BF16),
            pltpu.VMEM((3, C1, 256), F32),
        ],
        compiler_params=pltpu.CompilerParams(vmem_limit_bytes=48 << 20),
        name="mid",
    )(frames, assign, *parts, w_in, gain_in)


def wide_kernel(*refs):
    own, other, out, wf = refs[:PLANE], refs[PLANE : 2 * PLANE], refs[2 * PLANE], refs[2 * PLANE + 1]
    z, q, c = place()
    wf[...] = jnp.zeros((768, 1152), F32)
    for side, group in ((c, own), (1 - c, other)):
        for d in range(PLANE):
            for k in range(LINE):
                shard = lax.rem(z - k + LINE, LINE) * PLANE + (q ^ d)
                part = group[d][k].astype(F32)
                for r in range(3):
                    block = side * 3 + r
                    at = lax.div(block, 2) * 256 + shard * 16 + lax.rem(block, 2) * 8
                    at = pl.multiple_of(at, 8)
                    for j in range(9):
                        wf[pl.ds(at, 8), 128 * j : 128 * j + C3] = part[8 * r : 8 * r + 8, C3 * j : C3 * (j + 1)]
    out[...] = wf[...].astype(BF16)


def wide(own, other):
    return pl.pallas_call(
        wide_kernel,
        out_shape=jax.ShapeDtypeStruct((768, 1152), BF16),
        in_specs=[VMEM()] * (2 * PLANE),
        out_specs=VMEM(),
        scratch_shapes=[pltpu.VMEM((768, 1152), F32)],
        compiler_params=pltpu.CompilerParams(vmem_limit_bytes=48 << 20),
        name="wide",
    )(*own, *other)


def out_kernel(frames, assign, *refs):
    own, other, (w_ref, gmid_ref, gout_ref, out_ref) = refs[:LINE], refs[LINE : 2 * LINE], refs[2 * LINE : 2 * LINE + 4]
    hid, lhs, prod = refs[2 * LINE + 4 :]
    z, q, c = place()
    count = frames[assign[z * PLANE + q]]
    hid[...] = jnp.zeros((4, 256, 256), F32)
    for side, group in ((c, own), (1 - c, other)):
        for k in range(LINE):
            block = lax.rem(z - k + LINE, LINE) * 2 + side
            part = group[k][...].astype(F32)
            for p in range(4):
                for half in range(2):
                    at = pl.multiple_of((block * 2 + half) * 16, 16)
                    first = OUT_BLK * p + MID_SH * half
                    hid[p, pl.ds(at, MID_SH), :] = part[first : first + MID_SH]
    acts = []
    for p in range(4):
        h = hid[p]
        scale = lax.rsqrt(jnp.sum(h * h, axis=0, keepdims=True) * (1.0 / C2) + 1e-6)
        acts.append(silu(h * scale * gmid_ref[...]).astype(BF16))
    r, l = iota((256, 256), 0), iota((256, 256), 1)
    same = (r // 8) == ((l // 64) % 2) * WL + l % WL
    mid_row = 2 * ((l // WL) % 4) + l // 128
    for b in range(3):
        wanted = (c * 8 + r % 8 + b - 1) >> 1
        pick = (same & (mid_row == wanted)).astype(F32).astype(BF16)
        for tp in range(2):
            for px in range(2):
                src = jnp.concatenate([acts[2 * py + px][:, 128 * tp : 128 * tp + 128] for py in range(2)], axis=1)
                lhs[tp, px, :, 256 * b : 256 * b + 256] = dot_nt(pick, src).astype(BF16)
    for tp in range(2):
        for px in range(2):
            prod[tp, px] = jnp.dot(lhs[tp, px], w_ref[...], preferred_element_type=F32)
    lane = iota((1, 8, 128), 2)
    below = [lane < 128 - 32 * i for i in range(4)]
    for t in range(FMAX):
        sums = []
        for px in range(2):
            row = []
            for e in range(3):
                total = None
                for a in range(3):
                    s = t + a - 2
                    if s < 0:
                        continue
                    at = 128 * (3 * a + e)
                    term = prod[s // 2, px, 128 * (s % 2) : 128 * (s % 2) + 128, at : at + 128].reshape(WL, 8, 128)
                    total = term if total is None else total + term
                row.append(total)
            sums.append(row)
        zero = jnp.zeros((1, 8, 128), F32)
        after = jnp.concatenate([sums[0][2][1:], zero], axis=0)
        before = jnp.concatenate([zero, sums[1][0][:-1]], axis=0)
        outs = [
            before + sums[0][1] + sums[0][2],
            sums[0][0] + sums[0][1] + sums[1][2],
            sums[0][0] + sums[1][1] + sums[1][2],
            sums[1][0] + sums[1][1] + after,
        ]
        vals = []
        for i, o in enumerate(outs):
            scale = lax.rsqrt(jnp.sum(o * o, axis=2, keepdims=True) * (1.0 / C3) + 1e-6)
            v = jnp.where(t < count, silu(o * scale * gout_ref[...]), 0.0)
            vals.append(pltpu.roll(v, 128 - 32 * i, 2) if i else v)
        tiles = [
            jnp.where(lane < 96, vals[0], vals[1]),
            jnp.where(lane < 64, vals[1], vals[2]),
            jnp.where(lane < 32, vals[2], vals[3]),
        ]
        for x in range(WL):
            both = jnp.concatenate([tile[x] for tile in tiles], axis=1)
            out_ref[0, t, :, 384 * x : 384 * x + 384] = both.astype(BF16)


def finish(frames, assign, own, other, w_out, gain_mid, gain_out):
    return pl.pallas_call(
        out_kernel,
        out_shape=jax.ShapeDtypeStruct((1, FMAX, 4 * RL, 4 * WL * C3), BF16),
        in_specs=[SMEM(), SMEM()] + [VMEM()] * (2 * LINE + 3),
        out_specs=VMEM(),
        scratch_shapes=[
            pltpu.VMEM((4, 256, 256), F32),
            pltpu.VMEM((2, 2, 256, 768), BF16),
            pltpu.VMEM((2, 2, 256, 1152), F32),
        ],
        compiler_params=pltpu.CompilerParams(vmem_limit_bytes=48 << 20),
        name="finish",
    )(frames, assign, *own, *other, w_out, gain_mid, gain_out)


def along_z(value, step):
    return lax.ppermute(value, "grp", [(g, (g + PLANE * step) % (LINE * PLANE)) for g in range(LINE * PLANE)])


def in_plane(value, flip):
    return lax.ppermute(value, "grp", [(g, g ^ flip) for g in range(LINE * PLANE)])


def other_core(value):
    return lax.ppermute(value, "row", [(0, 1), (1, 0)])


def per_device_fast(latents, frames, offsets, assign, w_in, w_mid, w_out, gain_in, gain_mid, gain_out):
    core = lax.axis_index("row")
    pieces = pack(offsets, assign, jnp.transpose(w_mid, (1, 0, 2)), latents)
    pieces = [pieces[0]] + [along_z(pieces[k], k) for k in range(1, LINE)]
    parts = join(pieces)
    parts = [parts[0]] + [in_plane(parts[d], d) for d in range(1, PLANE)]
    rows = w_out.reshape(MID_SH, 3, 3, 3, C3).transpose(2, 0, 1, 3, 4).reshape(3, MID_SH, 9 * C3)
    rows = jnp.pad(rows, ((0, 0), (0, 16 - MID_SH), (0, WOUT_LANES - 9 * C3))).reshape(48, WOUT_LANES)
    half = lax.dynamic_slice_in_dim(rows, core * 24, 24, axis=0)
    line = jnp.stack([half] + [along_z(half, k) for k in range(1, LINE)])
    own = [line] + [in_plane(line, d) for d in range(1, PLANE)]
    other = [other_core(v) for v in own]
    w_last = wide(own, other)
    hidden = mid(frames, assign, parts, w_in.transpose(1, 0, 2).reshape(27 * ZC, C1), gain_in[None, :])
    hidden = [hidden[0]] + [along_z(hidden[k], k) for k in range(1, LINE)]
    swapped = [other_core(v) for v in hidden]
    gmid = jnp.pad(gain_mid.reshape(16, MID_SH), ((0, 0), (0, 16 - MID_SH))).reshape(256, 1)
    gout = jnp.pad(gain_out, (0, 128 - C3)).reshape(1, 128)
    return finish(frames, assign, hidden, swapped, w_last, gmid, gout)


def solution(mesh):
    fast = mesh.shape["grp"] == LINE * PLANE and mesh.shape["row"] == 2
    placed = (
        P("grp", None),
        P(),
        P(),
        P(),
        P(),
        P("grp", None, None),
        P("grp", None, None),
        P(),
        P(),
        P(),
    )
    return jax.shard_map(
        per_device_fast if fast else per_device_general,
        mesh=mesh,
        in_specs=placed,
        out_specs=P("grp", None, "row", None),
        check_vma=False,
    )
```

```python
import functools

import jax
import jax.numpy as jnp
from jax import lax
from jax.experimental import pallas as pl
from jax.experimental.pallas import tpu as pltpu
from jax.sharding import PartitionSpec as P

RL = 2
WL = 16
FMAX = 4


def extended_2(cells, sides, width):
    for axis, dim in sides:
        count = lax.axis_size(axis)
        ends = count - 1
        head = lax.slice_in_dim(cells, 0, width, axis=dim)
        tail = lax.slice_in_dim(cells, cells.shape[dim] - width, cells.shape[dim], axis=dim)
        cells = jnp.concatenate(
            [
                lax.ppermute(tail, axis, [(i, (i + 1) % count) for i in range(ends)]),
                cells,
                lax.ppermute(head, axis, [((i + 1) % count, i) for i in range(ends)]),
            ],
            axis=dim,
        )
    return cells


def rms_silu(hidden, gain):
    mean_sq = jnp.mean(hidden * hidden, axis=-1, keepdims=True)
    scaled = hidden * lax.rsqrt(mean_sq + 1e-06) * gain
    return jax.nn.silu(scaled)


def causal_conv(extended, weight):
    count_t = extended.shape[0]
    count_r = extended.shape[1] - 2
    count_c = extended.shape[2]
    width_in = extended.shape[3]
    width_out = weight.shape[2]
    padded = jnp.pad(extended, ((2, 0), (0, 0), (1, 1), (0, 0)))
    total = jnp.zeros((count_t * count_r * count_c, width_out), jnp.float32)
    for time_tap in range(3):
        for row_tap in range(3):
            for col_tap in range(3):
                window = padded[
                    time_tap : time_tap + count_t,
                    row_tap : row_tap + count_r,
                    col_tap : col_tap + count_c,
                ]
                window = window.reshape(count_t * count_r * count_c, width_in)
                tap_index = 9 * time_tap + 3 * row_tap + col_tap
                total = total + jnp.dot(
                    window, weight[:, tap_index, :], preferred_element_type=jnp.float32
                )
    return total.reshape(count_t, count_r, count_c, width_out)


def upsample(values):
    return jnp.repeat(jnp.repeat(values, 2, axis=1), 2, axis=2)


def per_device_general(latents, frames, offsets, assign, w_in, w_mid, w_out, gain_in, gain_mid, gain_out):
    groups = lax.axis_size("grp")
    row_count = lax.axis_size("row")
    row_index = lax.axis_index("row")
    group_index = lax.axis_index("grp")
    channels = w_in.shape[0]
    cap_vals = latents.shape[1] // groups
    cap_tokens = cap_vals // channels
    span_len = cap_tokens // FMAX
    flat = latents[0]
    slot_ids = jnp.arange(cap_vals, dtype=jnp.int32)

    def select_span(request):
        start = offsets[request] * channels
        block = lax.dynamic_slice_in_dim(flat, start, cap_vals)
        keep = slot_ids < frames[request] * span_len * channels
        return jnp.where(keep, block, jnp.zeros((), block.dtype))

    outgoing = jax.vmap(select_span)(assign)
    incoming = lax.all_to_all(outgoing, "grp", split_axis=0, concat_axis=0, tiled=True)
    table = incoming.reshape(groups * cap_tokens, channels)
    request = assign[group_index]
    count = frames[request]
    fill_len = count * span_len
    image_rows = RL * row_count
    frame_ids = jnp.arange(FMAX, dtype=jnp.int32)[:, None, None]
    row_ids = row_index * RL + jnp.arange(RL, dtype=jnp.int32)[None, :, None]
    col_ids = jnp.arange(WL, dtype=jnp.int32)[None, None, :]
    position = (frame_ids * image_rows + row_ids) * WL + col_ids
    shard = jnp.minimum(position // fill_len, groups - 1)
    within = position % fill_len
    tokens = table[shard * cap_tokens + within]
    valid = (frame_ids < count)[..., None]
    latent_in = jnp.where(valid, tokens, jnp.zeros((), tokens.dtype))
    full_mid, full_out = (
        lax.all_gather(w_mid, "grp", axis=0, tiled=True),
        lax.all_gather(w_out, "grp", axis=0, tiled=True),
    )
    latent_ext = extended_2(latent_in, (("row", 1),), 1)
    act_in = rms_silu(causal_conv(latent_ext, w_in), gain_in).astype(jnp.bfloat16)
    mid_ext = extended_2(upsample(act_in), (("row", 1),), 1)
    act_mid = rms_silu(causal_conv(mid_ext, full_mid), gain_mid).astype(jnp.bfloat16)
    out_ext = extended_2(upsample(act_mid), (("row", 1),), 1)
    final = rms_silu(causal_conv(out_ext, full_out), gain_out)
    final = jnp.where(valid, final, jnp.zeros((), jnp.float32)).astype(jnp.bfloat16)
    return final.reshape(1, FMAX, 4 * RL, 4 * WL * final.shape[3])


LINE = 4
PLANE = 4
ZC, C1, C2, C3 = 16, 384, 192, 96
TOK = 16
IN_SH = C1 // 16
MID_SH = C2 // 16
OUT_BLK = C2 // (2 * LINE)
PIECE_ROWS = 96
W_ROWS = 3 * IN_SH
B_ROWS = LINE * W_ROWS + LINE * LINE
WOUT_LANES = 896
F32, BF16 = jnp.float32, jnp.bfloat16
VMEM = functools.partial(pl.BlockSpec, memory_space=pltpu.VMEM)
SMEM = functools.partial(pl.BlockSpec, memory_space=pltpu.SMEM)
HBM = functools.partial(pl.BlockSpec, memory_space=pltpu.HBM)


def cost(us):
    return pl.CostEstimate(flops=int(us * 1.15e9), bytes_accessed=0, transcendentals=0)


def iota(shape, dim):
    return lax.broadcasted_iota(jnp.int32, shape, dim)


def place():
    group = lax.axis_index("grp")
    return lax.div(group, PLANE), lax.rem(group, PLANE), lax.axis_index("row")


def silu(v):
    return v / (1.0 + jnp.exp(-v))


def dot_nt(lhs, rhs):
    return lax.dot_general(lhs, rhs, (((1,), (1,)), ((), ())), preferred_element_type=F32)


def pack_kernel(offsets_hbm, assign_hbm, w_hbm, lat_hbm, *refs):
    outs, (wf, lf, pf, w_ref, lat_ref, offsets, assign, sems) = refs[:LINE], refs[LINE:]
    moves = [(offsets_hbm, offsets), (assign_hbm, assign), (lat_hbm, lat_ref), (w_hbm, w_ref)]
    copies = [pltpu.make_async_copy(src, dst, sems.at[i]) for i, (src, dst) in enumerate(moves)]
    for copy in copies:
        copy.start()
    z, _, c = place()
    for copy in copies:
        copy.wait()
    wf[:, :, :C2] = w_ref[...].astype(F32)
    lat = lat_ref[...].astype(F32)
    lf[32:40, :] = jnp.zeros((8, 128), F32)
    for j in range(32):
        lf[j : j + 1, :] = lat[:, 128 * j : 128 * j + 128]
    lane1 = iota((1, 128), 1)
    pf[PIECE_ROWS - 8 :, :] = jnp.zeros((8, 256), F32)
    for g in range(16):
        off = offsets[assign[g]]
        row, rem = lax.div(off, 8), lax.rem(off, 8)
        x = pltpu.roll(lf[pl.ds(row, 8), :], lax.rem(128 - ZC * rem, 128), 1)
        keep = lane1 < 128 - ZC * rem
        pf[g : g + 1, 0:128] = jnp.where(keep, x[0:1], x[1:2])
        pf[g : g + 1, 128:256] = jnp.where(keep, x[1:2], x[2:3])
    lane = iota((IN_SH, 256), 1)
    for k in range(LINE):
        first = (lax.rem(z + k, LINE) * 2 + c) * OUT_BLK
        for b in range(3):
            acc = jnp.zeros((IN_SH, 256), F32)
            for j in range(9):
                tap = 9 * (j // 3) + 3 * b + j % 3
                at = OUT_BLK * j
                moved = pltpu.roll(wf[tap], lax.rem(at - first + 256, 256), 1)
                acc = jnp.where((lane >= at) & (lane < at + OUT_BLK), moved, acc)
            pf[TOK + IN_SH * b : TOK + IN_SH * (b + 1), :] = acc
        outs[k][...] = pf[...].astype(BF16)


def pack(offsets, assign, w_mid, latents):
    piece = jax.ShapeDtypeStruct((PIECE_ROWS, 256), BF16)
    return pl.pallas_call(
        pack_kernel,
        out_shape=[piece] * LINE,
        in_specs=[HBM()] * 4,
        out_specs=[VMEM()] * LINE,
        scratch_shapes=[
            pltpu.VMEM((27, IN_SH, 256), F32),
            pltpu.VMEM((40, 128), F32),
            pltpu.VMEM((PIECE_ROWS, 256), F32),
            pltpu.VMEM((27, IN_SH, C2), BF16),
            pltpu.VMEM(latents.shape, BF16),
            pltpu.SMEM(offsets.shape, jnp.int32),
            pltpu.SMEM(assign.shape, jnp.int32),
            pltpu.SemaphoreType.DMA((4,)),
        ],
        cost_estimate=cost(2),
        compiler_params=pltpu.CompilerParams(vmem_limit_bytes=32 << 20),
        name="pack",
    )(*(pltpu.with_memory_space_constraint(v, pltpu.HBM) for v in (offsets, assign, w_mid, latents)))


def join_kernel(*refs):
    pieces, outs, (pf, bf) = refs[:LINE], refs[LINE : LINE + PLANE], refs[LINE + PLANE :]
    _, q, _ = place()
    for k in range(LINE):
        whole = pieces[k][...].astype(F32)
        pf[TOK * k : TOK * (k + 1), :] = whole[:TOK]
        bf[W_ROWS * k : W_ROWS * (k + 1), :] = whole[TOK : TOK + W_ROWS]
    base = LINE * W_ROWS
    for d in range(PLANE):
        for k in range(LINE):
            for line in range(LINE):
                at = base + LINE * k + line
                bf[at : at + 1, :] = pf[pl.ds(TOK * k + PLANE * line + (q ^ d), 1), :]
        outs[d][...] = bf[...].astype(BF16)


def join(pieces):
    out = jax.ShapeDtypeStruct((B_ROWS, 256), BF16)
    return pl.pallas_call(
        join_kernel,
        out_shape=[out] * PLANE,
        in_specs=[VMEM()] * LINE,
        out_specs=[VMEM()] * PLANE,
        scratch_shapes=[pltpu.VMEM((LINE * TOK, 256), F32), pltpu.VMEM((B_ROWS, 256), F32)],
        compiler_params=pltpu.CompilerParams(vmem_limit_bytes=32 << 20),
        cost_estimate=cost(5),
        name="join",
    )(*pieces)


def mid_kernel(frames, assign, *refs):
    parts, (win_ref, gain_ref), outs = refs[:PLANE], refs[PLANE : PLANE + 2], refs[PLANE + 2 : PLANE + 2 + LINE]
    lt, xs, zlo, zhi, w1, act, wf = refs[PLANE + 2 + LINE :]
    z, q, _ = place()
    base = LINE * W_ROWS
    for d in range(PLANE):
        part = parts[d][...].astype(F32)
        lt[...] = part[base:]
        for k in range(LINE):
            shard = lax.rem(z - k + LINE, LINE) * PLANE + (q ^ d)
            for b in range(3):
                at = W_ROWS * k + IN_SH * b
                wf[b, pl.ds(pl.multiple_of(shard * IN_SH, 8), IN_SH), :] = part[at : at + IN_SH]
            for i in range(LINE):
                xs[i, pl.ds(shard, 1), :] = lt[pl.ds(LINE * k + lax.rem(z + i, LINE), 1), :]
    zero_rows = jnp.zeros((1, 6, WL, 640), BF16)
    zero_cols = jnp.zeros((4, 1, WL, 640), BF16)
    for ref in (zlo, zhi):
        for i in range(LINE):
            ref[i, 0:1] = zero_rows
            ref[i, 1:2] = zero_rows
            ref[i, 2:6, 0:1] = zero_cols
            ref[i, 2:6, 5:6] = zero_cols
    w1[...] = jnp.zeros((640, C1), BF16)
    for n in range(9):
        w1[64 * n : 64 * n + 48, :] = win_ref[48 * n : 48 * n + 48, :]
    lane_n, row_l = iota((256, 640), 1), iota((256, 640), 0)
    spread = ((row_l % ZC == lane_n % ZC) & (lane_n % 64 < 48) & (lane_n < 576)).astype(F32).astype(BF16)
    tap_e = (lane_n % 64) // ZC
    col = row_l % WL
    from_left = (tap_e == 0) & (col > 0)
    from_right = (tap_e == 2) & (col < WL - 1)
    is_mid = tap_e == 1
    low = lane_n % 128 < 64
    pos16, shard16 = iota((256, 16), 0), iota((256, 16), 1)
    pos, tok_l = iota((256, 256), 0).astype(F32), (iota((256, 256), 1) // ZC).astype(F32)
    for i in range(LINE):
        group = lax.rem(z + i, LINE) * PLANE + q
        fill = frames[assign[group]] * (TOK // FMAX)
        hit = (pos16 >= fill * shard16) & (pos16 < fill * (shard16 + 1))
        first = jnp.sum(jnp.where(hit, (fill * shard16).astype(F32), 0.0), axis=1, keepdims=True)
        rows = jnp.dot(hit.astype(F32).astype(BF16), xs[i].astype(BF16), preferred_element_type=F32)
        own = jnp.where(pos - first == tok_l, rows, 0.0).astype(BF16)
        wide = jnp.dot(own, spread, preferred_element_type=F32)
        left, right = pltpu.roll(wide, 1, 0), pltpu.roll(wide, 255, 0)
        cols = jnp.where(is_mid, wide, jnp.where(from_left, left, jnp.where(from_right, right, 0.0)))
        zlo[i, 2:6, 1:5] = jnp.where(low, cols, 0.0).astype(BF16).reshape(4, 4, WL, 640)
        zhi[i, 2:6, 1:5] = jnp.where(low, 0.0, cols).astype(BF16).reshape(4, 4, WL, 640)
        taps = []
        for j in range(5):
            a0, b0 = divmod(2 * j, 3)
            a1, b1 = divmod(min(2 * j + 1, 8), 3)
            at = slice(128 * j, 128 * j + 128)
            tile = zlo[i, a0 : a0 + 4, b0 : b0 + 4, :, at] + zhi[i, a1 : a1 + 4, b1 : b1 + 4, :, at]
            taps.append(tile.reshape(256, 128))
        h = jnp.dot(jnp.concatenate(taps, axis=1), w1[...], preferred_element_type=F32)
        scale = lax.rsqrt(jnp.mean(h * h, axis=1, keepdims=True) + 1e-6)
        act[256 * i : 256 * i + 256, :] = silu(h * scale * gain_ref[...]).astype(BF16)
    lanes = LINE * 256
    at = iota((OUT_BLK, lanes), 1)
    frame, row, column = (at // 64) % FMAX, (at // WL) % 4, at % WL
    summed = []
    for b in range(3):
        prod = dot_nt(wf[b].T.astype(BF16), act[...])
        for e in range(3):
            now, before, two = (prod[OUT_BLK * (3 * a + e) : OUT_BLK * (3 * a + e + 1)] for a in (2, 1, 0))
            summed.append(
                now
                + jnp.where(frame >= 1, pltpu.roll(before, 64, 1), 0.0)
                + jnp.where(frame >= 2, pltpu.roll(two, 128, 1), 0.0)
            )
    halves = [[], []]
    for b in range(3):
        e0, e1, e2 = summed[3 * b : 3 * b + 3]
        halves[0].append(jnp.where(column > 0, pltpu.roll(e0, 1, 1), 0.0) + e1 + e2)
        halves[1].append(e0 + e1 + jnp.where(column < WL - 1, pltpu.roll(e2, lanes - 1, 1), 0.0))
    phases = [None] * 4
    for px in range(2):
        b0, b1, b2 = halves[px]
        phases[px] = jnp.where(row > 0, pltpu.roll(b0, WL, 1), 0.0) + b1 + b2
        phases[2 + px] = b0 + b1 + jnp.where(row < 3, pltpu.roll(b2, lanes - WL, 1), 0.0)
    for i in range(LINE):
        outs[i][...] = jnp.concatenate([p[:, 256 * i : 256 * i + 256] for p in phases], axis=0).astype(BF16)


def mid(frames, assign, parts, w_in, gain_in):
    out = jax.ShapeDtypeStruct((4 * OUT_BLK, 256), BF16)
    return pl.pallas_call(
        mid_kernel,
        out_shape=[out] * LINE,
        in_specs=[SMEM(), SMEM()] + [VMEM()] * (PLANE + 2),
        out_specs=[VMEM()] * LINE,
        scratch_shapes=[
            pltpu.VMEM((LINE * LINE, 256), F32),
            pltpu.VMEM((LINE, 16, 256), F32),
            pltpu.VMEM((LINE, 6, 6, WL, 640), BF16),
            pltpu.VMEM((LINE, 6, 6, WL, 640), BF16),
            pltpu.VMEM((640, C1), BF16),
            pltpu.VMEM((LINE * 256, C1), BF16),
            pltpu.VMEM((3, C1, 256), F32),
        ],
        compiler_params=pltpu.CompilerParams(vmem_limit_bytes=48 << 20),
        cost_estimate=cost(5),
        name="mid",
    )(frames, assign, *parts, w_in, gain_in)


def wide_kernel(*refs):
    parts, out, wf = refs[:PLANE], refs[PLANE], refs[PLANE + 1]
    z, q, _ = place()
    wf[...] = jnp.zeros((384, 1152), F32)
    for d in range(PLANE):
        for k in range(LINE):
            shard = lax.rem(z - k + LINE, LINE) * PLANE + (q ^ d)
            at = pl.multiple_of(shard * 8, 8)
            part = parts[d][k].astype(F32)
            for r in range(3):
                for j in range(9):
                    wf[pl.ds(128 * r + at, 8), 128 * j : 128 * j + C3] = part[8 * r : 8 * r + 8, C3 * j : C3 * (j + 1)]
    out[...] = wf[...].astype(BF16)


def wide(parts):
    return pl.pallas_call(
        wide_kernel,
        out_shape=jax.ShapeDtypeStruct((384, 1152), BF16),
        in_specs=[VMEM()] * PLANE,
        out_specs=VMEM(),
        scratch_shapes=[pltpu.VMEM((384, 1152), F32)],
        cost_estimate=cost(0.5),
        compiler_params=pltpu.CompilerParams(vmem_limit_bytes=48 << 20),
        name="wide",
    )(*parts)


def stack_kernel(*refs):
    rows = refs[0].shape[0]
    for i, ref in enumerate(refs[:-1]):
        refs[-1][rows * i : rows * (i + 1), :] = ref[...]


def stack(parts):
    rows, lanes = parts[0].shape
    return pl.pallas_call(
        stack_kernel,
        out_shape=jax.ShapeDtypeStruct((len(parts) * rows, lanes), BF16),
        in_specs=[VMEM()] * len(parts),
        out_specs=VMEM(),
        cost_estimate=cost(5),
        compiler_params=pltpu.CompilerParams(vmem_limit_bytes=32 << 20),
        name="stack",
    )(*parts)


def out_kernel(frames, assign, *refs):
    own, other, w_own, w_other, gmid_ref, gout_ref, out_ref, hid, lhs, prod = refs
    z, q, c = place()
    count = frames[assign[z * PLANE + q]]
    hid[...] = jnp.zeros((4, 256, 256), F32)
    for side, group in ((c, own), (1 - c, other)):
        for k in range(LINE):
            block = lax.rem(z - k + LINE, LINE) * 2 + side
            part = group[96 * k : 96 * k + 96, :].astype(F32)
            for p in range(4):
                for half in range(2):
                    at = pl.multiple_of((block * 2 + half) * 8, 8)
                    first = OUT_BLK * p + MID_SH * half
                    hid[p, pl.ds(at, 8), :] = part[first : first + 8]
                    hid[p, pl.ds(128 + at, 4), :] = part[first + 8 : first + MID_SH]
    acts = []
    for p in range(4):
        h = hid[p]
        scale = lax.rsqrt(jnp.sum(h * h, axis=0, keepdims=True) * (1.0 / C2) + 1e-6)
        acts.append(silu(h * scale * gmid_ref[...]).astype(BF16))
    r, l = iota((256, 256), 0), iota((256, 256), 1)
    same = (r // 8) == ((l // 64) % 2) * WL + l % WL
    mid_row = 2 * ((l // WL) % 4) + l // 128
    for b in range(3):
        wanted = (c * 8 + r % 8 + b - 1) >> 1
        pick = (same & (mid_row == wanted)).astype(F32).astype(BF16)
        for tp in range(2):
            for px in range(2):
                src = jnp.concatenate([acts[2 * py + px][:, 128 * tp : 128 * tp + 128] for py in range(2)], axis=1)
                lhs[tp, px, :, 256 * b : 256 * b + 256] = dot_nt(pick, src).astype(BF16)
    for tp in range(2):
        for px in range(2):
            prod[tp, px] = jnp.dot(
                lhs[tp, px, :, pl.ds(pl.multiple_of(c * 384, 128), 384)], w_own[...], preferred_element_type=F32
            ) + jnp.dot(
                lhs[tp, px, :, pl.ds(pl.multiple_of((1 - c) * 384, 128), 384)], w_other[...], preferred_element_type=F32
            )
    lane = iota((1, 8, 128), 2)
    below = [lane < 128 - 32 * i for i in range(4)]
    for t in range(FMAX):
        sums = []
        for px in range(2):
            row = []
            for e in range(3):
                total = None
                for a in range(3):
                    s = t + a - 2
                    if s < 0:
                        continue
                    at = 128 * (3 * a + e)
                    term = prod[s // 2, px, 128 * (s % 2) : 128 * (s % 2) + 128, at : at + 128].reshape(WL, 8, 128)
                    total = term if total is None else total + term
                row.append(total)
            sums.append(row)
        zero = jnp.zeros((1, 8, 128), F32)
        after = jnp.concatenate([sums[0][2][1:], zero], axis=0)
        before = jnp.concatenate([zero, sums[1][0][:-1]], axis=0)
        outs = [
            before + sums[0][1] + sums[0][2],
            sums[0][0] + sums[0][1] + sums[1][2],
            sums[0][0] + sums[1][1] + sums[1][2],
            sums[1][0] + sums[1][1] + after,
        ]
        vals = []
        for i, o in enumerate(outs):
            scale = lax.rsqrt(jnp.sum(o * o, axis=2, keepdims=True) * (1.0 / C3) + 1e-6)
            v = jnp.where(t < count, silu(o * scale * gout_ref[...]), 0.0)
            vals.append(pltpu.roll(v, 128 - 32 * i, 2) if i else v)
        tiles = [
            jnp.where(lane < 96, vals[0], vals[1]),
            jnp.where(lane < 64, vals[1], vals[2]),
            jnp.where(lane < 32, vals[2], vals[3]),
        ]
        for x in range(WL):
            both = jnp.concatenate([tile[x] for tile in tiles], axis=1)
            out_ref[0, t, :, 384 * x : 384 * x + 384] = both.astype(BF16)


def finish(frames, assign, *rest):
    return pl.pallas_call(
        out_kernel,
        out_shape=jax.ShapeDtypeStruct((1, FMAX, 4 * RL, 4 * WL * C3), BF16),
        in_specs=[SMEM(), SMEM()] + [VMEM()] * len(rest),
        out_specs=VMEM(),
        scratch_shapes=[
            pltpu.VMEM((4, 256, 256), F32),
            pltpu.VMEM((2, 2, 256, 768), BF16),
            pltpu.VMEM((2, 2, 256, 1152), F32),
        ],
        compiler_params=pltpu.CompilerParams(vmem_limit_bytes=48 << 20),
        cost_estimate=cost(4.8),
        name="finish",
    )(frames, assign, *rest)


def along_z(value, step):
    return lax.ppermute(value, "grp", [(g, (g + PLANE * step) % (LINE * PLANE)) for g in range(LINE * PLANE)])


def in_plane(value, flip):
    return lax.ppermute(value, "grp", [(g, g ^ flip) for g in range(LINE * PLANE)])


def other_core(value):
    return lax.ppermute(value, "row", [(0, 1), (1, 0)])


def per_device_fast(latents, frames, offsets, assign, w_in, w_mid, w_out, gain_in, gain_mid, gain_out):
    core = lax.axis_index("row")
    pieces = pack(offsets, assign, jnp.transpose(w_mid, (1, 0, 2)), latents)
    pieces = [pieces[0]] + [along_z(pieces[k], k) for k in range(1, LINE)]
    parts = join(pieces)
    parts = [parts[0]] + [in_plane(parts[d], d) for d in range(1, PLANE)]
    rows = w_out.reshape(MID_SH, 3, 3, 3, C3).transpose(2, 0, 1, 3, 4).reshape(3, MID_SH, 9 * C3)
    rows = jnp.pad(rows, ((0, 0), (0, 16 - MID_SH), (0, WOUT_LANES - 9 * C3))).reshape(48, WOUT_LANES)
    half = lax.dynamic_slice_in_dim(rows, core * 24, 24, axis=0)
    line = stack([half] + [along_z(half, k) for k in range(1, LINE)]).reshape(LINE, 24, WOUT_LANES)
    own = [line] + [in_plane(line, d) for d in range(1, PLANE)]
    hidden = mid(frames, assign, parts, w_in.transpose(1, 0, 2).reshape(27 * ZC, C1), gain_in[None, :])
    own, _ = lax.optimization_barrier((own, hidden[0]))
    w_last = wide(own)
    hidden = stack([hidden[0]] + [along_z(hidden[k], k) for k in range(1, LINE)])
    gmid = jnp.pad(gain_mid.reshape(16, MID_SH), ((0, 0), (0, 16 - MID_SH)))
    gmid = jnp.concatenate([gmid[:, :8], gmid[:, 8:]]).reshape(256, 1)
    gout = jnp.pad(gain_out, (0, 128 - C3)).reshape(1, 128)
    return finish(frames, assign, hidden, other_core(hidden), w_last, other_core(w_last), gmid, gout)


def solution(mesh):
    fast = mesh.shape["grp"] == LINE * PLANE and mesh.shape["row"] == 2
    placed = (
        P("grp", None),
        P(),
        P(),
        P(),
        P(),
        P("grp", None, None),
        P("grp", None, None),
        P(),
        P(),
        P(),
    )
    return jax.shard_map(
        per_device_fast if fast else per_device_general,
        mesh=mesh,
        in_specs=placed,
        out_specs=P("grp", None, "row", None),
        check_vma=False,
    )
```

```python
import functools

import jax
import jax.numpy as jnp
from jax import lax
from jax.experimental import pallas as pl
from jax.experimental.pallas import tpu as pltpu
from jax.sharding import PartitionSpec as P

RL = 2
WL = 16
FMAX = 4


def extended_2(cells, sides, width):
    for axis, dim in sides:
        count = lax.axis_size(axis)
        ends = count - 1
        head = lax.slice_in_dim(cells, 0, width, axis=dim)
        tail = lax.slice_in_dim(cells, cells.shape[dim] - width, cells.shape[dim], axis=dim)
        cells = jnp.concatenate(
            [
                lax.ppermute(tail, axis, [(i, (i + 1) % count) for i in range(ends)]),
                cells,
                lax.ppermute(head, axis, [((i + 1) % count, i) for i in range(ends)]),
            ],
            axis=dim,
        )
    return cells


def rms_silu(hidden, gain):
    mean_sq = jnp.mean(hidden * hidden, axis=-1, keepdims=True)
    scaled = hidden * lax.rsqrt(mean_sq + 1e-06) * gain
    return jax.nn.silu(scaled)


def causal_conv(extended, weight):
    count_t = extended.shape[0]
    count_r = extended.shape[1] - 2
    count_c = extended.shape[2]
    width_in = extended.shape[3]
    width_out = weight.shape[2]
    padded = jnp.pad(extended, ((2, 0), (0, 0), (1, 1), (0, 0)))
    total = jnp.zeros((count_t * count_r * count_c, width_out), jnp.float32)
    for time_tap in range(3):
        for row_tap in range(3):
            for col_tap in range(3):
                window = padded[
                    time_tap : time_tap + count_t,
                    row_tap : row_tap + count_r,
                    col_tap : col_tap + count_c,
                ]
                window = window.reshape(count_t * count_r * count_c, width_in)
                tap_index = 9 * time_tap + 3 * row_tap + col_tap
                total = total + jnp.dot(
                    window, weight[:, tap_index, :], preferred_element_type=jnp.float32
                )
    return total.reshape(count_t, count_r, count_c, width_out)


def upsample(values):
    return jnp.repeat(jnp.repeat(values, 2, axis=1), 2, axis=2)


def per_device_general(latents, frames, offsets, assign, w_in, w_mid, w_out, gain_in, gain_mid, gain_out):
    groups = lax.axis_size("grp")
    row_count = lax.axis_size("row")
    row_index = lax.axis_index("row")
    group_index = lax.axis_index("grp")
    channels = w_in.shape[0]
    cap_vals = latents.shape[1] // groups
    cap_tokens = cap_vals // channels
    span_len = cap_tokens // FMAX
    flat = latents[0]
    slot_ids = jnp.arange(cap_vals, dtype=jnp.int32)

    def select_span(request):
        start = offsets[request] * channels
        block = lax.dynamic_slice_in_dim(flat, start, cap_vals)
        keep = slot_ids < frames[request] * span_len * channels
        return jnp.where(keep, block, jnp.zeros((), block.dtype))

    outgoing = jax.vmap(select_span)(assign)
    incoming = lax.all_to_all(outgoing, "grp", split_axis=0, concat_axis=0, tiled=True)
    table = incoming.reshape(groups * cap_tokens, channels)
    request = assign[group_index]
    count = frames[request]
    fill_len = count * span_len
    image_rows = RL * row_count
    frame_ids = jnp.arange(FMAX, dtype=jnp.int32)[:, None, None]
    row_ids = row_index * RL + jnp.arange(RL, dtype=jnp.int32)[None, :, None]
    col_ids = jnp.arange(WL, dtype=jnp.int32)[None, None, :]
    position = (frame_ids * image_rows + row_ids) * WL + col_ids
    shard = jnp.minimum(position // fill_len, groups - 1)
    within = position % fill_len
    tokens = table[shard * cap_tokens + within]
    valid = (frame_ids < count)[..., None]
    latent_in = jnp.where(valid, tokens, jnp.zeros((), tokens.dtype))
    full_mid, full_out = (
        lax.all_gather(w_mid, "grp", axis=0, tiled=True),
        lax.all_gather(w_out, "grp", axis=0, tiled=True),
    )
    latent_ext = extended_2(latent_in, (("row", 1),), 1)
    act_in = rms_silu(causal_conv(latent_ext, w_in), gain_in).astype(jnp.bfloat16)
    mid_ext = extended_2(upsample(act_in), (("row", 1),), 1)
    act_mid = rms_silu(causal_conv(mid_ext, full_mid), gain_mid).astype(jnp.bfloat16)
    out_ext = extended_2(upsample(act_mid), (("row", 1),), 1)
    final = rms_silu(causal_conv(out_ext, full_out), gain_out)
    final = jnp.where(valid, final, jnp.zeros((), jnp.float32)).astype(jnp.bfloat16)
    return final.reshape(1, FMAX, 4 * RL, 4 * WL * final.shape[3])


LINE = 4
PLANE = 4
ZC, C1, C2, C3 = 16, 384, 192, 96
TOK = 16
IN_SH = C1 // 16
MID_SH = C2 // 16
OUT_BLK = C2 // (2 * LINE)
PIECE_ROWS = 96
W_ROWS = 3 * IN_SH
B_ROWS = LINE * W_ROWS + LINE * LINE
WOUT_LANES = 896
F32, BF16 = jnp.float32, jnp.bfloat16
VMEM = functools.partial(pl.BlockSpec, memory_space=pltpu.VMEM)
SMEM = functools.partial(pl.BlockSpec, memory_space=pltpu.SMEM)
HBM = functools.partial(pl.BlockSpec, memory_space=pltpu.HBM)


def cost(us):
    return pl.CostEstimate(flops=int(us * 1.15e9), bytes_accessed=0, transcendentals=0)


def iota(shape, dim):
    return lax.broadcasted_iota(jnp.int32, shape, dim)


def place():
    group = lax.axis_index("grp")
    return lax.div(group, PLANE), lax.rem(group, PLANE), lax.axis_index("row")


def silu(v):
    return v / (1.0 + jnp.exp(-v))


def dot_nt(lhs, rhs):
    return lax.dot_general(lhs, rhs, (((1,), (1,)), ((), ())), preferred_element_type=F32)


def pack_kernel(offsets_hbm, assign_hbm, w_hbm, lat_hbm, *refs):
    outs, (wf, lf, pf, w_ref, lat_ref, offsets, assign, sems) = refs[:LINE], refs[LINE:]
    moves = [(offsets_hbm, offsets), (assign_hbm, assign), (lat_hbm, lat_ref), (w_hbm, w_ref)]
    copies = [pltpu.make_async_copy(src, dst, sems.at[i]) for i, (src, dst) in enumerate(moves)]
    for copy in copies:
        copy.start()
    z, _, c = place()
    for copy in copies:
        copy.wait()
    wf[:, :, :C2] = w_ref[...].astype(F32)
    lat = lat_ref[...].astype(F32)
    lf[32:40, :] = jnp.zeros((8, 128), F32)
    for j in range(32):
        lf[j : j + 1, :] = lat[:, 128 * j : 128 * j + 128]
    lane1 = iota((1, 128), 1)
    pf[PIECE_ROWS - 8 :, :] = jnp.zeros((8, 256), F32)
    for g in range(16):
        off = offsets[assign[g]]
        row, rem = lax.div(off, 8), lax.rem(off, 8)
        x = pltpu.roll(lf[pl.ds(row, 8), :], lax.rem(128 - ZC * rem, 128), 1)
        keep = lane1 < 128 - ZC * rem
        pf[g : g + 1, 0:128] = jnp.where(keep, x[0:1], x[1:2])
        pf[g : g + 1, 128:256] = jnp.where(keep, x[1:2], x[2:3])
    lane = iota((IN_SH, 256), 1)
    for k in range(LINE):
        first = (lax.rem(z + k, LINE) * 2 + c) * OUT_BLK
        for b in range(3):
            acc = jnp.zeros((IN_SH, 256), F32)
            for j in range(9):
                tap = 9 * (j // 3) + 3 * b + j % 3
                at = OUT_BLK * j
                moved = pltpu.roll(wf[tap], lax.rem(at - first + 256, 256), 1)
                acc = jnp.where((lane >= at) & (lane < at + OUT_BLK), moved, acc)
            pf[TOK + IN_SH * b : TOK + IN_SH * (b + 1), :] = acc
        outs[k][...] = pf[...].astype(BF16)


def pack(offsets, assign, w_mid, latents):
    piece = jax.ShapeDtypeStruct((PIECE_ROWS, 256), BF16)
    return pl.pallas_call(
        pack_kernel,
        out_shape=[piece] * LINE,
        in_specs=[HBM()] * 4,
        out_specs=[VMEM()] * LINE,
        scratch_shapes=[
            pltpu.VMEM((27, IN_SH, 256), F32),
            pltpu.VMEM((40, 128), F32),
            pltpu.VMEM((PIECE_ROWS, 256), F32),
            pltpu.VMEM((27, IN_SH, C2), BF16),
            pltpu.VMEM(latents.shape, BF16),
            pltpu.SMEM(offsets.shape, jnp.int32),
            pltpu.SMEM(assign.shape, jnp.int32),
            pltpu.SemaphoreType.DMA((4,)),
        ],
        cost_estimate=cost(2),
        compiler_params=pltpu.CompilerParams(vmem_limit_bytes=32 << 20),
        name="pack",
    )(*(pltpu.with_memory_space_constraint(v, pltpu.HBM) for v in (offsets, assign, w_mid, latents)))


def join_kernel(*refs):
    pieces, outs, (pf, bf) = refs[:LINE], refs[LINE : LINE + PLANE], refs[LINE + PLANE :]
    _, q, _ = place()
    for k in range(LINE):
        whole = pieces[k][...].astype(F32)
        pf[TOK * k : TOK * (k + 1), :] = whole[:TOK]
        bf[W_ROWS * k : W_ROWS * (k + 1), :] = whole[TOK : TOK + W_ROWS]
    base = LINE * W_ROWS
    for d in range(PLANE):
        for k in range(LINE):
            for line in range(LINE):
                at = base + LINE * k + line
                bf[at : at + 1, :] = pf[pl.ds(TOK * k + PLANE * line + (q ^ d), 1), :]
        outs[d][...] = bf[...].astype(BF16)


def join(pieces):
    out = jax.ShapeDtypeStruct((B_ROWS, 256), BF16)
    return pl.pallas_call(
        join_kernel,
        out_shape=[out] * PLANE,
        in_specs=[VMEM()] * LINE,
        out_specs=[VMEM()] * PLANE,
        scratch_shapes=[pltpu.VMEM((LINE * TOK, 256), F32), pltpu.VMEM((B_ROWS, 256), F32)],
        compiler_params=pltpu.CompilerParams(vmem_limit_bytes=32 << 20),
        cost_estimate=cost(5),
        name="join",
    )(*pieces)


def mid_kernel(frames, assign, *refs):
    parts, (win_ref, gain_ref), outs = refs[:PLANE], refs[PLANE : PLANE + 2], refs[PLANE + 2 : PLANE + 2 + LINE]
    lt, xs, zlo, zhi, w1, act, wf = refs[PLANE + 2 + LINE :]
    z, q, _ = place()
    base = LINE * W_ROWS
    for d in range(PLANE):
        part = parts[d][...].astype(F32)
        lt[...] = part[base:]
        for k in range(LINE):
            shard = lax.rem(z - k + LINE, LINE) * PLANE + (q ^ d)
            for b in range(3):
                at = W_ROWS * k + IN_SH * b
                wf[b, pl.ds(pl.multiple_of(shard * IN_SH, 8), IN_SH), :] = part[at : at + IN_SH]
            for i in range(LINE):
                xs[i, pl.ds(shard, 1), :] = lt[pl.ds(LINE * k + lax.rem(z + i, LINE), 1), :]
    zero_rows = jnp.zeros((1, 6, WL, 640), BF16)
    zero_cols = jnp.zeros((4, 1, WL, 640), BF16)
    for ref in (zlo, zhi):
        for i in range(LINE):
            ref[i, 0:1] = zero_rows
            ref[i, 1:2] = zero_rows
            ref[i, 2:6, 0:1] = zero_cols
            ref[i, 2:6, 5:6] = zero_cols
    w1[...] = jnp.zeros((640, C1), BF16)
    for n in range(9):
        w1[64 * n : 64 * n + 48, :] = win_ref[48 * n : 48 * n + 48, :]
    lane_n, row_l = iota((256, 640), 1), iota((256, 640), 0)
    spread = ((row_l % ZC == lane_n % ZC) & (lane_n % 64 < 48) & (lane_n < 576)).astype(F32).astype(BF16)
    tap_e = (lane_n % 64) // ZC
    col = row_l % WL
    from_left = (tap_e == 0) & (col > 0)
    from_right = (tap_e == 2) & (col < WL - 1)
    is_mid = tap_e == 1
    low = lane_n % 128 < 64
    pos16, shard16 = iota((256, 16), 0), iota((256, 16), 1)
    pos, tok_l = iota((256, 256), 0).astype(F32), (iota((256, 256), 1) // ZC).astype(F32)
    for i in range(LINE):
        group = lax.rem(z + i, LINE) * PLANE + q
        fill = frames[assign[group]] * (TOK // FMAX)
        hit = (pos16 >= fill * shard16) & (pos16 < fill * (shard16 + 1))
        first = jnp.sum(jnp.where(hit, (fill * shard16).astype(F32), 0.0), axis=1, keepdims=True)
        rows = jnp.dot(hit.astype(F32).astype(BF16), xs[i].astype(BF16), preferred_element_type=F32)
        own = jnp.where(pos - first == tok_l, rows, 0.0).astype(BF16)
        wide = jnp.dot(own, spread, preferred_element_type=F32)
        left, right = pltpu.roll(wide, 1, 0), pltpu.roll(wide, 255, 0)
        cols = jnp.where(is_mid, wide, jnp.where(from_left, left, jnp.where(from_right, right, 0.0)))
        zlo[i, 2:6, 1:5] = jnp.where(low, cols, 0.0).astype(BF16).reshape(4, 4, WL, 640)
        zhi[i, 2:6, 1:5] = jnp.where(low, 0.0, cols).astype(BF16).reshape(4, 4, WL, 640)
        taps = []
        for j in range(5):
            a0, b0 = divmod(2 * j, 3)
            a1, b1 = divmod(min(2 * j + 1, 8), 3)
            at = slice(128 * j, 128 * j + 128)
            tile = zlo[i, a0 : a0 + 4, b0 : b0 + 4, :, at] + zhi[i, a1 : a1 + 4, b1 : b1 + 4, :, at]
            taps.append(tile.reshape(256, 128))
        h = jnp.dot(jnp.concatenate(taps, axis=1), w1[...], preferred_element_type=F32)
        scale = lax.rsqrt(jnp.mean(h * h, axis=1, keepdims=True) + 1e-6)
        act[256 * i : 256 * i + 256, :] = silu(h * scale * gain_ref[...]).astype(BF16)
    lanes = LINE * 256
    at = iota((OUT_BLK, lanes), 1)
    frame, row, column = (at // 64) % FMAX, (at // WL) % 4, at % WL
    summed = []
    for b in range(3):
        prod = dot_nt(wf[b].T.astype(BF16), act[...])
        for e in range(3):
            now, before, two = (prod[OUT_BLK * (3 * a + e) : OUT_BLK * (3 * a + e + 1)] for a in (2, 1, 0))
            summed.append(
                now
                + jnp.where(frame >= 1, pltpu.roll(before, 64, 1), 0.0)
                + jnp.where(frame >= 2, pltpu.roll(two, 128, 1), 0.0)
            )
    halves = [[], []]
    for b in range(3):
        e0, e1, e2 = summed[3 * b : 3 * b + 3]
        halves[0].append(jnp.where(column > 0, pltpu.roll(e0, 1, 1), 0.0) + e1 + e2)
        halves[1].append(e0 + e1 + jnp.where(column < WL - 1, pltpu.roll(e2, lanes - 1, 1), 0.0))
    phases = [None] * 4
    for px in range(2):
        b0, b1, b2 = halves[px]
        phases[px] = jnp.where(row > 0, pltpu.roll(b0, WL, 1), 0.0) + b1 + b2
        phases[2 + px] = b0 + b1 + jnp.where(row < 3, pltpu.roll(b2, lanes - WL, 1), 0.0)
    for i in range(LINE):
        outs[i][...] = jnp.concatenate([p[:, 256 * i : 256 * i + 256] for p in phases], axis=0).astype(BF16)


def mid(frames, assign, parts, w_in, gain_in):
    out = jax.ShapeDtypeStruct((4 * OUT_BLK, 256), BF16)
    return pl.pallas_call(
        mid_kernel,
        out_shape=[out] * LINE,
        in_specs=[SMEM(), SMEM()] + [VMEM()] * (PLANE + 2),
        out_specs=[VMEM()] * LINE,
        scratch_shapes=[
            pltpu.VMEM((LINE * LINE, 256), F32),
            pltpu.VMEM((LINE, 16, 256), F32),
            pltpu.VMEM((LINE, 6, 6, WL, 640), BF16),
            pltpu.VMEM((LINE, 6, 6, WL, 640), BF16),
            pltpu.VMEM((640, C1), BF16),
            pltpu.VMEM((LINE * 256, C1), BF16),
            pltpu.VMEM((3, C1, 256), F32),
        ],
        compiler_params=pltpu.CompilerParams(vmem_limit_bytes=48 << 20),
        cost_estimate=cost(5),
        name="mid",
    )(frames, assign, *parts, w_in, gain_in)


def wide_kernel(*refs):
    parts, out, wf = refs[:LINE], refs[LINE], refs[LINE + 1]
    z, q, _ = place()
    wf[...] = jnp.zeros((384, 1152), F32)
    for k in range(LINE):
        for d in range(PLANE):
            shard = lax.rem(z - k + LINE, LINE) * PLANE + (q ^ d)
            at = pl.multiple_of(shard * 8, 8)
            part = parts[k][d].astype(F32)
            for r in range(3):
                for j in range(9):
                    wf[pl.ds(128 * r + at, 8), 128 * j : 128 * j + C3] = part[8 * r : 8 * r + 8, C3 * j : C3 * (j + 1)]
    out[...] = wf[...].astype(BF16)


def wide(parts):
    return pl.pallas_call(
        wide_kernel,
        out_shape=jax.ShapeDtypeStruct((384, 1152), BF16),
        in_specs=[VMEM()] * LINE,
        out_specs=VMEM(),
        scratch_shapes=[pltpu.VMEM((384, 1152), F32)],
        cost_estimate=cost(0.5),
        compiler_params=pltpu.CompilerParams(vmem_limit_bytes=48 << 20),
        name="wide",
    )(*parts)


def stack_kernel(*refs):
    rows = refs[0].shape[0]
    for i, ref in enumerate(refs[:-1]):
        refs[-1][rows * i : rows * (i + 1), :] = ref[...]


def stack(parts):
    rows, lanes = parts[0].shape
    return pl.pallas_call(
        stack_kernel,
        out_shape=jax.ShapeDtypeStruct((len(parts) * rows, lanes), BF16),
        in_specs=[VMEM()] * len(parts),
        out_specs=VMEM(),
        cost_estimate=cost(5),
        compiler_params=pltpu.CompilerParams(vmem_limit_bytes=32 << 20),
        name="stack",
    )(*parts)


def out_kernel(frames, assign, *refs):
    own, other, w_own, w_other, gmid_ref, gout_ref, out_ref, hid, lhs, prod = refs
    z, q, c = place()
    count = frames[assign[z * PLANE + q]]
    hid[...] = jnp.zeros((4, 256, 256), F32)
    for side, group in ((c, own), (1 - c, other)):
        for k in range(LINE):
            block = lax.rem(z - k + LINE, LINE) * 2 + side
            part = group[96 * k : 96 * k + 96, :].astype(F32)
            for p in range(4):
                for half in range(2):
                    at = pl.multiple_of((block * 2 + half) * 8, 8)
                    first = OUT_BLK * p + MID_SH * half
                    hid[p, pl.ds(at, 8), :] = part[first : first + 8]
                    hid[p, pl.ds(128 + at, 4), :] = part[first + 8 : first + MID_SH]
    acts = []
    for p in range(4):
        h = hid[p]
        scale = lax.rsqrt(jnp.sum(h * h, axis=0, keepdims=True) * (1.0 / C2) + 1e-6)
        acts.append(silu(h * scale * gmid_ref[...]).astype(BF16))
    r, l = iota((256, 256), 0), iota((256, 256), 1)
    same = (r // 8) == ((l // 64) % 2) * WL + l % WL
    mid_row = 2 * ((l // WL) % 4) + l // 128
    for b in range(3):
        wanted = (c * 8 + r % 8 + b - 1) >> 1
        pick = (same & (mid_row == wanted)).astype(F32).astype(BF16)
        for tp in range(2):
            for px in range(2):
                src = jnp.concatenate([acts[2 * py + px][:, 128 * tp : 128 * tp + 128] for py in range(2)], axis=1)
                lhs[tp, px, :, 256 * b : 256 * b + 256] = dot_nt(pick, src).astype(BF16)
    for tp in range(2):
        for px in range(2):
            prod[tp, px] = jnp.dot(
                lhs[tp, px, :, pl.ds(pl.multiple_of(c * 384, 128), 384)], w_own[...], preferred_element_type=F32
            ) + jnp.dot(
                lhs[tp, px, :, pl.ds(pl.multiple_of((1 - c) * 384, 128), 384)], w_other[...], preferred_element_type=F32
            )
    lane = iota((1, 8, 128), 2)
    below = [lane < 128 - 32 * i for i in range(4)]
    for t in range(FMAX):
        sums = []
        for px in range(2):
            row = []
            for e in range(3):
                total = None
                for a in range(3):
                    s = t + a - 2
                    if s < 0:
                        continue
                    at = 128 * (3 * a + e)
                    term = prod[s // 2, px, 128 * (s % 2) : 128 * (s % 2) + 128, at : at + 128].reshape(WL, 8, 128)
                    total = term if total is None else total + term
                row.append(total)
            sums.append(row)
        zero = jnp.zeros((1, 8, 128), F32)
        after = jnp.concatenate([sums[0][2][1:], zero], axis=0)
        before = jnp.concatenate([zero, sums[1][0][:-1]], axis=0)
        outs = [
            before + sums[0][1] + sums[0][2],
            sums[0][0] + sums[0][1] + sums[1][2],
            sums[0][0] + sums[1][1] + sums[1][2],
            sums[1][0] + sums[1][1] + after,
        ]
        vals = []
        for i, o in enumerate(outs):
            scale = lax.rsqrt(jnp.sum(o * o, axis=2, keepdims=True) * (1.0 / C3) + 1e-6)
            v = jnp.where(t < count, silu(o * scale * gout_ref[...]), 0.0)
            vals.append(pltpu.roll(v, 128 - 32 * i, 2) if i else v)
        tiles = [
            jnp.where(lane < 96, vals[0], vals[1]),
            jnp.where(lane < 64, vals[1], vals[2]),
            jnp.where(lane < 32, vals[2], vals[3]),
        ]
        for x in range(WL):
            both = jnp.concatenate([tile[x] for tile in tiles], axis=1)
            out_ref[0, t, :, 384 * x : 384 * x + 384] = both.astype(BF16)


def finish(frames, assign, *rest):
    return pl.pallas_call(
        out_kernel,
        out_shape=jax.ShapeDtypeStruct((1, FMAX, 4 * RL, 4 * WL * C3), BF16),
        in_specs=[SMEM(), SMEM()] + [VMEM()] * len(rest),
        out_specs=VMEM(),
        scratch_shapes=[
            pltpu.VMEM((4, 256, 256), F32),
            pltpu.VMEM((2, 2, 256, 768), BF16),
            pltpu.VMEM((2, 2, 256, 1152), F32),
        ],
        compiler_params=pltpu.CompilerParams(vmem_limit_bytes=48 << 20),
        cost_estimate=cost(4.8),
        name="finish",
    )(frames, assign, *rest)


def along_z(value, step):
    return lax.ppermute(value, "grp", [(g, (g + PLANE * step) % (LINE * PLANE)) for g in range(LINE * PLANE)])


def in_plane(value, flip):
    return lax.ppermute(value, "grp", [(g, g ^ flip) for g in range(LINE * PLANE)])


def other_core(value):
    return lax.ppermute(value, "row", [(0, 1), (1, 0)])


def per_device_fast(latents, frames, offsets, assign, w_in, w_mid, w_out, gain_in, gain_mid, gain_out):
    core = lax.axis_index("row")
    pieces = pack(offsets, assign, jnp.transpose(w_mid, (1, 0, 2)), latents)
    pieces = [pieces[0]] + [along_z(pieces[k], k) for k in range(1, LINE)]
    parts = join(pieces)
    parts = [parts[0]] + [in_plane(parts[d], d) for d in range(1, PLANE)]
    rows = w_out.reshape(MID_SH, 3, 3, 3, C3).transpose(2, 0, 1, 3, 4).reshape(3, MID_SH, 9 * C3)
    rows = jnp.pad(rows, ((0, 0), (0, 16 - MID_SH), (0, WOUT_LANES - 9 * C3))).reshape(48, WOUT_LANES)
    half = lax.dynamic_slice_in_dim(rows, core * 24, 24, axis=0)
    plane = stack([half] + [in_plane(half, d) for d in range(1, PLANE)]).reshape(PLANE, 24, WOUT_LANES)
    own = [plane] + [along_z(plane, k) for k in range(1, LINE)]
    hidden = mid(frames, assign, parts, w_in.transpose(1, 0, 2).reshape(27 * ZC, C1), gain_in[None, :])
    own, _ = lax.optimization_barrier((own, hidden[0]))
    w_last = wide(own)
    hidden = stack([hidden[0]] + [along_z(hidden[k], k) for k in range(1, LINE)])
    gmid = jnp.pad(gain_mid.reshape(16, MID_SH), ((0, 0), (0, 16 - MID_SH)))
    gmid = jnp.concatenate([gmid[:, :8], gmid[:, 8:]]).reshape(256, 1)
    gout = jnp.pad(gain_out, (0, 128 - C3)).reshape(1, 128)
    return finish(frames, assign, hidden, other_core(hidden), w_last, other_core(w_last), gmid, gout)


def solution(mesh):
    fast = mesh.shape["grp"] == LINE * PLANE and mesh.shape["row"] == 2
    placed = (
        P("grp", None),
        P(),
        P(),
        P(),
        P(),
        P("grp", None, None),
        P("grp", None, None),
        P(),
        P(),
        P(),
    )
    return jax.shard_map(
        per_device_fast if fast else per_device_general,
        mesh=mesh,
        in_specs=placed,
        out_specs=P("grp", None, "row", None),
        check_vma=False,
    )
```

```python
import functools

import jax
import jax.numpy as jnp
from jax import lax
from jax.experimental import pallas as pl
from jax.experimental.pallas import tpu as pltpu
from jax.sharding import PartitionSpec as P

RL = 2
WL = 16
FMAX = 4


def extended_2(cells, sides, width):
    for axis, dim in sides:
        count = lax.axis_size(axis)
        ends = count - 1
        head = lax.slice_in_dim(cells, 0, width, axis=dim)
        tail = lax.slice_in_dim(cells, cells.shape[dim] - width, cells.shape[dim], axis=dim)
        cells = jnp.concatenate(
            [
                lax.ppermute(tail, axis, [(i, (i + 1) % count) for i in range(ends)]),
                cells,
                lax.ppermute(head, axis, [((i + 1) % count, i) for i in range(ends)]),
            ],
            axis=dim,
        )
    return cells


def rms_silu(hidden, gain):
    mean_sq = jnp.mean(hidden * hidden, axis=-1, keepdims=True)
    scaled = hidden * lax.rsqrt(mean_sq + 1e-06) * gain
    return jax.nn.silu(scaled)


def causal_conv(extended, weight):
    count_t = extended.shape[0]
    count_r = extended.shape[1] - 2
    count_c = extended.shape[2]
    width_in = extended.shape[3]
    width_out = weight.shape[2]
    padded = jnp.pad(extended, ((2, 0), (0, 0), (1, 1), (0, 0)))
    total = jnp.zeros((count_t * count_r * count_c, width_out), jnp.float32)
    for time_tap in range(3):
        for row_tap in range(3):
            for col_tap in range(3):
                window = padded[
                    time_tap : time_tap + count_t,
                    row_tap : row_tap + count_r,
                    col_tap : col_tap + count_c,
                ]
                window = window.reshape(count_t * count_r * count_c, width_in)
                tap_index = 9 * time_tap + 3 * row_tap + col_tap
                total = total + jnp.dot(
                    window, weight[:, tap_index, :], preferred_element_type=jnp.float32
                )
    return total.reshape(count_t, count_r, count_c, width_out)


def upsample(values):
    return jnp.repeat(jnp.repeat(values, 2, axis=1), 2, axis=2)


def per_device_general(latents, frames, offsets, assign, w_in, w_mid, w_out, gain_in, gain_mid, gain_out):
    groups = lax.axis_size("grp")
    row_count = lax.axis_size("row")
    row_index = lax.axis_index("row")
    group_index = lax.axis_index("grp")
    channels = w_in.shape[0]
    cap_vals = latents.shape[1] // groups
    cap_tokens = cap_vals // channels
    span_len = cap_tokens // FMAX
    flat = latents[0]
    slot_ids = jnp.arange(cap_vals, dtype=jnp.int32)

    def select_span(request):
        start = offsets[request] * channels
        block = lax.dynamic_slice_in_dim(flat, start, cap_vals)
        keep = slot_ids < frames[request] * span_len * channels
        return jnp.where(keep, block, jnp.zeros((), block.dtype))

    outgoing = jax.vmap(select_span)(assign)
    incoming = lax.all_to_all(outgoing, "grp", split_axis=0, concat_axis=0, tiled=True)
    table = incoming.reshape(groups * cap_tokens, channels)
    request = assign[group_index]
    count = frames[request]
    fill_len = count * span_len
    image_rows = RL * row_count
    frame_ids = jnp.arange(FMAX, dtype=jnp.int32)[:, None, None]
    row_ids = row_index * RL + jnp.arange(RL, dtype=jnp.int32)[None, :, None]
    col_ids = jnp.arange(WL, dtype=jnp.int32)[None, None, :]
    position = (frame_ids * image_rows + row_ids) * WL + col_ids
    shard = jnp.minimum(position // fill_len, groups - 1)
    within = position % fill_len
    tokens = table[shard * cap_tokens + within]
    valid = (frame_ids < count)[..., None]
    latent_in = jnp.where(valid, tokens, jnp.zeros((), tokens.dtype))
    full_mid, full_out = (
        lax.all_gather(w_mid, "grp", axis=0, tiled=True),
        lax.all_gather(w_out, "grp", axis=0, tiled=True),
    )
    latent_ext = extended_2(latent_in, (("row", 1),), 1)
    act_in = rms_silu(causal_conv(latent_ext, w_in), gain_in).astype(jnp.bfloat16)
    mid_ext = extended_2(upsample(act_in), (("row", 1),), 1)
    act_mid = rms_silu(causal_conv(mid_ext, full_mid), gain_mid).astype(jnp.bfloat16)
    out_ext = extended_2(upsample(act_mid), (("row", 1),), 1)
    final = rms_silu(causal_conv(out_ext, full_out), gain_out)
    final = jnp.where(valid, final, jnp.zeros((), jnp.float32)).astype(jnp.bfloat16)
    return final.reshape(1, FMAX, 4 * RL, 4 * WL * final.shape[3])


LINE = 4
PLANE = 4
ZC, C1, C2, C3 = 16, 384, 192, 96
TOK = 16
IN_SH = C1 // 16
MID_SH = C2 // 16
OUT_BLK = C2 // (2 * LINE)
PIECE_ROWS = 96
W_ROWS = 3 * IN_SH
B_ROWS = LINE * W_ROWS + LINE * LINE
WOUT_LANES = 896
HALF_CH = C2 // 2
FOLD = 9 * C3 // 8
F32, BF16 = jnp.float32, jnp.bfloat16
VMEM = functools.partial(pl.BlockSpec, memory_space=pltpu.VMEM)
SMEM = functools.partial(pl.BlockSpec, memory_space=pltpu.SMEM)
HBM = functools.partial(pl.BlockSpec, memory_space=pltpu.HBM)


def in_hbm(*values):
    return [pltpu.with_memory_space_constraint(v, pltpu.HBM) for v in values]


def cost(us):
    return pl.CostEstimate(flops=int(us * 1.15e9), bytes_accessed=0, transcendentals=0)


def iota(shape, dim):
    return lax.broadcasted_iota(jnp.int32, shape, dim)


def place():
    group = lax.axis_index("grp")
    return lax.div(group, PLANE), lax.rem(group, PLANE), lax.axis_index("row")


def silu(v):
    return v / (1.0 + jnp.exp(-v))


def dot_nt(lhs, rhs):
    return lax.dot_general(lhs, rhs, (((1,), (1,)), ((), ())), preferred_element_type=F32)


def pack_kernel(offsets_hbm, assign_hbm, w_hbm, lat_hbm, *refs):
    outs, (wf, lf, pf, w_ref, lat_ref, offsets, assign, sems) = refs[:LINE], refs[LINE:]
    moves = [(offsets_hbm, offsets), (assign_hbm, assign), (lat_hbm, lat_ref), (w_hbm, w_ref)]
    copies = [pltpu.make_async_copy(src, dst, sems.at[i]) for i, (src, dst) in enumerate(moves)]
    for copy in copies:
        copy.start()
    z, _, c = place()
    for copy in copies:
        copy.wait()
    wf[:, :, :C2] = w_ref[...].astype(F32)
    lat = lat_ref[...].astype(F32)
    lf[32:40, :] = jnp.zeros((8, 128), F32)
    for j in range(32):
        lf[j : j + 1, :] = lat[:, 128 * j : 128 * j + 128]
    lane1 = iota((1, 128), 1)
    pf[PIECE_ROWS - 8 :, :] = jnp.zeros((8, 256), F32)
    for g in range(16):
        off = offsets[assign[g]]
        row, rem = lax.div(off, 8), lax.rem(off, 8)
        x = pltpu.roll(lf[pl.ds(row, 8), :], lax.rem(128 - ZC * rem, 128), 1)
        keep = lane1 < 128 - ZC * rem
        pf[g : g + 1, 0:128] = jnp.where(keep, x[0:1], x[1:2])
        pf[g : g + 1, 128:256] = jnp.where(keep, x[1:2], x[2:3])
    lane = iota((IN_SH, 256), 1)
    for k in range(LINE):
        first = (lax.rem(z + k, LINE) * 2 + c) * OUT_BLK
        for b in range(3):
            acc = jnp.zeros((IN_SH, 256), F32)
            for j in range(9):
                tap = 9 * (j // 3) + 3 * b + j % 3
                at = OUT_BLK * j
                moved = pltpu.roll(wf[tap], lax.rem(at - first + 256, 256), 1)
                acc = jnp.where((lane >= at) & (lane < at + OUT_BLK), moved, acc)
            pf[TOK + IN_SH * b : TOK + IN_SH * (b + 1), :] = acc
        outs[k][...] = pf[...].astype(BF16)


def pack(offsets, assign, w_mid, latents):
    piece = jax.ShapeDtypeStruct((PIECE_ROWS, 256), BF16)
    return pl.pallas_call(
        pack_kernel,
        out_shape=[piece] * LINE,
        in_specs=[HBM()] * 4,
        out_specs=[VMEM()] * LINE,
        scratch_shapes=[
            pltpu.VMEM((27, IN_SH, 256), F32),
            pltpu.VMEM((40, 128), F32),
            pltpu.VMEM((PIECE_ROWS, 256), F32),
            pltpu.VMEM((27, IN_SH, C2), BF16),
            pltpu.VMEM(latents.shape, BF16),
            pltpu.SMEM(offsets.shape, jnp.int32),
            pltpu.SMEM(assign.shape, jnp.int32),
            pltpu.SemaphoreType.DMA((4,)),
        ],
        cost_estimate=cost(2),
        compiler_params=pltpu.CompilerParams(vmem_limit_bytes=32 << 20),
        name="pack",
    )(*in_hbm(offsets, assign, w_mid, latents))


def join_kernel(*refs):
    pieces, outs, (pf, bf) = refs[:LINE], refs[LINE : LINE + PLANE], refs[LINE + PLANE :]
    _, q, _ = place()
    for k in range(LINE):
        whole = pieces[k][...].astype(F32)
        pf[TOK * k : TOK * (k + 1), :] = whole[:TOK]
        bf[W_ROWS * k : W_ROWS * (k + 1), :] = whole[TOK : TOK + W_ROWS]
    base = LINE * W_ROWS
    for d in range(PLANE):
        for k in range(LINE):
            for line in range(LINE):
                at = base + LINE * k + line
                bf[at : at + 1, :] = pf[pl.ds(TOK * k + PLANE * line + (q ^ d), 1), :]
        outs[d][...] = bf[...].astype(BF16)


def join(pieces):
    out = jax.ShapeDtypeStruct((B_ROWS, 256), BF16)
    return pl.pallas_call(
        join_kernel,
        out_shape=[out] * PLANE,
        in_specs=[VMEM()] * LINE,
        out_specs=[VMEM()] * PLANE,
        scratch_shapes=[pltpu.VMEM((LINE * TOK, 256), F32), pltpu.VMEM((B_ROWS, 256), F32)],
        compiler_params=pltpu.CompilerParams(vmem_limit_bytes=32 << 20),
        cost_estimate=cost(5),
        name="join",
    )(*pieces)


def mid_kernel(frames_hbm, assign_hbm, win_hbm, gain_ref, *refs):
    parts, outs = refs[:PLANE], refs[PLANE : PLANE + LINE]
    lt, xs, tokens, shifted, w1, act, wf, frames, assign, sems = refs[PLANE + LINE :]
    z, q, _ = place()
    base = LINE * W_ROWS
    moves = [(frames_hbm, frames), (assign_hbm, assign), (win_hbm, w1.at[0 : 27 * ZC])]
    loads = [pltpu.make_async_copy(src, dst, sems.at[i]) for i, (src, dst) in enumerate(moves)]
    for load in loads:
        load.start()
    w1[27 * ZC :, :] = jnp.zeros((512 - 27 * ZC, C1), BF16)
    for d in range(PLANE):
        part = parts[d][...].astype(F32)
        lt[...] = part[base:]
        for k in range(LINE):
            shard = lax.rem(z - k + LINE, LINE) * PLANE + (q ^ d)
            for b in range(3):
                at = W_ROWS * k + IN_SH * b
                wf[b, pl.ds(pl.multiple_of(shard * IN_SH, 8), IN_SH), :] = part[at : at + IN_SH]
            for i in range(LINE):
                xs[i, pl.ds(shard, 1), :] = lt[pl.ds(LINE * k + lax.rem(z + i, LINE), 1), :]
    own_lane = iota((16, 16, 256), 1) == iota((16, 16, 256), 2) // ZC
    repeat = (iota((256, 128), 0) % ZC == iota((256, 128), 1) % ZC).astype(F32).astype(BF16)
    lane, col = iota((256, 128), 1), iota((256, 128), 0) % WL
    inner_l, inner_r = col > 0, col < WL - 1
    block = lane // ZC
    tap_col = [(block + r) % 3 for r in range(3)]
    lane1 = iota((1, 128), 1)
    zero_rows = jnp.zeros((2, 6, WL, 128), BF16)
    zero_cols = jnp.zeros((4, 1, WL, 128), BF16)
    for load in loads[:2]:
        load.wait()
    for i in range(LINE):
        fill = frames[assign[lax.rem(z + i, LINE) * PLANE + q]] * (TOK // FMAX)
        spread = jnp.where(own_lane, jnp.broadcast_to(xs[i][:, None, :], (16, 16, 256)), 0.0)
        rows = jnp.dot(spread.reshape(256, 256).astype(BF16), repeat, preferred_element_type=F32)
        tokens[i] = jnp.zeros((288, 128), F32)
        for shard in range(16):
            tokens[i, pl.ds(8 + shard * fill, TOK), :] = rows[TOK * shard : TOK * (shard + 1)]
        tokens[i, pl.ds(8 + 16 * fill, TOK), :] = jnp.zeros((TOK, 128), F32)
        here = tokens[i, 8:264, :]
        left = jnp.where(inner_l, tokens[i, 7:263, :], 0.0)
        right = jnp.where(inner_r, tokens[i, 9:265, :], 0.0)
        for r in range(3):
            v = jnp.where(tap_col[r] == 0, left, jnp.where(tap_col[r] == 1, here, right)).astype(BF16)
            shifted[i, r, 0:2] = zero_rows
            shifted[i, r, 2:6, 0:1] = zero_cols
            shifted[i, r, 2:6, 5:6] = zero_cols
            shifted[i, r, 2:6, 1:5] = v.reshape(4, 4, WL, 128)
    for load in loads[2:]:
        load.wait()
    for i in range(LINE):
        tiles = []
        for j in range(4):
            tile = None
            for tap in range(8 * j // 3, min(8 * j + 7, 26) // 3 + 1):
                a, b = divmod(tap, 3)
                lo, hi = max(3 * tap - 8 * j, 0) * ZC, min(3 * tap + 3 - 8 * j, 8) * ZC
                keep = ((lane1 >= lo) & (lane1 < hi)).astype(F32).astype(BF16)
                term = shifted[i, 8 * j % 3, a : a + 4, b : b + 4].reshape(256, 128) * keep
                tile = term if tile is None else tile + term
            tiles.append(tile)
        h = jnp.dot(jnp.concatenate(tiles, axis=1), w1[...], preferred_element_type=F32)
        scale = lax.rsqrt(jnp.mean(h * h, axis=1, keepdims=True) + 1e-6)
        act[256 * i : 256 * i + 256, :] = silu(h * scale * gain_ref[...]).astype(BF16)
    lanes = LINE * 256
    at = iota((OUT_BLK, lanes), 1)
    frame, row, column = (at // 64) % FMAX, (at // WL) % 4, at % WL
    summed = []
    for b in range(3):
        prod = dot_nt(wf[b].T.astype(BF16), act[...])
        for e in range(3):
            now, before, two = (prod[OUT_BLK * (3 * a + e) : OUT_BLK * (3 * a + e + 1)] for a in (2, 1, 0))
            summed.append(
                now
                + jnp.where(frame >= 1, pltpu.roll(before, 64, 1), 0.0)
                + jnp.where(frame >= 2, pltpu.roll(two, 128, 1), 0.0)
            )
    halves = [[], []]
    for b in range(3):
        e0, e1, e2 = summed[3 * b : 3 * b + 3]
        halves[0].append(jnp.where(column > 0, pltpu.roll(e0, 1, 1), 0.0) + e1 + e2)
        halves[1].append(e0 + e1 + jnp.where(column < WL - 1, pltpu.roll(e2, lanes - 1, 1), 0.0))
    phases = [None] * 4
    for px in range(2):
        b0, b1, b2 = halves[px]
        phases[px] = jnp.where(row > 0, pltpu.roll(b0, WL, 1), 0.0) + b1 + b2
        phases[2 + px] = b0 + b1 + jnp.where(row < 3, pltpu.roll(b2, lanes - WL, 1), 0.0)
    for i in range(LINE):
        outs[i][...] = jnp.concatenate([p[:, 256 * i : 256 * i + 256] for p in phases], axis=0).astype(BF16)


def mid(frames, assign, parts, w_in, gain_in):
    out = jax.ShapeDtypeStruct((4 * OUT_BLK, 256), BF16)
    return pl.pallas_call(
        mid_kernel,
        out_shape=[out] * LINE,
        in_specs=[HBM()] * 3 + [VMEM()] * (PLANE + 1),
        out_specs=[VMEM()] * LINE,
        scratch_shapes=[
            pltpu.VMEM((LINE * LINE, 256), F32),
            pltpu.VMEM((LINE, 16, 256), F32),
            pltpu.VMEM((LINE, 288, 128), F32),
            pltpu.VMEM((LINE, 3, 6, 6, WL, 128), BF16),
            pltpu.VMEM((512, C1), BF16),
            pltpu.VMEM((LINE * 256, C1), BF16),
            pltpu.VMEM((3, C1, 256), F32),
            pltpu.SMEM(frames.shape, jnp.int32),
            pltpu.SMEM(assign.shape, jnp.int32),
            pltpu.SemaphoreType.DMA((3,)),
        ],
        compiler_params=pltpu.CompilerParams(vmem_limit_bytes=48 << 20),
        cost_estimate=cost(5),
        name="mid",
    )(*in_hbm(frames, assign, w_in), gain_in, *parts)


def wide_kernel(frames_hbm, assign_hbm, gmid_hbm, gout_hbm, *refs):
    parts, (out, gmid_out, gout_out, limit_out) = refs[:LINE], refs[LINE : LINE + 4]
    rows, wf, gmid_ref, gout_ref, frames, assign, sems = refs[LINE + 4 :]
    moves = [(gmid_hbm, gmid_ref), (gout_hbm, gout_ref), (frames_hbm, frames), (assign_hbm, assign)]
    loads = [pltpu.make_async_copy(src, dst, sems.at[i]) for i, (src, dst) in enumerate(moves)]
    for load in loads:
        load.start()
    z, q, _ = place()
    wf[...] = jnp.zeros((9, 3 * HALF_CH, 128), F32)
    for k in range(LINE):
        for d in range(PLANE):
            shard = lax.rem(z - k + LINE, LINE) * PLANE + (q ^ d)
            part = parts[k][16 * d : 16 * d + 16, :].astype(F32)
            rows[0:16, : 9 * C3] = part[:, : 9 * C3]
            for g in range(8):
                rows[16:18, FOLD * g : FOLD * (g + 1)] = part[2 * g : 2 * g + 2, 9 * C3 : 9 * C3 + FOLD]
            for j in range(9):
                tap = rows[:, C3 * j : C3 * (j + 1)]
                for b in range(3):
                    wf[j, pl.ds(HALF_CH * b + 6 * shard, 6), :C3] = tap[6 * b : 6 * b + 6]
    for j in range(9):
        out[:, 128 * j : 128 * (j + 1)] = wf[j].astype(BF16)
    for load in loads:
        load.wait()
    row, channel = iota((C2, C2), 0), iota((C2, C2), 1)
    wanted = (row % HALF_CH) // 6 * MID_SH + row // HALF_CH * 6 + row % 6
    column = jnp.sum(jnp.where(channel == wanted, gmid_ref[...], 0.0), axis=1, keepdims=True)
    gmid_out[...] = jnp.broadcast_to(column, (C2, 128))
    gout_out[...] = jnp.zeros((1, 128), F32)
    gout_out[:, :C3] = gout_ref[...]
    limit_out[...] = jnp.full((1, 128), frames[assign[z * PLANE + q]], jnp.int32).astype(F32)


def wide(frames, assign, gain_mid, gain_out, parts):
    return pl.pallas_call(
        wide_kernel,
        out_shape=[
            jax.ShapeDtypeStruct((3 * HALF_CH, 1152), BF16),
            jax.ShapeDtypeStruct((C2, 128), F32),
            jax.ShapeDtypeStruct((1, 128), F32),
            jax.ShapeDtypeStruct((1, 128), F32),
        ],
        in_specs=[HBM()] * 4 + [VMEM()] * LINE,
        out_specs=[VMEM()] * 4,
        scratch_shapes=[
            pltpu.VMEM((24, WOUT_LANES), F32),
            pltpu.VMEM((9, 3 * HALF_CH, 128), F32),
            pltpu.VMEM(gain_mid.shape, F32),
            pltpu.VMEM(gain_out.shape, F32),
            pltpu.SMEM(frames.shape, jnp.int32),
            pltpu.SMEM(assign.shape, jnp.int32),
            pltpu.SemaphoreType.DMA((4,)),
        ],
        cost_estimate=cost(0.01),
        compiler_params=pltpu.CompilerParams(vmem_limit_bytes=48 << 20),
        name="wide",
    )(*in_hbm(frames, assign, gain_mid, gain_out), *parts)


def stack_kernel(*refs):
    rows = refs[0].shape[0]
    for i, ref in enumerate(refs[:-1]):
        refs[-1][rows * i : rows * (i + 1), :] = ref[...]


def stack(parts, us=5):
    rows, lanes = parts[0].shape
    return pl.pallas_call(
        stack_kernel,
        out_shape=jax.ShapeDtypeStruct((len(parts) * rows, lanes), BF16),
        in_specs=[VMEM()] * len(parts),
        out_specs=VMEM(),
        cost_estimate=cost(us),
        compiler_params=pltpu.CompilerParams(vmem_limit_bytes=32 << 20),
        name="stack",
    )(*parts)


def out_kernel(own, other, w_own, w_other, gmid_ref, gout_ref, limit_ref, out_ref, hid, lhs, prod, w_all):
    z, q, c = place()
    for b in range(3):
        for side, half in ((c, w_own), (1 - c, w_other)):
            at = pl.multiple_of(256 * b + HALF_CH * side, 32)
            w_all[pl.ds(at, HALF_CH), :] = half[HALF_CH * b : HALF_CH * (b + 1), :]
        w_all[256 * b + C2 : 256 * (b + 1), :] = jnp.zeros((64, 1152), BF16)
    lhs[:, :, :, :] = jnp.zeros(lhs.shape, BF16)
    for side, group in ((c, own), (1 - c, other)):
        for k in range(LINE):
            block = lax.rem(z - k + LINE, LINE) * 2 + side
            part = group[96 * k : 96 * k + 96, :].astype(F32)
            for p in range(4):
                for half in range(2):
                    for shard in range(2):
                        first = OUT_BLK * p + MID_SH * shard + 6 * half
                        at = HALF_CH * half + 12 * block + 6 * shard
                        for tp in range(2):
                            hid[p, tp, pl.ds(at, 6), :] = part[first : first + 6, 128 * tp : 128 * tp + 128]
    acts = []
    for p in range(4):
        halves = []
        for tp in range(2):
            h = hid[p, tp]
            scale = lax.rsqrt(jnp.sum(h * h, axis=0, keepdims=True) * (1.0 / C2) + 1e-6)
            halves.append(silu(h * scale * gmid_ref[...]).astype(BF16))
        acts.append(halves)
    r, l = iota((256, 256), 0), iota((256, 256), 1)
    same = (r // 8) == ((l // 64) % 2) * WL + l % WL
    mid_row = 2 * ((l // WL) % 4) + l // 128
    for b in range(3):
        wanted = (c * 8 + r % 8 + b - 1) >> 1
        pick = (same & (mid_row == wanted)).astype(F32).astype(BF16)
        for tp in range(2):
            for px in range(2):
                src = jnp.concatenate([acts[2 * py + px][tp] for py in range(2)], axis=1)
                rows = dot_nt(pick, src).astype(BF16)
                for half in range(2):
                    lhs[2 * tp + half, px, :, 256 * b : 256 * b + C2] = rows[128 * half : 128 * half + 128]
    prod[0:2] = jnp.dot(lhs[0:2].reshape(512, 768), w_all[...], preferred_element_type=F32).reshape(2, 2, 128, 1152)
    for t in (2, 3):
        at = 384 * (t - 1)
        prod[t, :, :, at:] = jnp.dot(
            lhs[t].reshape(256, 768), w_all[:, at:], preferred_element_type=F32
        ).reshape(2, 128, 1152 - at)
    lane = iota((1, 8, 128), 2)
    limit = limit_ref[...]
    below = [lane < 128 - 32 * i for i in range(4)]
    for t in range(FMAX):
        sums = []
        for px in range(2):
            row = []
            for e in range(3):
                total = None
                for a in range(3):
                    s = t + a - 2
                    if s < 0:
                        continue
                    at = 128 * (3 * a + e)
                    term = prod[s, px, :, at : at + 128].reshape(WL, 8, 128)
                    total = term if total is None else total + term
                row.append(total)
            sums.append(row)
        zero = jnp.zeros((1, 8, 128), F32)
        after = jnp.concatenate([sums[0][2][1:], zero], axis=0)
        before = jnp.concatenate([zero, sums[1][0][:-1]], axis=0)
        outs = [
            before + sums[0][1] + sums[0][2],
            sums[0][0] + sums[0][1] + sums[1][2],
            sums[0][0] + sums[1][1] + sums[1][2],
            sums[1][0] + sums[1][1] + after,
        ]
        vals = []
        for i, o in enumerate(outs):
            scale = lax.rsqrt(jnp.sum(o * o, axis=2, keepdims=True) * (1.0 / C3) + 1e-6)
            v = jnp.where(t < limit, silu(o * scale * gout_ref[...]), 0.0)
            vals.append(pltpu.roll(v, 128 - 32 * i, 2) if i else v)
        tiles = [
            jnp.where(lane < 96, vals[0], vals[1]),
            jnp.where(lane < 64, vals[1], vals[2]),
            jnp.where(lane < 32, vals[2], vals[3]),
        ]
        for x in range(WL):
            both = jnp.concatenate([tile[x] for tile in tiles], axis=1)
            out_ref[0, t, :, 384 * x : 384 * x + 384] = both.astype(BF16)


def finish(*rest):
    return pl.pallas_call(
        out_kernel,
        out_shape=jax.ShapeDtypeStruct((1, FMAX, 4 * RL, 4 * WL * C3), BF16),
        in_specs=[VMEM()] * len(rest),
        out_specs=VMEM(),
        scratch_shapes=[
            pltpu.VMEM((4, 2, C2, 128), F32),
            pltpu.VMEM((4, 2, 128, 768), BF16),
            pltpu.VMEM((4, 2, 128, 1152), F32),
            pltpu.VMEM((768, 1152), BF16),
        ],
        compiler_params=pltpu.CompilerParams(vmem_limit_bytes=48 << 20),
        cost_estimate=cost(4.8),
        name="finish",
    )(*rest)


def along_z(value, step):
    return lax.ppermute(value, "grp", [(g, (g + PLANE * step) % (LINE * PLANE)) for g in range(LINE * PLANE)])


def in_plane(value, flip):
    return lax.ppermute(value, "grp", [(g, g ^ flip) for g in range(LINE * PLANE)])


def other_core(value):
    return lax.ppermute(value, "row", [(0, 1), (1, 0)])


def per_device_fast(latents, frames, offsets, assign, w_in, w_mid, w_out, gain_in, gain_mid, gain_out):
    core = lax.axis_index("row")
    pieces = pack(offsets, assign, jnp.transpose(w_mid, (1, 0, 2)), latents)
    pieces = [pieces[0]] + [along_z(pieces[k], k) for k in range(1, LINE)]
    parts = join(pieces)
    parts = [parts[0]] + [in_plane(parts[d], d) for d in range(1, PLANE)]
    rows = lax.dynamic_slice_in_dim(w_out, core * 6, 6, axis=0)
    rows = rows.reshape(6, 3, 3, 3, C3).transpose(2, 0, 1, 3, 4).reshape(18, 9 * C3)
    fold = rows[16:].reshape(2, 8, FOLD).transpose(1, 0, 2).reshape(16, FOLD)
    half = jnp.pad(jnp.concatenate([rows[:16], fold], axis=1), ((0, 0), (0, 1024 - 9 * C3 - FOLD)))
    plane = stack([half] + [in_plane(half, d) for d in range(1, PLANE)])
    own = [plane] + [along_z(plane, k) for k in range(1, LINE)]
    hidden = mid(frames, assign, parts, w_in.transpose(1, 0, 2).reshape(27 * ZC, C1), gain_in[None, :])
    own, _ = lax.optimization_barrier((own, hidden[0]))
    w_last, gmid, gout, limit = wide(frames, assign, gain_mid[None, :], gain_out[None, :], own)
    hidden = stack([hidden[0]] + [along_z(hidden[k], k) for k in range(1, LINE)], 30)
    return finish(hidden, other_core(hidden), w_last, other_core(w_last), gmid, gout, limit)


def solution(mesh):
    fast = mesh.shape["grp"] == LINE * PLANE and mesh.shape["row"] == 2
    placed = (
        P("grp", None),
        P(),
        P(),
        P(),
        P(),
        P("grp", None, None),
        P("grp", None, None),
        P(),
        P(),
        P(),
    )
    return jax.shard_map(
        per_device_fast if fast else per_device_general,
        mesh=mesh,
        in_specs=placed,
        out_specs=P("grp", None, "row", None),
        check_vma=False,
    )
```

```python
import functools

import jax
import jax.numpy as jnp
from jax import lax
from jax.experimental import pallas as pl
from jax.experimental.pallas import tpu as pltpu
from jax.sharding import PartitionSpec as P

RL = 2
WL = 16
FMAX = 4


def extended_2(cells, sides, width):
    for axis, dim in sides:
        count = lax.axis_size(axis)
        ends = count - 1
        head = lax.slice_in_dim(cells, 0, width, axis=dim)
        tail = lax.slice_in_dim(cells, cells.shape[dim] - width, cells.shape[dim], axis=dim)
        cells = jnp.concatenate(
            [
                lax.ppermute(tail, axis, [(i, (i + 1) % count) for i in range(ends)]),
                cells,
                lax.ppermute(head, axis, [((i + 1) % count, i) for i in range(ends)]),
            ],
            axis=dim,
        )
    return cells


def rms_silu(hidden, gain):
    mean_sq = jnp.mean(hidden * hidden, axis=-1, keepdims=True)
    scaled = hidden * lax.rsqrt(mean_sq + 1e-06) * gain
    return jax.nn.silu(scaled)


def causal_conv(extended, weight):
    count_t = extended.shape[0]
    count_r = extended.shape[1] - 2
    count_c = extended.shape[2]
    width_in = extended.shape[3]
    width_out = weight.shape[2]
    padded = jnp.pad(extended, ((2, 0), (0, 0), (1, 1), (0, 0)))
    total = jnp.zeros((count_t * count_r * count_c, width_out), jnp.float32)
    for time_tap in range(3):
        for row_tap in range(3):
            for col_tap in range(3):
                window = padded[
                    time_tap : time_tap + count_t,
                    row_tap : row_tap + count_r,
                    col_tap : col_tap + count_c,
                ]
                window = window.reshape(count_t * count_r * count_c, width_in)
                tap_index = 9 * time_tap + 3 * row_tap + col_tap
                total = total + jnp.dot(
                    window, weight[:, tap_index, :], preferred_element_type=jnp.float32
                )
    return total.reshape(count_t, count_r, count_c, width_out)


def upsample(values):
    return jnp.repeat(jnp.repeat(values, 2, axis=1), 2, axis=2)


def per_device_general(latents, frames, offsets, assign, w_in, w_mid, w_out, gain_in, gain_mid, gain_out):
    groups = lax.axis_size("grp")
    row_count = lax.axis_size("row")
    row_index = lax.axis_index("row")
    group_index = lax.axis_index("grp")
    channels = w_in.shape[0]
    cap_vals = latents.shape[1] // groups
    cap_tokens = cap_vals // channels
    span_len = cap_tokens // FMAX
    flat = latents[0]
    slot_ids = jnp.arange(cap_vals, dtype=jnp.int32)

    def select_span(request):
        start = offsets[request] * channels
        block = lax.dynamic_slice_in_dim(flat, start, cap_vals)
        keep = slot_ids < frames[request] * span_len * channels
        return jnp.where(keep, block, jnp.zeros((), block.dtype))

    outgoing = jax.vmap(select_span)(assign)
    incoming = lax.all_to_all(outgoing, "grp", split_axis=0, concat_axis=0, tiled=True)
    table = incoming.reshape(groups * cap_tokens, channels)
    request = assign[group_index]
    count = frames[request]
    fill_len = count * span_len
    image_rows = RL * row_count
    frame_ids = jnp.arange(FMAX, dtype=jnp.int32)[:, None, None]
    row_ids = row_index * RL + jnp.arange(RL, dtype=jnp.int32)[None, :, None]
    col_ids = jnp.arange(WL, dtype=jnp.int32)[None, None, :]
    position = (frame_ids * image_rows + row_ids) * WL + col_ids
    shard = jnp.minimum(position // fill_len, groups - 1)
    within = position % fill_len
    tokens = table[shard * cap_tokens + within]
    valid = (frame_ids < count)[..., None]
    latent_in = jnp.where(valid, tokens, jnp.zeros((), tokens.dtype))
    full_mid, full_out = (
        lax.all_gather(w_mid, "grp", axis=0, tiled=True),
        lax.all_gather(w_out, "grp", axis=0, tiled=True),
    )
    latent_ext = extended_2(latent_in, (("row", 1),), 1)
    act_in = rms_silu(causal_conv(latent_ext, w_in), gain_in).astype(jnp.bfloat16)
    mid_ext = extended_2(upsample(act_in), (("row", 1),), 1)
    act_mid = rms_silu(causal_conv(mid_ext, full_mid), gain_mid).astype(jnp.bfloat16)
    out_ext = extended_2(upsample(act_mid), (("row", 1),), 1)
    final = rms_silu(causal_conv(out_ext, full_out), gain_out)
    final = jnp.where(valid, final, jnp.zeros((), jnp.float32)).astype(jnp.bfloat16)
    return final.reshape(1, FMAX, 4 * RL, 4 * WL * final.shape[3])


LINE = 4
PLANE = 4
ZC, C1, C2, C3 = 16, 384, 192, 96
TOK = 16
IN_SH = C1 // 16
MID_SH = C2 // 16
OUT_BLK = C2 // (2 * LINE)
PIECE_ROWS = 96
W_ROWS = 3 * IN_SH
B_ROWS = LINE * W_ROWS + LINE * LINE
WOUT_LANES = 896
HALF_CH = C2 // 2
F32, BF16 = jnp.float32, jnp.bfloat16
VMEM = functools.partial(pl.BlockSpec, memory_space=pltpu.VMEM)
SMEM = functools.partial(pl.BlockSpec, memory_space=pltpu.SMEM)
HBM = functools.partial(pl.BlockSpec, memory_space=pltpu.HBM)


def in_hbm(*values):
    return [pltpu.with_memory_space_constraint(v, pltpu.HBM) for v in values]


def cost(us):
    return pl.CostEstimate(flops=int(us * 1.15e9), bytes_accessed=0, transcendentals=0)


def iota(shape, dim):
    return lax.broadcasted_iota(jnp.int32, shape, dim)


def place():
    group = lax.axis_index("grp")
    return lax.div(group, PLANE), lax.rem(group, PLANE), lax.axis_index("row")


def silu(v):
    return v / (1.0 + jnp.exp(-v))


def dot_nt(lhs, rhs):
    return lax.dot_general(lhs, rhs, (((1,), (1,)), ((), ())), preferred_element_type=F32)


def pack_kernel(offsets_hbm, assign_hbm, w_hbm, lat_hbm, *refs):
    outs, (wf, lf, pf, w_ref, lat_ref, offsets, assign, sems) = refs[:LINE], refs[LINE:]
    parts = [pl.ds(9 * a, 9) for a in range(3)]
    moves = [(w_hbm.at[p], w_ref.at[p]) for p in parts]
    moves = [(offsets_hbm, offsets), (assign_hbm, assign), (lat_hbm, lat_ref)] + moves
    copies = [pltpu.make_async_copy(src, dst, sems.at[i]) for i, (src, dst) in enumerate(moves)]
    for copy in copies:
        copy.start()
    z, _, c = place()
    lf[32:40, :] = jnp.zeros((8, 128), F32)
    for k in range(LINE):
        pf[k, TOK:, :] = jnp.zeros((PIECE_ROWS - TOK, 256), F32)
    lane1 = iota((1, 128), 1)
    lane = iota((IN_SH, 256), 1)
    for copy in copies[:3]:
        copy.wait()
    lat = lat_ref[...].astype(F32)
    for j in range(32):
        lf[j : j + 1, :] = lat[:, 128 * j : 128 * j + 128]
    for g in range(16):
        off = offsets[assign[g]]
        row, rem = lax.div(off, 8), lax.rem(off, 8)
        x = pltpu.roll(lf[pl.ds(row, 8), :], lax.rem(128 - ZC * rem, 128), 1)
        keep = lane1 < 128 - ZC * rem
        pf[0, g : g + 1, 0:128] = jnp.where(keep, x[0:1], x[1:2])
        pf[0, g : g + 1, 128:256] = jnp.where(keep, x[1:2], x[2:3])
    for k in range(1, LINE):
        pf[k, 0:TOK, :] = pf[0, 0:TOK, :]
    for a in range(3):
        copies[3 + a].wait()
        wf[9 * a : 9 * a + 9, :, :C2] = w_ref[9 * a : 9 * a + 9].astype(F32)
        for k in range(LINE):
            first = (lax.rem(z + k, LINE) * 2 + c) * OUT_BLK
            for b in range(3):
                rows = slice(TOK + IN_SH * b, TOK + IN_SH * (b + 1))
                acc = pf[k, rows, :]
                for e in range(3):
                    at = OUT_BLK * (3 * a + e)
                    moved = pltpu.roll(wf[9 * a + 3 * b + e], lax.rem(at - first + 256, 256), 1)
                    acc = jnp.where((lane >= at) & (lane < at + OUT_BLK), moved, acc)
                pf[k, rows, :] = acc
    for k in range(LINE):
        outs[k][...] = pf[k].astype(BF16)


def pack(offsets, assign, w_mid, latents):
    piece = jax.ShapeDtypeStruct((PIECE_ROWS, 256), BF16)
    return pl.pallas_call(
        pack_kernel,
        out_shape=[piece] * LINE,
        in_specs=[HBM()] * 4,
        out_specs=[VMEM()] * LINE,
        scratch_shapes=[
            pltpu.VMEM((27, IN_SH, 256), F32),
            pltpu.VMEM((40, 128), F32),
            pltpu.VMEM((LINE, PIECE_ROWS, 256), F32),
            pltpu.VMEM((27, IN_SH, C2), BF16),
            pltpu.VMEM(latents.shape, BF16),
            pltpu.SMEM(offsets.shape, jnp.int32),
            pltpu.SMEM(assign.shape, jnp.int32),
            pltpu.SemaphoreType.DMA((6,)),
        ],
        cost_estimate=cost(2),
        compiler_params=pltpu.CompilerParams(vmem_limit_bytes=32 << 20),
        name="pack",
    )(*in_hbm(offsets, assign, w_mid, latents))


def join_kernel(*refs):
    pieces, outs, (pf, bf) = refs[:LINE], refs[LINE : LINE + PLANE], refs[LINE + PLANE :]
    _, q, _ = place()
    for k in range(LINE):
        whole = pieces[k][...].astype(F32)
        pf[TOK * k : TOK * (k + 1), :] = whole[:TOK]
        bf[W_ROWS * k : W_ROWS * (k + 1), :] = whole[TOK : TOK + W_ROWS]
    base = LINE * W_ROWS
    for d in range(PLANE):
        for k in range(LINE):
            for line in range(LINE):
                at = base + LINE * k + line
                bf[at : at + 1, :] = pf[pl.ds(TOK * k + PLANE * line + (q ^ d), 1), :]
        outs[d][...] = bf[...].astype(BF16)


def join(pieces):
    out = jax.ShapeDtypeStruct((B_ROWS, 256), BF16)
    return pl.pallas_call(
        join_kernel,
        out_shape=[out] * PLANE,
        in_specs=[VMEM()] * LINE,
        out_specs=[VMEM()] * PLANE,
        scratch_shapes=[pltpu.VMEM((LINE * TOK, 256), F32), pltpu.VMEM((B_ROWS, 256), F32)],
        compiler_params=pltpu.CompilerParams(vmem_limit_bytes=32 << 20),
        cost_estimate=cost(5),
        name="join",
    )(*pieces)


def mid_kernel(frames_hbm, assign_hbm, win_hbm, gain_ref, *refs):
    parts, outs = refs[:PLANE], refs[PLANE : PLANE + LINE]
    lt, xs, tokens, shifted, w1, act, wf, frames, assign, sems = refs[PLANE + LINE :]
    z, q, _ = place()
    base = LINE * W_ROWS
    moves = [(frames_hbm, frames), (assign_hbm, assign), (win_hbm, w1.at[0 : 27 * ZC])]
    loads = [pltpu.make_async_copy(src, dst, sems.at[i]) for i, (src, dst) in enumerate(moves)]
    for load in loads:
        load.start()
    w1[27 * ZC :, :] = jnp.zeros((512 - 27 * ZC, C1), BF16)
    for d in range(PLANE):
        part = parts[d][...].astype(F32)
        lt[...] = part[base:]
        for k in range(LINE):
            shard = lax.rem(z - k + LINE, LINE) * PLANE + (q ^ d)
            for b in range(3):
                at = W_ROWS * k + IN_SH * b
                wf[b, pl.ds(pl.multiple_of(shard * IN_SH, 8), IN_SH), :] = part[at : at + IN_SH]
            for i in range(LINE):
                xs[i, pl.ds(shard, 1), :] = lt[pl.ds(LINE * k + lax.rem(z + i, LINE), 1), :]
    own_lane = iota((16, 16, 256), 1) == iota((16, 16, 256), 2) // ZC
    repeat = (iota((256, 128), 0) % ZC == iota((256, 128), 1) % ZC).astype(F32).astype(BF16)
    lane, col = iota((256, 128), 1), iota((256, 128), 0) % WL
    inner_l, inner_r = col > 0, col < WL - 1
    block = lane // ZC
    tap_col = [(block + r) % 3 for r in range(3)]
    lane1 = iota((1, 128), 1)
    zero_rows = jnp.zeros((2, 6, WL, 128), BF16)
    zero_cols = jnp.zeros((4, 1, WL, 128), BF16)
    for load in loads[:2]:
        load.wait()
    for i in range(LINE):
        fill = frames[assign[lax.rem(z + i, LINE) * PLANE + q]] * (TOK // FMAX)
        spread = jnp.where(own_lane, jnp.broadcast_to(xs[i][:, None, :], (16, 16, 256)), 0.0)
        rows = jnp.dot(spread.reshape(256, 256).astype(BF16), repeat, preferred_element_type=F32)
        tokens[i] = jnp.zeros((288, 128), F32)
        for shard in range(16):
            tokens[i, pl.ds(8 + shard * fill, TOK), :] = rows[TOK * shard : TOK * (shard + 1)]
        tokens[i, pl.ds(8 + 16 * fill, TOK), :] = jnp.zeros((TOK, 128), F32)
        here = tokens[i, 8:264, :]
        left = jnp.where(inner_l, tokens[i, 7:263, :], 0.0)
        right = jnp.where(inner_r, tokens[i, 9:265, :], 0.0)
        for r in range(3):
            v = jnp.where(tap_col[r] == 0, left, jnp.where(tap_col[r] == 1, here, right)).astype(BF16)
            shifted[i, r, 0:2] = zero_rows
            shifted[i, r, 2:6, 0:1] = zero_cols
            shifted[i, r, 2:6, 5:6] = zero_cols
            shifted[i, r, 2:6, 1:5] = v.reshape(4, 4, WL, 128)
    for load in loads[2:]:
        load.wait()
    for i in range(LINE):
        tiles = []
        for j in range(4):
            tile = None
            for tap in range(8 * j // 3, min(8 * j + 7, 26) // 3 + 1):
                a, b = divmod(tap, 3)
                lo, hi = max(3 * tap - 8 * j, 0) * ZC, min(3 * tap + 3 - 8 * j, 8) * ZC
                keep = ((lane1 >= lo) & (lane1 < hi)).astype(F32).astype(BF16)
                term = shifted[i, 8 * j % 3, a : a + 4, b : b + 4].reshape(256, 128) * keep
                tile = term if tile is None else tile + term
            tiles.append(tile)
        h = jnp.dot(jnp.concatenate(tiles, axis=1), w1[...], preferred_element_type=F32)
        scale = lax.rsqrt(jnp.mean(h * h, axis=1, keepdims=True) + 1e-6)
        act[256 * i : 256 * i + 256, :] = silu(h * scale * gain_ref[...]).astype(BF16)
    lanes = LINE * 256
    at = iota((OUT_BLK, lanes), 1)
    frame, row, column = (at // 64) % FMAX, (at // WL) % 4, at % WL
    summed = []
    for b in range(3):
        prod = dot_nt(wf[b].T.astype(BF16), act[...])
        for e in range(3):
            now, before, two = (prod[OUT_BLK * (3 * a + e) : OUT_BLK * (3 * a + e + 1)] for a in (2, 1, 0))
            summed.append(
                now
                + jnp.where(frame >= 1, pltpu.roll(before, 64, 1), 0.0)
                + jnp.where(frame >= 2, pltpu.roll(two, 128, 1), 0.0)
            )
    halves = [[], []]
    for b in range(3):
        e0, e1, e2 = summed[3 * b : 3 * b + 3]
        halves[0].append(jnp.where(column > 0, pltpu.roll(e0, 1, 1), 0.0) + e1 + e2)
        halves[1].append(e0 + e1 + jnp.where(column < WL - 1, pltpu.roll(e2, lanes - 1, 1), 0.0))
    phases = [None] * 4
    for px in range(2):
        b0, b1, b2 = halves[px]
        phases[px] = jnp.where(row > 0, pltpu.roll(b0, WL, 1), 0.0) + b1 + b2
        phases[2 + px] = b0 + b1 + jnp.where(row < 3, pltpu.roll(b2, lanes - WL, 1), 0.0)
    for i in range(LINE):
        outs[i][...] = jnp.concatenate([p[:, 256 * i : 256 * i + 256] for p in phases], axis=0).astype(BF16)


def mid(frames, assign, parts, w_in, gain_in):
    out = jax.ShapeDtypeStruct((4 * OUT_BLK, 256), BF16)
    return pl.pallas_call(
        mid_kernel,
        out_shape=[out] * LINE,
        in_specs=[HBM()] * 3 + [VMEM()] * (PLANE + 1),
        out_specs=[VMEM()] * LINE,
        scratch_shapes=[
            pltpu.VMEM((LINE * LINE, 256), F32),
            pltpu.VMEM((LINE, 16, 256), F32),
            pltpu.VMEM((LINE, 288, 128), F32),
            pltpu.VMEM((LINE, 3, 6, 6, WL, 128), BF16),
            pltpu.VMEM((512, C1), BF16),
            pltpu.VMEM((LINE * 256, C1), BF16),
            pltpu.VMEM((3, C1, 256), F32),
            pltpu.SMEM(frames.shape, jnp.int32),
            pltpu.SMEM(assign.shape, jnp.int32),
            pltpu.SemaphoreType.DMA((3,)),
        ],
        compiler_params=pltpu.CompilerParams(vmem_limit_bytes=48 << 20),
        cost_estimate=cost(5),
        name="mid",
    )(*in_hbm(frames, assign, w_in), gain_in, *parts)


def regroup_kernel(*refs):
    parts, out, rows = refs[:PLANE], refs[PLANE], refs[PLANE + 1]
    for d in range(PLANE):
        part = parts[d][...].astype(F32)
        for b in range(3):
            at = OUT_BLK * b + 6 * d
            rows[at : at + 6, :] = part[8 * b : 8 * b + 6]
    out[...] = rows[...].astype(BF16)


def regroup(parts):
    return pl.pallas_call(
        regroup_kernel,
        out_shape=jax.ShapeDtypeStruct((3 * OUT_BLK, WOUT_LANES), BF16),
        in_specs=[VMEM()] * PLANE,
        out_specs=VMEM(),
        scratch_shapes=[pltpu.VMEM((3 * OUT_BLK, WOUT_LANES), F32)],
        cost_estimate=cost(5),
        compiler_params=pltpu.CompilerParams(vmem_limit_bytes=32 << 20),
        name="regroup",
    )(*parts)


def prep_kernel(frames_hbm, assign_hbm, gmid_hbm, gout_hbm, *refs):
    parts, (raw, order_out, pick_out, gmid_out, gout_out, limit_out) = refs[:LINE], refs[LINE : LINE + 6]
    gmid_ref, gout_ref, frames, assign, sems = refs[LINE + 6 :]
    moves = [(gmid_hbm, gmid_ref), (gout_hbm, gout_ref), (frames_hbm, frames), (assign_hbm, assign)]
    loads = [pltpu.make_async_copy(src, dst, sems.at[i]) for i, (src, dst) in enumerate(moves)]
    for load in loads:
        load.start()
    z, q, c = place()
    for k in range(LINE):
        raw[3 * OUT_BLK * k : 3 * OUT_BLK * (k + 1), :] = parts[k][...]
    row, channel = iota((C2, C2), 0), iota((C2, C2), 1)
    side, step = row // HALF_CH, row % HALF_CH // OUT_BLK
    flip = q ^ (2 * (c ^ side) + row % OUT_BLK // MID_SH)
    held = (c ^ (row % MID_SH // 6)) * HALF_CH + step * OUT_BLK + 6 * flip + row % 6
    order_out[...] = (channel == held).astype(F32).astype(BF16)
    r, l = iota((256, 256), 0), iota((256, 256), 1)
    same = (r // 8) == ((l // 64) % 2) * WL + l % WL
    mid_row = 2 * ((l // WL) % 4) + l // 128
    for b in range(3):
        pick_out[b] = (same & (mid_row == (c * 8 + r % 8 + b - 1) >> 1)).astype(F32).astype(BF16)
    for load in loads:
        load.wait()
    wanted = (2 * ((z - step) & (LINE - 1)) + (c ^ side)) * OUT_BLK + row % OUT_BLK
    column = jnp.sum(jnp.where(channel == wanted, gmid_ref[...], 0.0), axis=1, keepdims=True)
    gmid_out[...] = jnp.broadcast_to(column, (C2, 128))
    gout_out[...] = jnp.zeros((1, 128), F32)
    gout_out[:, :C3] = gout_ref[...]
    limit_out[...] = jnp.full((1, 128), frames[assign[z * PLANE + q]], jnp.int32).astype(F32)


def prep(frames, assign, gain_mid, gain_out, parts):
    return pl.pallas_call(
        prep_kernel,
        out_shape=[
            jax.ShapeDtypeStruct((LINE * 3 * OUT_BLK, WOUT_LANES), BF16),
            jax.ShapeDtypeStruct((C2, C2), BF16),
            jax.ShapeDtypeStruct((3, 256, 256), BF16),
            jax.ShapeDtypeStruct((C2, 128), F32),
            jax.ShapeDtypeStruct((1, 128), F32),
            jax.ShapeDtypeStruct((1, 128), F32),
        ],
        in_specs=[HBM()] * 4 + [VMEM()] * LINE,
        out_specs=[VMEM()] * 6,
        scratch_shapes=[
            pltpu.VMEM(gain_mid.shape, F32),
            pltpu.VMEM(gain_out.shape, F32),
            pltpu.SMEM(frames.shape, jnp.int32),
            pltpu.SMEM(assign.shape, jnp.int32),
            pltpu.SemaphoreType.DMA((4,)),
        ],
        cost_estimate=cost(0.01),
        compiler_params=pltpu.CompilerParams(vmem_limit_bytes=32 << 20),
        name="prep",
    )(*in_hbm(frames, assign, gain_mid, gain_out), *parts)


def wide_kernel(own, other, order, out, wf):
    wf[:, :, :, C3:] = jnp.zeros((3, 9, C2, 128 - C3), F32)
    for source, raw in enumerate((own, other)):
        for k in range(LINE):
            part = raw[72 * k : 72 * k + 72, :].astype(F32)
            at = (source * LINE + k) * OUT_BLK
            for j in range(9):
                tap = part[:, C3 * j : C3 * (j + 1)]
                for b in range(3):
                    wf[b, j, at : at + OUT_BLK, :C3] = tap[OUT_BLK * b : OUT_BLK * (b + 1)]
    for b in range(3):
        for j in range(9):
            moved = jnp.dot(order[...], wf[b, j].astype(BF16), preferred_element_type=F32)
            out[C2 * b : C2 * (b + 1), 128 * j : 128 * (j + 1)] = moved.astype(BF16)


def wide(own, other, order):
    return pl.pallas_call(
        wide_kernel,
        out_shape=jax.ShapeDtypeStruct((3 * C2, 1152), BF16),
        in_specs=[VMEM()] * 3,
        out_specs=VMEM(),
        scratch_shapes=[pltpu.VMEM((3, 9, C2, 128), F32)],
        cost_estimate=cost(0.01),
        compiler_params=pltpu.CompilerParams(vmem_limit_bytes=48 << 20),
        name="wide",
    )(own, other, order)


def stack_kernel(*refs):
    rows = refs[0].shape[0]
    for i, ref in enumerate(refs[:-1]):
        refs[-1][rows * i : rows * (i + 1), :] = ref[...]


def stack(parts, us=5):
    rows, lanes = parts[0].shape
    return pl.pallas_call(
        stack_kernel,
        out_shape=jax.ShapeDtypeStruct((len(parts) * rows, lanes), BF16),
        in_specs=[VMEM()] * len(parts),
        out_specs=VMEM(),
        cost_estimate=cost(us),
        compiler_params=pltpu.CompilerParams(vmem_limit_bytes=32 << 20),
        name="stack",
    )(*parts)


def out_kernel(own, other, w_all, pick, gmid_ref, gout_ref, limit_ref, out_ref, hid, lhs, prod):
    for side, group in enumerate((own, other)):
        for k in range(LINE):
            part = group[96 * k : 96 * k + 96, :].astype(F32)
            at = (side * LINE + k) * OUT_BLK
            for p in range(4):
                for tp in range(2):
                    hid[p, tp, at : at + OUT_BLK, :] = part[OUT_BLK * p : OUT_BLK * (p + 1), 128 * tp : 128 * tp + 128]
    acts = []
    for p in range(4):
        halves = []
        for tp in range(2):
            h = hid[p, tp]
            scale = lax.rsqrt(jnp.sum(h * h, axis=0, keepdims=True) * (1.0 / C2) + 1e-6)
            halves.append(silu(h * scale * gmid_ref[...]).astype(BF16))
        acts.append(halves)
    for b in range(3):
        for tp in range(2):
            for px in range(2):
                src = jnp.concatenate([acts[2 * py + px][tp] for py in range(2)], axis=1)
                rows = dot_nt(pick[b], src).astype(BF16)
                for half in range(2):
                    lhs[2 * tp + half, px, :, C2 * b : C2 * b + C2] = rows[128 * half : 128 * half + 128]
    prod[0:2] = jnp.dot(lhs[0:2].reshape(512, 3 * C2), w_all[...], preferred_element_type=F32).reshape(2, 2, 128, 1152)
    for t in (2, 3):
        at = 384 * (t - 1)
        prod[t, :, :, at:] = jnp.dot(
            lhs[t].reshape(256, 3 * C2), w_all[:, at:], preferred_element_type=F32
        ).reshape(2, 128, 1152 - at)
    lane = iota((1, 8, 128), 2)
    limit = limit_ref[...]
    below = [lane < 128 - 32 * i for i in range(4)]
    for t in range(FMAX):
        sums = []
        for px in range(2):
            row = []
            for e in range(3):
                total = None
                for a in range(3):
                    s = t + a - 2
                    if s < 0:
                        continue
                    at = 128 * (3 * a + e)
                    term = prod[s, px, :, at : at + 128].reshape(WL, 8, 128)
                    total = term if total is None else total + term
                row.append(total)
            sums.append(row)
        zero = jnp.zeros((1, 8, 128), F32)
        after = jnp.concatenate([sums[0][2][1:], zero], axis=0)
        before = jnp.concatenate([zero, sums[1][0][:-1]], axis=0)
        outs = [
            before + sums[0][1] + sums[0][2],
            sums[0][0] + sums[0][1] + sums[1][2],
            sums[0][0] + sums[1][1] + sums[1][2],
            sums[1][0] + sums[1][1] + after,
        ]
        vals = []
        for i, o in enumerate(outs):
            scale = lax.rsqrt(jnp.sum(o * o, axis=2, keepdims=True) * (1.0 / C3) + 1e-6)
            v = jnp.where(t < limit, silu(o * scale * gout_ref[...]), 0.0)
            vals.append(pltpu.roll(v, 128 - 32 * i, 2) if i else v)
        tiles = [
            jnp.where(lane < 96, vals[0], vals[1]),
            jnp.where(lane < 64, vals[1], vals[2]),
            jnp.where(lane < 32, vals[2], vals[3]),
        ]
        for x in range(WL):
            both = jnp.concatenate([tile[x] for tile in tiles], axis=1)
            out_ref[0, t, :, 384 * x : 384 * x + 384] = both.astype(BF16)


def finish(*rest):
    return pl.pallas_call(
        out_kernel,
        out_shape=jax.ShapeDtypeStruct((1, FMAX, 4 * RL, 4 * WL * C3), BF16),
        in_specs=[VMEM()] * len(rest),
        out_specs=VMEM(),
        scratch_shapes=[
            pltpu.VMEM((4, 2, C2, 128), F32),
            pltpu.VMEM((4, 2, 128, 3 * C2), BF16),
            pltpu.VMEM((4, 2, 128, 1152), F32),
        ],
        compiler_params=pltpu.CompilerParams(vmem_limit_bytes=48 << 20),
        cost_estimate=cost(4.8),
        name="finish",
    )(*rest)


def along_z(value, step):
    return lax.ppermute(value, "grp", [(g, (g + PLANE * step) % (LINE * PLANE)) for g in range(LINE * PLANE)])


def in_plane(value, flip):
    return lax.ppermute(value, "grp", [(g, g ^ flip) for g in range(LINE * PLANE)])


def other_core(value):
    return lax.ppermute(value, "row", [(0, 1), (1, 0)])


def per_device_fast(latents, frames, offsets, assign, w_in, w_mid, w_out, gain_in, gain_mid, gain_out):
    core = lax.axis_index("row")
    pieces = pack(offsets, assign, jnp.transpose(w_mid, (1, 0, 2)), latents)
    pieces = [pieces[0]] + [along_z(pieces[k], k) for k in range(1, LINE)]
    parts = join(pieces)
    parts = [parts[0]] + [in_plane(parts[d], d) for d in range(1, PLANE)]
    rows = lax.dynamic_slice_in_dim(w_out, core * 6, 6, axis=0)
    rows = rows.reshape(6, 3, 3, 3, C3).transpose(2, 0, 1, 3, 4).reshape(3, 6, 9 * C3)
    half = jnp.pad(rows, ((0, 0), (0, 2), (0, WOUT_LANES - 9 * C3))).reshape(24, WOUT_LANES)
    plane = regroup([half] + [in_plane(half, d) for d in range(1, PLANE)])
    own = [plane] + [along_z(plane, k) for k in range(1, LINE)]
    hidden = mid(frames, assign, parts, w_in.transpose(1, 0, 2).reshape(27 * ZC, C1), gain_in[None, :])
    own, _ = lax.optimization_barrier((own, hidden[0]))
    raw, order, pick, gmid, gout, limit = prep(frames, assign, gain_mid[None, :], gain_out[None, :], own)
    w_last = wide(raw, other_core(raw), order)
    hidden = stack([hidden[0]] + [along_z(hidden[k], k) for k in range(1, LINE)], 30)
    return finish(hidden, other_core(hidden), w_last, pick, gmid, gout, limit)


def solution(mesh):
    fast = mesh.shape["grp"] == LINE * PLANE and mesh.shape["row"] == 2
    placed = (
        P("grp", None),
        P(),
        P(),
        P(),
        P(),
        P("grp", None, None),
        P("grp", None, None),
        P(),
        P(),
        P(),
    )
    return jax.shard_map(
        per_device_fast if fast else per_device_general,
        mesh=mesh,
        in_specs=placed,
        out_specs=P("grp", None, "row", None),
        check_vma=False,
    )
```

```python
import functools

import jax
import jax.numpy as jnp
from jax import lax
from jax.experimental import pallas as pl
from jax.experimental.pallas import tpu as pltpu
from jax.sharding import PartitionSpec as P

RL = 2
WL = 16
FMAX = 4


def extended_2(cells, sides, width):
    for axis, dim in sides:
        count = lax.axis_size(axis)
        ends = count - 1
        head = lax.slice_in_dim(cells, 0, width, axis=dim)
        tail = lax.slice_in_dim(cells, cells.shape[dim] - width, cells.shape[dim], axis=dim)
        cells = jnp.concatenate(
            [
                lax.ppermute(tail, axis, [(i, (i + 1) % count) for i in range(ends)]),
                cells,
                lax.ppermute(head, axis, [((i + 1) % count, i) for i in range(ends)]),
            ],
            axis=dim,
        )
    return cells


def rms_silu(hidden, gain):
    mean_sq = jnp.mean(hidden * hidden, axis=-1, keepdims=True)
    scaled = hidden * lax.rsqrt(mean_sq + 1e-06) * gain
    return jax.nn.silu(scaled)


def causal_conv(extended, weight):
    count_t = extended.shape[0]
    count_r = extended.shape[1] - 2
    count_c = extended.shape[2]
    width_in = extended.shape[3]
    width_out = weight.shape[2]
    padded = jnp.pad(extended, ((2, 0), (0, 0), (1, 1), (0, 0)))
    total = jnp.zeros((count_t * count_r * count_c, width_out), jnp.float32)
    for time_tap in range(3):
        for row_tap in range(3):
            for col_tap in range(3):
                window = padded[
                    time_tap : time_tap + count_t,
                    row_tap : row_tap + count_r,
                    col_tap : col_tap + count_c,
                ]
                window = window.reshape(count_t * count_r * count_c, width_in)
                tap_index = 9 * time_tap + 3 * row_tap + col_tap
                total = total + jnp.dot(
                    window, weight[:, tap_index, :], preferred_element_type=jnp.float32
                )
    return total.reshape(count_t, count_r, count_c, width_out)


def upsample(values):
    return jnp.repeat(jnp.repeat(values, 2, axis=1), 2, axis=2)


def per_device_general(latents, frames, offsets, assign, w_in, w_mid, w_out, gain_in, gain_mid, gain_out):
    groups = lax.axis_size("grp")
    row_count = lax.axis_size("row")
    row_index = lax.axis_index("row")
    group_index = lax.axis_index("grp")
    channels = w_in.shape[0]
    cap_vals = latents.shape[1] // groups
    cap_tokens = cap_vals // channels
    span_len = cap_tokens // FMAX
    flat = latents[0]
    slot_ids = jnp.arange(cap_vals, dtype=jnp.int32)

    def select_span(request):
        start = offsets[request] * channels
        block = lax.dynamic_slice_in_dim(flat, start, cap_vals)
        keep = slot_ids < frames[request] * span_len * channels
        return jnp.where(keep, block, jnp.zeros((), block.dtype))

    outgoing = jax.vmap(select_span)(assign)
    incoming = lax.all_to_all(outgoing, "grp", split_axis=0, concat_axis=0, tiled=True)
    table = incoming.reshape(groups * cap_tokens, channels)
    request = assign[group_index]
    count = frames[request]
    fill_len = count * span_len
    image_rows = RL * row_count
    frame_ids = jnp.arange(FMAX, dtype=jnp.int32)[:, None, None]
    row_ids = row_index * RL + jnp.arange(RL, dtype=jnp.int32)[None, :, None]
    col_ids = jnp.arange(WL, dtype=jnp.int32)[None, None, :]
    position = (frame_ids * image_rows + row_ids) * WL + col_ids
    shard = jnp.minimum(position // fill_len, groups - 1)
    within = position % fill_len
    tokens = table[shard * cap_tokens + within]
    valid = (frame_ids < count)[..., None]
    latent_in = jnp.where(valid, tokens, jnp.zeros((), tokens.dtype))
    full_mid, full_out = (
        lax.all_gather(w_mid, "grp", axis=0, tiled=True),
        lax.all_gather(w_out, "grp", axis=0, tiled=True),
    )
    latent_ext = extended_2(latent_in, (("row", 1),), 1)
    act_in = rms_silu(causal_conv(latent_ext, w_in), gain_in).astype(jnp.bfloat16)
    mid_ext = extended_2(upsample(act_in), (("row", 1),), 1)
    act_mid = rms_silu(causal_conv(mid_ext, full_mid), gain_mid).astype(jnp.bfloat16)
    out_ext = extended_2(upsample(act_mid), (("row", 1),), 1)
    final = rms_silu(causal_conv(out_ext, full_out), gain_out)
    final = jnp.where(valid, final, jnp.zeros((), jnp.float32)).astype(jnp.bfloat16)
    return final.reshape(1, FMAX, 4 * RL, 4 * WL * final.shape[3])


LINE = 4
PLANE = 4
ZC, C1, C2, C3 = 16, 384, 192, 96
TOK = 16
IN_SH = C1 // 16
MID_SH = C2 // 16
OUT_BLK = C2 // (2 * LINE)
PIECE_ROWS = 80
USED = 9 * (C2 // (2 * LINE))
SPARE = 256 - USED
W_ROWS = 3 * IN_SH
B_ROWS = LINE * W_ROWS
WOUT_LANES = 896
HALF_CH = C2 // 2
F32, BF16 = jnp.float32, jnp.bfloat16
VMEM = functools.partial(pl.BlockSpec, memory_space=pltpu.VMEM)
SMEM = functools.partial(pl.BlockSpec, memory_space=pltpu.SMEM)
HBM = functools.partial(pl.BlockSpec, memory_space=pltpu.HBM)


def in_hbm(*values):
    return [pltpu.with_memory_space_constraint(v, pltpu.HBM) for v in values]


def cost(us):
    return pl.CostEstimate(flops=int(us * 1.15e9), bytes_accessed=0, transcendentals=0)


def iota(shape, dim):
    return lax.broadcasted_iota(jnp.int32, shape, dim)


def place():
    group = lax.axis_index("grp")
    return lax.div(group, PLANE), lax.rem(group, PLANE), lax.axis_index("row")


def silu(v):
    return v / (1.0 + jnp.exp(-v))


def dot_nt(lhs, rhs):
    return lax.dot_general(lhs, rhs, (((1,), (1,)), ((), ())), preferred_element_type=F32)


def hidden_lanes(table, part):
    moved = pltpu.roll(table, (USED - SPARE * part) % 256, 1)
    return jnp.where(iota(table.shape, 1) >= USED, moved, 0.0)


def found_lanes(rows, parts):
    table = jnp.zeros((TOK, 256), F32)
    for part in range(parts):
        moved = pltpu.roll(rows[TOK * part : TOK * (part + 1)], (SPARE * part - USED) % 256, 1)
        lane = iota((TOK, 256), 1)
        table = jnp.where((lane >= SPARE * part) & (lane < SPARE * (part + 1)), moved, table)
    return table


def pack_kernel(offsets_hbm, assign_hbm, w_hbm, lat_hbm, *refs):
    outs, (wf, lf, pf, tab, lat_rows, w_ref, lat_ref, offsets, assign, sems) = refs[:LINE], refs[LINE:]
    parts = [pl.ds(9 * a, 9) for a in range(3)]
    moves = [(w_hbm.at[p], w_ref.at[p]) for p in parts]
    moves = [(offsets_hbm, offsets), (assign_hbm, assign), (lat_hbm, lat_ref)] + moves
    copies = [pltpu.make_async_copy(src, dst, sems.at[i]) for i, (src, dst) in enumerate(moves)]
    for copy in copies:
        copy.start()
    z, _, c = place()
    lf[32:40, :] = jnp.zeros((8, 128), F32)
    for k in range(LINE):
        pf[k, W_ROWS:, :] = jnp.zeros((PIECE_ROWS - W_ROWS, 256), F32)
    lane1 = iota((1, 128), 1)
    for copy in copies[:3]:
        copy.wait()
    lat = lat_ref[...].astype(F32)
    for j in range(32):
        lf[j : j + 1, :] = lat[:, 128 * j : 128 * j + 128]
    for g in range(16):
        off = offsets[assign[g]]
        row, rem = lax.div(off, 8), lax.rem(off, 8)
        x = pltpu.roll(lf[pl.ds(row, 8), :], lax.rem(128 - ZC * rem, 128), 1)
        keep = lane1 < 128 - ZC * rem
        tab[g : g + 1, 0:128] = jnp.where(keep, x[0:1], x[1:2])
        tab[g : g + 1, 128:256] = jnp.where(keep, x[1:2], x[2:3])
    table = tab[...]
    for part in range(4):
        lat_rows[TOK * part : TOK * (part + 1), :] = hidden_lanes(table, part)
    lat_rows[4 * TOK : W_ROWS, :] = jnp.zeros((W_ROWS - 4 * TOK, 256), F32)
    low, high = pltpu.roll(table, 256 - 4 * SPARE, 1)[:8], pltpu.roll(table, 512 - 8 * SPARE, 1)[8:]
    lat_rows[W_ROWS:, :] = jnp.where(iota((8, 256), 1) < 256 - 4 * SPARE, low, high)
    for a in range(3):
        copies[3 + a].wait()
        wf[9 * a : 9 * a + 9, :, :C2] = w_ref[9 * a : 9 * a + 9].astype(F32)
    lane = iota((IN_SH, 128), 1)

    def choose(core):
        for line in range(LINE):
            start = (2 * line + core) * OUT_BLK
            tile, into = start // 128, start % 128
            for b in range(3):
                acc = [jnp.zeros((IN_SH, 128), F32)] * 2
                for j in range(9):
                    tap = 9 * (j // 3) + 3 * b + j % 3
                    x = wf[tap, :, 128 * tile : 128 * tile + 128]
                    if into + OUT_BLK > 128:
                        x = jnp.where(lane >= into, x, wf[tap, :, 128 : 256])
                    at, to = OUT_BLK * j // 128, OUT_BLK * j % 128
                    moved = pltpu.roll(x, (to - into) % 128, 1)
                    acc[at] = jnp.where((lane >= to) & (lane < to + OUT_BLK), moved, acc[at])
                    if to + OUT_BLK > 128:
                        acc[at + 1] = jnp.where(lane < to + OUT_BLK - 128, moved, acc[at + 1])
                for half in range(2):
                    pf[line, IN_SH * b : IN_SH * (b + 1), 128 * half : 128 * half + 128] = acc[half]

    for core in range(2):
        pl.when(c == core)(functools.partial(choose, core))
    for k in range(LINE):
        outs[k][...] = (pf[lax.rem(z + k, LINE)] + lat_rows[...]).astype(BF16)


def pack(offsets, assign, w_mid, latents):
    piece = jax.ShapeDtypeStruct((PIECE_ROWS, 256), BF16)
    return pl.pallas_call(
        pack_kernel,
        out_shape=[piece] * LINE,
        in_specs=[HBM()] * 4,
        out_specs=[VMEM()] * LINE,
        scratch_shapes=[
            pltpu.VMEM((27, IN_SH, 256), F32),
            pltpu.VMEM((40, 128), F32),
            pltpu.VMEM((LINE, PIECE_ROWS, 256), F32),
            pltpu.VMEM((TOK, 256), F32),
            pltpu.VMEM((PIECE_ROWS, 256), F32),
            pltpu.VMEM((27, IN_SH, C2), BF16),
            pltpu.VMEM(latents.shape, BF16),
            pltpu.SMEM(offsets.shape, jnp.int32),
            pltpu.SMEM(assign.shape, jnp.int32),
            pltpu.SemaphoreType.DMA((6,)),
        ],
        cost_estimate=cost(2),
        compiler_params=pltpu.CompilerParams(vmem_limit_bytes=32 << 20),
        name="pack",
    )(*in_hbm(offsets, assign, w_mid, latents))


def join_kernel(*refs):
    pieces, outs, (pf, bf, tab) = refs[:LINE], refs[LINE : LINE + PLANE], refs[LINE + PLANE :]
    _, q, _ = place()
    lane = iota((8, 256), 1)
    for k in range(LINE):
        whole = pieces[k][...].astype(F32)
        bf[W_ROWS * k : W_ROWS * (k + 1), :] = whole[:W_ROWS]
        table, rest = found_lanes(whole, 4), whole[W_ROWS:]
        low, high = pltpu.roll(rest, 4 * SPARE, 1), pltpu.roll(rest, 8 * SPARE - 256, 1)
        pf[TOK * k : TOK * k + 8, :] = jnp.where(lane >= 4 * SPARE, low, table[:8])
        pf[TOK * k + 8 : TOK * (k + 1), :] = jnp.where(lane >= 4 * SPARE, high, table[8:])
    for d in range(PLANE):
        for k in range(LINE):
            for line in range(LINE):
                at = LINE * k + line
                tab[at : at + 1, :] = pf[pl.ds(TOK * k + PLANE * line + (q ^ d), 1), :]
        table = tab[...]
        keep = iota((TOK, 256), 1) < USED
        for part in range(7):
            rows = slice(TOK * part, TOK * (part + 1))
            bf[rows, :] = jnp.where(keep, bf[rows, :], hidden_lanes(table, part))
        outs[d][...] = bf[...].astype(BF16)


def join(pieces):
    out = jax.ShapeDtypeStruct((B_ROWS, 256), BF16)
    return pl.pallas_call(
        join_kernel,
        out_shape=[out] * PLANE,
        in_specs=[VMEM()] * LINE,
        out_specs=[VMEM()] * PLANE,
        scratch_shapes=[
            pltpu.VMEM((LINE * TOK, 256), F32),
            pltpu.VMEM((B_ROWS, 256), F32),
            pltpu.VMEM((TOK, 256), F32),
        ],
        compiler_params=pltpu.CompilerParams(vmem_limit_bytes=32 << 20),
        cost_estimate=cost(5),
        name="join",
    )(*pieces)


def mid_kernel(frames_hbm, assign_hbm, win_hbm, gain_ref, *refs):
    parts, outs = refs[:PLANE], refs[PLANE : PLANE + LINE]
    lt, xs, tokens, shifted, w1, act, wf, frames, assign, sems = refs[PLANE + LINE :]
    z, q, _ = place()
    moves = [(frames_hbm, frames), (assign_hbm, assign), (win_hbm, w1.at[0 : 27 * ZC])]
    loads = [pltpu.make_async_copy(src, dst, sems.at[i]) for i, (src, dst) in enumerate(moves)]
    for load in loads:
        load.start()
    w1[27 * ZC :, :] = jnp.zeros((512 - 27 * ZC, C1), BF16)
    for d in range(PLANE):
        part = parts[d][...].astype(F32)
        lt[...] = found_lanes(part, 7)
        for k in range(LINE):
            shard = lax.rem(z - k + LINE, LINE) * PLANE + (q ^ d)
            for b in range(3):
                at = W_ROWS * k + IN_SH * b
                wf[b, pl.ds(pl.multiple_of(shard * IN_SH, 8), IN_SH), :] = part[at : at + IN_SH]
            for i in range(LINE):
                xs[i, pl.ds(shard, 1), :] = lt[pl.ds(LINE * k + lax.rem(z + i, LINE), 1), :]
    own_lane = iota((16, 16, 256), 1) == iota((16, 16, 256), 2) // ZC
    repeat = (iota((256, 128), 0) % ZC == iota((256, 128), 1) % ZC).astype(F32).astype(BF16)
    lane, col = iota((256, 128), 1), iota((256, 128), 0) % WL
    inner_l, inner_r = col > 0, col < WL - 1
    block = lane // ZC
    tap_col = [(block + r) % 3 for r in range(3)]
    lane1 = iota((1, 128), 1)
    zero_rows = jnp.zeros((2, 6, WL, 128), BF16)
    zero_cols = jnp.zeros((4, 1, WL, 128), BF16)
    for load in loads[:2]:
        load.wait()
    for i in range(LINE):
        fill = frames[assign[lax.rem(z + i, LINE) * PLANE + q]] * (TOK // FMAX)
        spread = jnp.where(own_lane, jnp.broadcast_to(xs[i][:, None, :], (16, 16, 256)), 0.0)
        rows = jnp.dot(spread.reshape(256, 256).astype(BF16), repeat, preferred_element_type=F32)
        tokens[i] = jnp.zeros((288, 128), F32)
        for shard in range(16):
            tokens[i, pl.ds(8 + shard * fill, TOK), :] = rows[TOK * shard : TOK * (shard + 1)]
        tokens[i, pl.ds(8 + 16 * fill, TOK), :] = jnp.zeros((TOK, 128), F32)
        here = tokens[i, 8:264, :]
        left = jnp.where(inner_l, tokens[i, 7:263, :], 0.0)
        right = jnp.where(inner_r, tokens[i, 9:265, :], 0.0)
        for r in range(3):
            v = jnp.where(tap_col[r] == 0, left, jnp.where(tap_col[r] == 1, here, right)).astype(BF16)
            shifted[i, r, 0:2] = zero_rows
            shifted[i, r, 2:6, 0:1] = zero_cols
            shifted[i, r, 2:6, 5:6] = zero_cols
            shifted[i, r, 2:6, 1:5] = v.reshape(4, 4, WL, 128)
    for load in loads[2:]:
        load.wait()
    for i in range(LINE):
        tiles = []
        for j in range(4):
            tile = None
            for tap in range(8 * j // 3, min(8 * j + 7, 26) // 3 + 1):
                a, b = divmod(tap, 3)
                lo, hi = max(3 * tap - 8 * j, 0) * ZC, min(3 * tap + 3 - 8 * j, 8) * ZC
                keep = ((lane1 >= lo) & (lane1 < hi)).astype(F32).astype(BF16)
                term = shifted[i, 8 * j % 3, a : a + 4, b : b + 4].reshape(256, 128) * keep
                tile = term if tile is None else tile + term
            tiles.append(tile)
        h = jnp.dot(jnp.concatenate(tiles, axis=1), w1[...], preferred_element_type=F32)
        scale = lax.rsqrt(jnp.mean(h * h, axis=1, keepdims=True) + 1e-6)
        act[256 * i : 256 * i + 256, :] = silu(h * scale * gain_ref[...]).astype(BF16)
    lanes = LINE * 256
    at = iota((OUT_BLK, lanes), 1)
    frame, row, column = (at // 64) % FMAX, (at // WL) % 4, at % WL
    summed = []
    for b in range(3):
        prod = dot_nt(wf[b].T.astype(BF16), act[...])
        for e in range(3):
            now, before, two = (prod[OUT_BLK * (3 * a + e) : OUT_BLK * (3 * a + e + 1)] for a in (2, 1, 0))
            summed.append(
                now
                + jnp.where(frame >= 1, pltpu.roll(before, 64, 1), 0.0)
                + jnp.where(frame >= 2, pltpu.roll(two, 128, 1), 0.0)
            )
    halves = [[], []]
    for b in range(3):
        e0, e1, e2 = summed[3 * b : 3 * b + 3]
        halves[0].append(jnp.where(column > 0, pltpu.roll(e0, 1, 1), 0.0) + e1 + e2)
        halves[1].append(e0 + e1 + jnp.where(column < WL - 1, pltpu.roll(e2, lanes - 1, 1), 0.0))
    phases = [None] * 4
    for px in range(2):
        b0, b1, b2 = halves[px]
        phases[px] = jnp.where(row > 0, pltpu.roll(b0, WL, 1), 0.0) + b1 + b2
        phases[2 + px] = b0 + b1 + jnp.where(row < 3, pltpu.roll(b2, lanes - WL, 1), 0.0)
    for i in range(LINE):
        outs[i][...] = jnp.concatenate([p[:, 256 * i : 256 * i + 256] for p in phases], axis=0).astype(BF16)


def mid(frames, assign, parts, w_in, gain_in):
    out = jax.ShapeDtypeStruct((4 * OUT_BLK, 256), BF16)
    return pl.pallas_call(
        mid_kernel,
        out_shape=[out] * LINE,
        in_specs=[HBM()] * 3 + [VMEM()] * (PLANE + 1),
        out_specs=[VMEM()] * LINE,
        scratch_shapes=[
            pltpu.VMEM((LINE * LINE, 256), F32),
            pltpu.VMEM((LINE, 16, 256), F32),
            pltpu.VMEM((LINE, 288, 128), F32),
            pltpu.VMEM((LINE, 3, 6, 6, WL, 128), BF16),
            pltpu.VMEM((512, C1), BF16),
            pltpu.VMEM((LINE * 256, C1), BF16),
            pltpu.VMEM((3, C1, 256), F32),
            pltpu.SMEM(frames.shape, jnp.int32),
            pltpu.SMEM(assign.shape, jnp.int32),
            pltpu.SemaphoreType.DMA((3,)),
        ],
        compiler_params=pltpu.CompilerParams(vmem_limit_bytes=48 << 20),
        cost_estimate=cost(5),
        name="mid",
    )(*in_hbm(frames, assign, w_in), gain_in, *parts)


def regroup_kernel(half, near, far, out, rows):
    for b in range(3):
        at = OUT_BLK * b
        rows[at : at + 6, :] = half[8 * b : 8 * b + 6, :].astype(F32)
        rows[at + 6 : at + 18, :] = near[16 * b : 16 * b + 16, :].astype(F32)[:MID_SH]
        rows[at + 18 : at + 24, :] = far[8 * b : 8 * b + 6, :].astype(F32)
    out[...] = rows[...].astype(BF16)


def regroup(half, near, far):
    return pl.pallas_call(
        regroup_kernel,
        out_shape=jax.ShapeDtypeStruct((3 * OUT_BLK, WOUT_LANES), BF16),
        in_specs=[VMEM()] * 3,
        out_specs=VMEM(),
        scratch_shapes=[pltpu.VMEM((3 * OUT_BLK, WOUT_LANES), F32)],
        cost_estimate=cost(5),
        compiler_params=pltpu.CompilerParams(vmem_limit_bytes=32 << 20),
        name="regroup",
    )(half, near, far)


def prep_kernel(frames_hbm, assign_hbm, gmid_hbm, gout_hbm, *refs):
    parts, (raw, order_out, pick_out, gmid_out, gout_out, limit_out) = refs[:LINE], refs[LINE : LINE + 6]
    gmid_ref, gout_ref, frames, assign, sems = refs[LINE + 6 :]
    moves = [(gmid_hbm, gmid_ref), (gout_hbm, gout_ref), (frames_hbm, frames), (assign_hbm, assign)]
    loads = [pltpu.make_async_copy(src, dst, sems.at[i]) for i, (src, dst) in enumerate(moves)]
    for load in loads:
        load.start()
    z, q, c = place()
    for k in range(LINE):
        raw[3 * OUT_BLK * k : 3 * OUT_BLK * (k + 1), :] = parts[k][...]
    row, channel = iota((C2, C2), 0), iota((C2, C2), 1)
    side, step, in_shard = row // HALF_CH, row % HALF_CH // OUT_BLK, row % MID_SH
    flip = q ^ (2 * (c ^ side) + row % OUT_BLK // MID_SH)
    near = (flip == 1) | (flip == 2)
    holder = jnp.where(near, flip - 1, in_shard // 6)
    slot = jnp.where(near, 6 + in_shard, 6 * flip + in_shard % 6)
    held = (c ^ holder) * HALF_CH + step * OUT_BLK + slot
    order_out[...] = (channel == held).astype(F32).astype(BF16)
    r, l = iota((256, 256), 0), iota((256, 256), 1)
    same = (r // 8) == ((l // 64) % 2) * WL + l % WL
    mid_row = 2 * ((l // WL) % 4) + l // 128
    for b in range(3):
        pick_out[b] = (same & (mid_row == (c * 8 + r % 8 + b - 1) >> 1)).astype(F32).astype(BF16)
    for load in loads:
        load.wait()
    wanted = (2 * ((z - step) & (LINE - 1)) + (c ^ side)) * OUT_BLK + row % OUT_BLK
    column = jnp.sum(jnp.where(channel == wanted, gmid_ref[...], 0.0), axis=1, keepdims=True)
    gmid_out[...] = jnp.broadcast_to(column, (C2, 128))
    gout_out[...] = jnp.zeros((1, 128), F32)
    gout_out[:, :C3] = gout_ref[...]
    limit_out[...] = jnp.full((1, 128), frames[assign[z * PLANE + q]], jnp.int32).astype(F32)


def prep(frames, assign, gain_mid, gain_out, parts):
    return pl.pallas_call(
        prep_kernel,
        out_shape=[
            jax.ShapeDtypeStruct((LINE * 3 * OUT_BLK, WOUT_LANES), BF16),
            jax.ShapeDtypeStruct((C2, C2), BF16),
            jax.ShapeDtypeStruct((3, 256, 256), BF16),
            jax.ShapeDtypeStruct((C2, 128), F32),
            jax.ShapeDtypeStruct((1, 128), F32),
            jax.ShapeDtypeStruct((1, 128), F32),
        ],
        in_specs=[HBM()] * 4 + [VMEM()] * LINE,
        out_specs=[VMEM()] * 6,
        scratch_shapes=[
            pltpu.VMEM(gain_mid.shape, F32),
            pltpu.VMEM(gain_out.shape, F32),
            pltpu.SMEM(frames.shape, jnp.int32),
            pltpu.SMEM(assign.shape, jnp.int32),
            pltpu.SemaphoreType.DMA((4,)),
        ],
        cost_estimate=cost(0.01),
        compiler_params=pltpu.CompilerParams(vmem_limit_bytes=32 << 20),
        name="prep",
    )(*in_hbm(frames, assign, gain_mid, gain_out), *parts)


def wide_kernel(own, other, order, out, wf):
    wf[:, :, :, C3:] = jnp.zeros((3, 9, C2, 128 - C3), F32)
    for source, raw in enumerate((own, other)):
        for k in range(LINE):
            part = raw[72 * k : 72 * k + 72, :].astype(F32)
            at = (source * LINE + k) * OUT_BLK
            for j in range(9):
                tap = part[:, C3 * j : C3 * (j + 1)]
                for b in range(3):
                    wf[b, j, at : at + OUT_BLK, :C3] = tap[OUT_BLK * b : OUT_BLK * (b + 1)]
    for b in range(3):
        for j in range(9):
            moved = jnp.dot(order[...], wf[b, j].astype(BF16), preferred_element_type=F32)
            out[C2 * b : C2 * (b + 1), 128 * j : 128 * (j + 1)] = moved.astype(BF16)


def wide(own, other, order):
    return pl.pallas_call(
        wide_kernel,
        out_shape=jax.ShapeDtypeStruct((3 * C2, 1152), BF16),
        in_specs=[VMEM()] * 3,
        out_specs=VMEM(),
        scratch_shapes=[pltpu.VMEM((3, 9, C2, 128), F32)],
        cost_estimate=cost(0.01),
        compiler_params=pltpu.CompilerParams(vmem_limit_bytes=48 << 20),
        name="wide",
    )(own, other, order)


def stack_kernel(*refs):
    rows = refs[0].shape[0]
    for i, ref in enumerate(refs[:-1]):
        refs[-1][rows * i : rows * (i + 1), :] = ref[...]


def stack(parts, us=5):
    rows, lanes = parts[0].shape
    return pl.pallas_call(
        stack_kernel,
        out_shape=jax.ShapeDtypeStruct((len(parts) * rows, lanes), BF16),
        in_specs=[VMEM()] * len(parts),
        out_specs=VMEM(),
        cost_estimate=cost(us),
        compiler_params=pltpu.CompilerParams(vmem_limit_bytes=32 << 20),
        name="stack",
    )(*parts)


def out_kernel(own, other, w_all, pick, gmid_ref, gout_ref, limit_ref, out_hbm, hid, lhs, prod, out_ref, sems):
    for side, group in enumerate((own, other)):
        for k in range(LINE):
            part = group[96 * k : 96 * k + 96, :].astype(F32)
            at = (side * LINE + k) * OUT_BLK
            for p in range(4):
                for tp in range(2):
                    hid[p, tp, at : at + OUT_BLK, :] = part[OUT_BLK * p : OUT_BLK * (p + 1), 128 * tp : 128 * tp + 128]
    acts = []
    for p in range(4):
        halves = []
        for tp in range(2):
            h = hid[p, tp]
            scale = lax.rsqrt(jnp.sum(h * h, axis=0, keepdims=True) * (1.0 / C2) + 1e-6)
            halves.append(silu(h * scale * gmid_ref[...]).astype(BF16))
        acts.append(halves)
    for b in range(3):
        for tp in range(2):
            for px in range(2):
                src = jnp.concatenate([acts[2 * py + px][tp] for py in range(2)], axis=1)
                rows = dot_nt(pick[b], src).astype(BF16)
                for half in range(2):
                    lhs[2 * tp + half, px, :, C2 * b : C2 * b + C2] = rows[128 * half : 128 * half + 128]
    lane = iota((1, 8, 128), 2)
    limit = limit_ref[...]
    below = [lane < 128 - 32 * i for i in range(4)]
    def multiply(t):
        if t == 0:
            both = jnp.dot(lhs[0:2].reshape(512, 3 * C2), w_all[...], preferred_element_type=F32)
            prod[0:2] = both.reshape(2, 2, 128, 1152)
        elif t > 1:
            at = 384 * (t - 1)
            prod[t, :, :, at:] = jnp.dot(
                lhs[t].reshape(256, 3 * C2), w_all[:, at:], preferred_element_type=F32
            ).reshape(2, 128, 1152 - at)

    def combine(t):
        sums = []
        for px in range(2):
            row = []
            for e in range(3):
                total = None
                for a in range(3):
                    s = t + a - 2
                    if s < 0:
                        continue
                    at = 128 * (3 * a + e)
                    term = prod[s, px, :, at : at + 128].reshape(WL, 8, 128)
                    total = term if total is None else total + term
                row.append(total)
            sums.append(row)
        zero = jnp.zeros((1, 8, 128), F32)
        after = jnp.concatenate([sums[0][2][1:], zero], axis=0)
        before = jnp.concatenate([zero, sums[1][0][:-1]], axis=0)
        outs = [
            before + sums[0][1] + sums[0][2],
            sums[0][0] + sums[0][1] + sums[1][2],
            sums[0][0] + sums[1][1] + sums[1][2],
            sums[1][0] + sums[1][1] + after,
        ]
        vals = []
        for i, o in enumerate(outs):
            scale = lax.rsqrt(jnp.sum(o * o, axis=2, keepdims=True) * (1.0 / C3) + 1e-6)
            v = jnp.where(t < limit, silu(o * scale * gout_ref[...]), 0.0)
            vals.append(pltpu.roll(v, 128 - 32 * i, 2) if i else v)
        tiles = [
            jnp.where(lane < 96, vals[0], vals[1]),
            jnp.where(lane < 64, vals[1], vals[2]),
            jnp.where(lane < 32, vals[2], vals[3]),
        ]
        for x in range(WL):
            both = jnp.concatenate([tile[x] for tile in tiles], axis=1)
            out_ref[0, t, :, 384 * x : 384 * x + 384] = both.astype(BF16)

    copies = [pltpu.make_async_copy(out_ref.at[:, t], out_hbm.at[:, t], sems.at[t]) for t in range(FMAX)]
    multiply(0)
    multiply(2)
    combine(0)
    copies[0].start()
    multiply(3)
    combine(1)
    copies[1].start()
    combine(2)
    copies[2].start()
    combine(3)
    copies[3].start()
    for copy in copies:
        copy.wait()


def finish(*rest):
    return pl.pallas_call(
        out_kernel,
        out_shape=jax.ShapeDtypeStruct((1, FMAX, 4 * RL, 4 * WL * C3), BF16),
        in_specs=[VMEM()] * len(rest),
        out_specs=HBM(),
        scratch_shapes=[
            pltpu.VMEM((4, 2, C2, 128), F32),
            pltpu.VMEM((4, 2, 128, 3 * C2), BF16),
            pltpu.VMEM((4, 2, 128, 1152), F32),
            pltpu.VMEM((1, FMAX, 4 * RL, 4 * WL * C3), BF16),
            pltpu.SemaphoreType.DMA((FMAX,)),
        ],
        compiler_params=pltpu.CompilerParams(vmem_limit_bytes=48 << 20),
        cost_estimate=cost(4.8),
        name="finish",
    )(*rest)


def along_z(value, step):
    return lax.ppermute(value, "grp", [(g, (g + PLANE * step) % (LINE * PLANE)) for g in range(LINE * PLANE)])


def in_plane(value, flip):
    return lax.ppermute(value, "grp", [(g, g ^ flip) for g in range(LINE * PLANE)])


def near_chip(value):
    pairs = [(2 * g + c, 2 * (g ^ (1 + c)) + c) for g in range(LINE * PLANE) for c in range(2)]
    return lax.ppermute(value, ("grp", "row"), pairs)


def other_core(value):
    return lax.ppermute(value, "row", [(0, 1), (1, 0)])


def per_device_fast(latents, frames, offsets, assign, w_in, w_mid, w_out, gain_in, gain_mid, gain_out):
    core = lax.axis_index("row")
    pieces = pack(offsets, assign, jnp.transpose(w_mid, (1, 0, 2)), latents)
    pieces = [pieces[0]] + [along_z(pieces[k], k) for k in range(1, LINE)]
    parts = join(pieces)
    parts = [parts[0]] + [in_plane(parts[d], d) for d in range(1, PLANE)]
    full = w_out.reshape(MID_SH, 3, 3, 3, C3).transpose(2, 0, 1, 3, 4).reshape(3, MID_SH, 9 * C3)
    half = lax.dynamic_slice_in_dim(full, core * 6, 6, axis=1)
    full = jnp.pad(full, ((0, 0), (0, 16 - MID_SH), (0, WOUT_LANES - 9 * C3))).reshape(48, WOUT_LANES)
    half = jnp.pad(half, ((0, 0), (0, 2), (0, WOUT_LANES - 9 * C3))).reshape(24, WOUT_LANES)
    plane = regroup(half, near_chip(full), in_plane(half, 3))
    own = [plane] + [along_z(plane, k) for k in range(1, LINE)]
    hidden = mid(frames, assign, parts, w_in.transpose(1, 0, 2).reshape(27 * ZC, C1), gain_in[None, :])
    own, _ = lax.optimization_barrier((own, hidden[0]))
    raw, order, pick, gmid, gout, limit = prep(frames, assign, gain_mid[None, :], gain_out[None, :], own)
    w_last = wide(raw, other_core(raw), order)
    hidden = stack([hidden[0]] + [along_z(hidden[k], k) for k in range(1, LINE)], 30)
    return finish(hidden, other_core(hidden), w_last, pick, gmid, gout, limit)


def solution(mesh):
    fast = mesh.shape["grp"] == LINE * PLANE and mesh.shape["row"] == 2
    placed = (
        P("grp", None),
        P(),
        P(),
        P(),
        P(),
        P("grp", None, None),
        P("grp", None, None),
        P(),
        P(),
        P(),
    )
    return jax.shard_map(
        per_device_fast if fast else per_device_general,
        mesh=mesh,
        in_specs=placed,
        out_specs=P("grp", None, "row", None),
        check_vma=False,
    )
```

```python
import functools

import jax
import jax.numpy as jnp
from jax import lax
from jax.experimental import pallas as pl
from jax.experimental.pallas import tpu as pltpu
from jax.sharding import PartitionSpec as P

RL = 2
WL = 16
FMAX = 4


def extended_2(cells, sides, width):
    for axis, dim in sides:
        count = lax.axis_size(axis)
        ends = count - 1
        head = lax.slice_in_dim(cells, 0, width, axis=dim)
        tail = lax.slice_in_dim(cells, cells.shape[dim] - width, cells.shape[dim], axis=dim)
        cells = jnp.concatenate(
            [
                lax.ppermute(tail, axis, [(i, (i + 1) % count) for i in range(ends)]),
                cells,
                lax.ppermute(head, axis, [((i + 1) % count, i) for i in range(ends)]),
            ],
            axis=dim,
        )
    return cells


def rms_silu(hidden, gain):
    mean_sq = jnp.mean(hidden * hidden, axis=-1, keepdims=True)
    scaled = hidden * lax.rsqrt(mean_sq + 1e-06) * gain
    return jax.nn.silu(scaled)


def causal_conv(extended, weight):
    count_t = extended.shape[0]
    count_r = extended.shape[1] - 2
    count_c = extended.shape[2]
    width_in = extended.shape[3]
    width_out = weight.shape[2]
    padded = jnp.pad(extended, ((2, 0), (0, 0), (1, 1), (0, 0)))
    total = jnp.zeros((count_t * count_r * count_c, width_out), jnp.float32)
    for time_tap in range(3):
        for row_tap in range(3):
            for col_tap in range(3):
                window = padded[
                    time_tap : time_tap + count_t,
                    row_tap : row_tap + count_r,
                    col_tap : col_tap + count_c,
                ]
                window = window.reshape(count_t * count_r * count_c, width_in)
                tap_index = 9 * time_tap + 3 * row_tap + col_tap
                total = total + jnp.dot(
                    window, weight[:, tap_index, :], preferred_element_type=jnp.float32
                )
    return total.reshape(count_t, count_r, count_c, width_out)


def upsample(values):
    return jnp.repeat(jnp.repeat(values, 2, axis=1), 2, axis=2)


def per_device_general(latents, frames, offsets, assign, w_in, w_mid, w_out, gain_in, gain_mid, gain_out):
    groups = lax.axis_size("grp")
    row_count = lax.axis_size("row")
    row_index = lax.axis_index("row")
    group_index = lax.axis_index("grp")
    channels = w_in.shape[0]
    cap_vals = latents.shape[1] // groups
    cap_tokens = cap_vals // channels
    span_len = cap_tokens // FMAX
    flat = latents[0]
    slot_ids = jnp.arange(cap_vals, dtype=jnp.int32)

    def select_span(request):
        start = offsets[request] * channels
        block = lax.dynamic_slice_in_dim(flat, start, cap_vals)
        keep = slot_ids < frames[request] * span_len * channels
        return jnp.where(keep, block, jnp.zeros((), block.dtype))

    outgoing = jax.vmap(select_span)(assign)
    incoming = lax.all_to_all(outgoing, "grp", split_axis=0, concat_axis=0, tiled=True)
    table = incoming.reshape(groups * cap_tokens, channels)
    request = assign[group_index]
    count = frames[request]
    fill_len = count * span_len
    image_rows = RL * row_count
    frame_ids = jnp.arange(FMAX, dtype=jnp.int32)[:, None, None]
    row_ids = row_index * RL + jnp.arange(RL, dtype=jnp.int32)[None, :, None]
    col_ids = jnp.arange(WL, dtype=jnp.int32)[None, None, :]
    position = (frame_ids * image_rows + row_ids) * WL + col_ids
    shard = jnp.minimum(position // fill_len, groups - 1)
    within = position % fill_len
    tokens = table[shard * cap_tokens + within]
    valid = (frame_ids < count)[..., None]
    latent_in = jnp.where(valid, tokens, jnp.zeros((), tokens.dtype))
    full_mid, full_out = (
        lax.all_gather(w_mid, "grp", axis=0, tiled=True),
        lax.all_gather(w_out, "grp", axis=0, tiled=True),
    )
    latent_ext = extended_2(latent_in, (("row", 1),), 1)
    act_in = rms_silu(causal_conv(latent_ext, w_in), gain_in).astype(jnp.bfloat16)
    mid_ext = extended_2(upsample(act_in), (("row", 1),), 1)
    act_mid = rms_silu(causal_conv(mid_ext, full_mid), gain_mid).astype(jnp.bfloat16)
    out_ext = extended_2(upsample(act_mid), (("row", 1),), 1)
    final = rms_silu(causal_conv(out_ext, full_out), gain_out)
    final = jnp.where(valid, final, jnp.zeros((), jnp.float32)).astype(jnp.bfloat16)
    return final.reshape(1, FMAX, 4 * RL, 4 * WL * final.shape[3])


LINE = 4
PLANE = 4
ZC, C1, C2, C3 = 16, 384, 192, 96
TOK = 16
IN_SH = C1 // 16
MID_SH = C2 // 16
OUT_BLK = C2 // (2 * LINE)
PIECE_ROWS = 80
USED = 9 * (C2 // (2 * LINE))
SPARE = 256 - USED
W_ROWS = 3 * IN_SH
B_ROWS = LINE * W_ROWS
WOUT_LANES = 896
HALF_CH = C2 // 2
F32, BF16 = jnp.float32, jnp.bfloat16
VMEM = functools.partial(pl.BlockSpec, memory_space=pltpu.VMEM)
SMEM = functools.partial(pl.BlockSpec, memory_space=pltpu.SMEM)
HBM = functools.partial(pl.BlockSpec, memory_space=pltpu.HBM)


def in_hbm(*values):
    return [pltpu.with_memory_space_constraint(v, pltpu.HBM) for v in values]


def cost(us):
    return pl.CostEstimate(flops=int(us * 1.15e9), bytes_accessed=0, transcendentals=0)


def iota(shape, dim):
    return lax.broadcasted_iota(jnp.int32, shape, dim)


def place():
    group = lax.axis_index("grp")
    return lax.div(group, PLANE), lax.rem(group, PLANE), lax.axis_index("row")


def silu(v):
    return v / (1.0 + jnp.exp(-v))


def dot_nt(lhs, rhs):
    return lax.dot_general(lhs, rhs, (((1,), (1,)), ((), ())), preferred_element_type=F32)


def hidden_lanes(table, part):
    moved = pltpu.roll(table, (USED - SPARE * part) % 256, 1)
    return jnp.where(iota(table.shape, 1) >= USED, moved, 0.0)


def found_lanes(rows, parts):
    table = jnp.zeros((TOK, 256), F32)
    for part in range(parts):
        moved = pltpu.roll(rows[TOK * part : TOK * (part + 1)], (SPARE * part - USED) % 256, 1)
        lane = iota((TOK, 256), 1)
        table = jnp.where((lane >= SPARE * part) & (lane < SPARE * (part + 1)), moved, table)
    return table


def pack_kernel(offsets_hbm, assign_hbm, w_hbm, lat_hbm, win_hbm, frames_hbm, *refs):
    outs, w1, fills, (frames, wf, lf, pf, tab, lat_rows, w_ref, lat_ref, offsets, assign, sems) = refs[:LINE], refs[LINE], refs[LINE + 1], refs[LINE + 2 :]
    parts = [pl.ds(9 * a, 9) for a in range(3)]
    moves = [(w_hbm.at[p], w_ref.at[p]) for p in parts]
    moves = [(offsets_hbm, offsets), (assign_hbm, assign), (lat_hbm, lat_ref)] + moves
    moves += [(win_hbm, w1.at[0 : 27 * ZC]), (frames_hbm, frames)]
    copies = [pltpu.make_async_copy(src, dst, sems.at[i]) for i, (src, dst) in enumerate(moves)]
    for copy in copies:
        copy.start()
    z, q, c = place()
    lf[32:40, :] = jnp.zeros((8, 128), F32)
    w1[27 * ZC :, :] = jnp.zeros((512 - 27 * ZC, C1), BF16)
    for k in range(LINE):
        pf[k, W_ROWS:, :] = jnp.zeros((PIECE_ROWS - W_ROWS, 256), F32)
    lane1 = iota((1, 128), 1)
    for copy in copies[:3]:
        copy.wait()
    lat = lat_ref[...].astype(F32)
    for j in range(32):
        lf[j : j + 1, :] = lat[:, 128 * j : 128 * j + 128]
    for g in range(16):
        off = offsets[assign[g]]
        row, rem = lax.div(off, 8), lax.rem(off, 8)
        x = pltpu.roll(lf[pl.ds(row, 8), :], lax.rem(128 - ZC * rem, 128), 1)
        keep = lane1 < 128 - ZC * rem
        tab[g : g + 1, 0:128] = jnp.where(keep, x[0:1], x[1:2])
        tab[g : g + 1, 128:256] = jnp.where(keep, x[1:2], x[2:3])
    table = tab[...]
    for part in range(4):
        lat_rows[TOK * part : TOK * (part + 1), :] = hidden_lanes(table, part)
    lat_rows[4 * TOK : W_ROWS, :] = jnp.zeros((W_ROWS - 4 * TOK, 256), F32)
    low, high = pltpu.roll(table, 256 - 4 * SPARE, 1)[:8], pltpu.roll(table, 512 - 8 * SPARE, 1)[8:]
    lat_rows[W_ROWS:, :] = jnp.where(iota((8, 256), 1) < 256 - 4 * SPARE, low, high)
    for a in range(3):
        copies[3 + a].wait()
        wf[9 * a : 9 * a + 9, :, :C2] = w_ref[9 * a : 9 * a + 9].astype(F32)
    lane = iota((IN_SH, 128), 1)

    def choose(core):
        for line in range(LINE):
            start = (2 * line + core) * OUT_BLK
            tile, into = start // 128, start % 128
            for b in range(3):
                acc = [jnp.zeros((IN_SH, 128), F32)] * 2
                for j in range(9):
                    tap = 9 * (j // 3) + 3 * b + j % 3
                    x = wf[tap, :, 128 * tile : 128 * tile + 128]
                    if into + OUT_BLK > 128:
                        x = jnp.where(lane >= into, x, wf[tap, :, 128 : 256])
                    at, to = OUT_BLK * j // 128, OUT_BLK * j % 128
                    moved = pltpu.roll(x, (to - into) % 128, 1)
                    acc[at] = jnp.where((lane >= to) & (lane < to + OUT_BLK), moved, acc[at])
                    if to + OUT_BLK > 128:
                        acc[at + 1] = jnp.where(lane < to + OUT_BLK - 128, moved, acc[at + 1])
                for half in range(2):
                    pf[line, IN_SH * b : IN_SH * (b + 1), 128 * half : 128 * half + 128] = acc[half]

    for core in range(2):
        pl.when(c == core)(functools.partial(choose, core))
    for k in range(LINE):
        outs[k][...] = (pf[lax.rem(z + k, LINE)] + lat_rows[...]).astype(BF16)
    copies[6].wait()
    copies[7].wait()
    for i in range(LINE):
        fill = frames[assign[lax.rem(z + i, LINE) * PLANE + q]] * (TOK // FMAX)
        fills[i : i + 1, :] = jnp.full((1, 128), fill, jnp.int32).astype(F32)


def pack(offsets, assign, w_mid, latents, w_in, frames):
    piece = jax.ShapeDtypeStruct((PIECE_ROWS, 256), BF16)
    return pl.pallas_call(
        pack_kernel,
        out_shape=[piece] * LINE + [jax.ShapeDtypeStruct((512, C1), BF16), jax.ShapeDtypeStruct((LINE, 128), F32)],
        in_specs=[HBM()] * 6,
        out_specs=[VMEM()] * (LINE + 2),
        scratch_shapes=[
            pltpu.SMEM(frames.shape, jnp.int32),
            pltpu.VMEM((27, IN_SH, 256), F32),
            pltpu.VMEM((40, 128), F32),
            pltpu.VMEM((LINE, PIECE_ROWS, 256), F32),
            pltpu.VMEM((TOK, 256), F32),
            pltpu.VMEM((PIECE_ROWS, 256), F32),
            pltpu.VMEM((27, IN_SH, C2), BF16),
            pltpu.VMEM(latents.shape, BF16),
            pltpu.SMEM(offsets.shape, jnp.int32),
            pltpu.SMEM(assign.shape, jnp.int32),
            pltpu.SemaphoreType.DMA((8,)),
        ],
        cost_estimate=cost(2),
        compiler_params=pltpu.CompilerParams(vmem_limit_bytes=32 << 20),
        name="pack",
    )(*in_hbm(offsets, assign, w_mid, latents, w_in, frames))


def join_kernel(*refs):
    pieces, outs, (pf, bf, tab) = refs[:LINE], refs[LINE : LINE + PLANE], refs[LINE + PLANE :]
    _, q, _ = place()
    lane = iota((8, 256), 1)
    for k in range(LINE):
        whole = pieces[k][...].astype(F32)
        bf[W_ROWS * k : W_ROWS * (k + 1), :] = whole[:W_ROWS]
        table, rest = found_lanes(whole, 4), whole[W_ROWS:]
        low, high = pltpu.roll(rest, 4 * SPARE, 1), pltpu.roll(rest, 8 * SPARE - 256, 1)
        pf[TOK * k : TOK * k + 8, :] = jnp.where(lane >= 4 * SPARE, low, table[:8])
        pf[TOK * k + 8 : TOK * (k + 1), :] = jnp.where(lane >= 4 * SPARE, high, table[8:])
    for d in range(PLANE):
        for k in range(LINE):
            for line in range(LINE):
                at = LINE * k + line
                tab[at : at + 1, :] = pf[pl.ds(TOK * k + PLANE * line + (q ^ d), 1), :]
        table = tab[...]
        keep = iota((TOK, 256), 1) < USED
        for part in range(7):
            rows = slice(TOK * part, TOK * (part + 1))
            bf[rows, :] = jnp.where(keep, bf[rows, :], hidden_lanes(table, part))
        outs[d][...] = bf[...].astype(BF16)


def join(pieces):
    out = jax.ShapeDtypeStruct((B_ROWS, 256), BF16)
    return pl.pallas_call(
        join_kernel,
        out_shape=[out] * PLANE,
        in_specs=[VMEM()] * LINE,
        out_specs=[VMEM()] * PLANE,
        scratch_shapes=[
            pltpu.VMEM((LINE * TOK, 256), F32),
            pltpu.VMEM((B_ROWS, 256), F32),
            pltpu.VMEM((TOK, 256), F32),
        ],
        compiler_params=pltpu.CompilerParams(vmem_limit_bytes=32 << 20),
        cost_estimate=cost(5),
        name="join",
    )(*pieces)


def mid_kernel(fills, w1, gain_ref, *refs):
    parts, outs = refs[:PLANE], refs[PLANE : PLANE + LINE]
    lt, xs, tokens, shifted, act, wf = refs[PLANE + LINE :]
    z, q, _ = place()
    for d in range(PLANE):
        part = parts[d][...].astype(F32)
        lt[...] = found_lanes(part, 7)
        for k in range(LINE):
            shard = lax.rem(z - k + LINE, LINE) * PLANE + (q ^ d)
            for b in range(3):
                at = W_ROWS * k + IN_SH * b
                wf[b, pl.ds(pl.multiple_of(shard * IN_SH, 8), IN_SH), :] = part[at : at + IN_SH]
            for i in range(LINE):
                xs[i, pl.ds(shard, 1), :] = lt[pl.ds(LINE * k + lax.rem(z + i, LINE), 1), :]
    repeat = (iota((256, 128), 0) % ZC == iota((256, 128), 1) % ZC).astype(F32).astype(BF16)
    pos16, shard16 = iota((256, 16), 0).astype(F32), iota((256, 16), 1).astype(F32)
    pos, token = iota((256, 256), 0).astype(F32), (iota((256, 256), 1) // ZC).astype(F32)
    lane, col = iota((256, 128), 1), iota((256, 128), 0) % WL
    inner_l, inner_r = col > 0, col < WL - 1
    block = lane // ZC
    tap_col = [(block + r) % 3 for r in range(3)]
    lane1 = iota((1, 128), 1)
    zero_rows = jnp.zeros((2, 6, WL, 128), BF16)
    zero_cols = jnp.zeros((4, 1, WL, 128), BF16)
    for i in range(LINE):
        fill = fills[i : i + 1, 0:16]
        start = fill * shard16
        hit = (pos16 >= start) & (pos16 < start + fill)
        first = jnp.sum(jnp.where(hit, start, 0.0), axis=1, keepdims=True)
        rows = jnp.dot(hit.astype(F32).astype(BF16), xs[i].astype(BF16), preferred_element_type=F32)
        own = jnp.where(pos - first == token, rows, 0.0).astype(BF16)
        tokens[i, 8:264, :] = jnp.dot(own, repeat, preferred_element_type=F32)
        here = tokens[i, 8:264, :]
        left = jnp.where(inner_l, tokens[i, 7:263, :], 0.0)
        right = jnp.where(inner_r, tokens[i, 9:265, :], 0.0)
        for r in range(3):
            v = jnp.where(tap_col[r] == 0, left, jnp.where(tap_col[r] == 1, here, right)).astype(BF16)
            shifted[i, r, 0:2] = zero_rows
            shifted[i, r, 2:6, 0:1] = zero_cols
            shifted[i, r, 2:6, 5:6] = zero_cols
            shifted[i, r, 2:6, 1:5] = v.reshape(4, 4, WL, 128)
    for i in range(LINE):
        tiles = []
        for j in range(4):
            tile = None
            for tap in range(8 * j // 3, min(8 * j + 7, 26) // 3 + 1):
                a, b = divmod(tap, 3)
                lo, hi = max(3 * tap - 8 * j, 0) * ZC, min(3 * tap + 3 - 8 * j, 8) * ZC
                keep = ((lane1 >= lo) & (lane1 < hi)).astype(F32).astype(BF16)
                term = shifted[i, 8 * j % 3, a : a + 4, b : b + 4].reshape(256, 128) * keep
                tile = term if tile is None else tile + term
            tiles.append(tile)
        h = jnp.dot(jnp.concatenate(tiles, axis=1), w1[...], preferred_element_type=F32)
        scale = lax.rsqrt(jnp.mean(h * h, axis=1, keepdims=True) + 1e-6)
        out = silu(h * scale * gain_ref[...]).astype(BF16)
        for tp in range(2):
            act[512 * tp + 128 * i : 512 * tp + 128 * i + 128, :] = out[128 * tp : 128 * tp + 128]
    lane = iota((OUT_BLK, 128), 1)
    second, row, column = lane >= 64, lane // WL % 4, lane % WL
    sums = [[[] for _ in range(2)] for _ in range(LINE)]
    for b in range(3):
        turned = wf[b].T.astype(BF16)
        prods = [dot_nt(turned[0:224], act[0:512, :]), dot_nt(turned[64:224], act[512:1024, :])]

        def tile(i, tp, a, e):
            at = OUT_BLK * (3 * a + e) - 64 * tp
            return prods[tp][at : at + OUT_BLK, 128 * i : 128 * i + 128]

        for i in range(LINE):
            for e in range(3):
                early, late = (pltpu.roll(tile(i, tp, 1, e), 64, 1) for tp in range(2))
                sums[i][0].append(tile(i, 0, 2, e) + jnp.where(second, early, 0.0))
                sums[i][1].append(tile(i, 1, 2, e) + jnp.where(second, late, early) + tile(i, 0, 0, e))
    for i in range(LINE):
        for tp in range(2):
            halves = [[], []]
            for b in range(3):
                e0, e1, e2 = sums[i][tp][3 * b : 3 * b + 3]
                halves[0].append(jnp.where(column > 0, pltpu.roll(e0, 1, 1), 0.0) + e1 + e2)
                halves[1].append(e0 + e1 + jnp.where(column < WL - 1, pltpu.roll(e2, 127, 1), 0.0))
            phases = [None] * 4
            for px in range(2):
                b0, b1, b2 = halves[px]
                phases[px] = jnp.where(row > 0, pltpu.roll(b0, WL, 1), 0.0) + b1 + b2
                phases[2 + px] = b0 + b1 + jnp.where(row < 3, pltpu.roll(b2, 128 - WL, 1), 0.0)
            outs[i][:, 128 * tp : 128 * tp + 128] = jnp.concatenate(phases, axis=0).astype(BF16)


def mid(fills, parts, w_in, gain_in):
    out = jax.ShapeDtypeStruct((4 * OUT_BLK, 256), BF16)
    return pl.pallas_call(
        mid_kernel,
        out_shape=[out] * LINE,
        in_specs=[VMEM()] * (PLANE + 3),
        out_specs=[VMEM()] * LINE,
        scratch_shapes=[
            pltpu.VMEM((LINE * LINE, 256), F32),
            pltpu.VMEM((LINE, 16, 256), F32),
            pltpu.VMEM((LINE, 288, 128), F32),
            pltpu.VMEM((LINE, 3, 6, 6, WL, 128), BF16),
            pltpu.VMEM((LINE * 256, C1), BF16),
            pltpu.VMEM((3, C1, 256), F32),
        ],
        compiler_params=pltpu.CompilerParams(vmem_limit_bytes=48 << 20),
        cost_estimate=cost(5),
        name="mid",
    )(fills, w_in, gain_in, *parts)


def regroup_kernel(half, near, far, out, rows):
    for b in range(3):
        at = OUT_BLK * b
        rows[at : at + 6, :] = half[8 * b : 8 * b + 6, :].astype(F32)
        rows[at + 6 : at + 18, :] = near[16 * b : 16 * b + 16, :].astype(F32)[:MID_SH]
        rows[at + 18 : at + 24, :] = far[8 * b : 8 * b + 6, :].astype(F32)
    out[...] = rows[...].astype(BF16)


def regroup(half, near, far):
    return pl.pallas_call(
        regroup_kernel,
        out_shape=jax.ShapeDtypeStruct((3 * OUT_BLK, WOUT_LANES), BF16),
        in_specs=[VMEM()] * 3,
        out_specs=VMEM(),
        scratch_shapes=[pltpu.VMEM((3 * OUT_BLK, WOUT_LANES), F32)],
        cost_estimate=cost(5),
        compiler_params=pltpu.CompilerParams(vmem_limit_bytes=32 << 20),
        name="regroup",
    )(half, near, far)


def prep_kernel(frames_hbm, assign_hbm, gmid_hbm, gout_hbm, *refs):
    parts, (raw, order_out, pick_out, gmid_out, gout_out, limit_out) = refs[:LINE], refs[LINE : LINE + 6]
    gmid_ref, gout_ref, frames, assign, sems = refs[LINE + 6 :]
    moves = [(gmid_hbm, gmid_ref), (gout_hbm, gout_ref), (frames_hbm, frames), (assign_hbm, assign)]
    loads = [pltpu.make_async_copy(src, dst, sems.at[i]) for i, (src, dst) in enumerate(moves)]
    for load in loads:
        load.start()
    z, q, c = place()
    for k in range(LINE):
        raw[3 * OUT_BLK * k : 3 * OUT_BLK * (k + 1), :] = parts[k][...]
    row, channel = iota((C2, C2), 0), iota((C2, C2), 1)
    side, step, in_shard = row // HALF_CH, row % HALF_CH // OUT_BLK, row % MID_SH
    flip = q ^ (2 * (c ^ side) + row % OUT_BLK // MID_SH)
    near = (flip == 1) | (flip == 2)
    holder = jnp.where(near, flip - 1, in_shard // 6)
    slot = jnp.where(near, 6 + in_shard, 6 * flip + in_shard % 6)
    held = (c ^ holder) * HALF_CH + step * OUT_BLK + slot
    order_out[...] = (channel == held).astype(F32).astype(BF16)
    r, l = iota((256, 256), 0), iota((256, 256), 1)
    same = (r // 8) == ((l // 64) % 2) * WL + l % WL
    mid_row = 2 * ((l // WL) % 4) + l // 128
    for b in range(3):
        pick_out[b] = (same & (mid_row == (c * 8 + r % 8 + b - 1) >> 1)).astype(F32).astype(BF16)
    for load in loads:
        load.wait()
    wanted = (2 * ((z - step) & (LINE - 1)) + (c ^ side)) * OUT_BLK + row % OUT_BLK
    column = jnp.sum(jnp.where(channel == wanted, gmid_ref[...], 0.0), axis=1, keepdims=True)
    gmid_out[...] = jnp.broadcast_to(column, (C2, 128))
    gout_out[...] = jnp.zeros((1, 128), F32)
    gout_out[:, :C3] = gout_ref[...]
    limit_out[...] = jnp.full((1, 128), frames[assign[z * PLANE + q]], jnp.int32).astype(F32)


def prep(frames, assign, gain_mid, gain_out, parts):
    return pl.pallas_call(
        prep_kernel,
        out_shape=[
            jax.ShapeDtypeStruct((LINE * 3 * OUT_BLK, WOUT_LANES), BF16),
            jax.ShapeDtypeStruct((C2, C2), BF16),
            jax.ShapeDtypeStruct((3, 256, 256), BF16),
            jax.ShapeDtypeStruct((C2, 128), F32),
            jax.ShapeDtypeStruct((1, 128), F32),
            jax.ShapeDtypeStruct((1, 128), F32),
        ],
        in_specs=[HBM()] * 4 + [VMEM()] * LINE,
        out_specs=[VMEM()] * 6,
        scratch_shapes=[
            pltpu.VMEM(gain_mid.shape, F32),
            pltpu.VMEM(gain_out.shape, F32),
            pltpu.SMEM(frames.shape, jnp.int32),
            pltpu.SMEM(assign.shape, jnp.int32),
            pltpu.SemaphoreType.DMA((4,)),
        ],
        cost_estimate=cost(0.01),
        compiler_params=pltpu.CompilerParams(vmem_limit_bytes=32 << 20),
        name="prep",
    )(*in_hbm(frames, assign, gain_mid, gain_out), *parts)


def wide_kernel(own, other, order, out, wf):
    wf[:, :, :, C3:] = jnp.zeros((3, 9, C2, 128 - C3), F32)
    for source, raw in enumerate((own, other)):
        for k in range(LINE):
            part = raw[72 * k : 72 * k + 72, :].astype(F32)
            at = (source * LINE + k) * OUT_BLK
            for j in range(9):
                tap = part[:, C3 * j : C3 * (j + 1)]
                for b in range(3):
                    wf[b, j, at : at + OUT_BLK, :C3] = tap[OUT_BLK * b : OUT_BLK * (b + 1)]
    for b in range(3):
        for j in range(9):
            moved = jnp.dot(order[...], wf[b, j].astype(BF16), preferred_element_type=F32)
            out[C2 * b : C2 * (b + 1), 128 * j : 128 * (j + 1)] = moved.astype(BF16)


def wide(own, other, order):
    return pl.pallas_call(
        wide_kernel,
        out_shape=jax.ShapeDtypeStruct((3 * C2, 1152), BF16),
        in_specs=[VMEM()] * 3,
        out_specs=VMEM(),
        scratch_shapes=[pltpu.VMEM((3, 9, C2, 128), F32)],
        cost_estimate=cost(0.01),
        compiler_params=pltpu.CompilerParams(vmem_limit_bytes=48 << 20),
        name="wide",
    )(own, other, order)


def stack_kernel(*refs):
    rows = refs[0].shape[0]
    for i, ref in enumerate(refs[:-1]):
        refs[-1][rows * i : rows * (i + 1), :] = ref[...]


def stack(parts, us=5):
    rows, lanes = parts[0].shape
    return pl.pallas_call(
        stack_kernel,
        out_shape=jax.ShapeDtypeStruct((len(parts) * rows, lanes), BF16),
        in_specs=[VMEM()] * len(parts),
        out_specs=VMEM(),
        cost_estimate=cost(us),
        compiler_params=pltpu.CompilerParams(vmem_limit_bytes=32 << 20),
        name="stack",
    )(*parts)


def out_kernel(own, other, w_all, pick, gmid_ref, gout_ref, limit_ref, out_hbm, hid, lhs, prod, out_ref, sems):
    for side, group in enumerate((own, other)):
        for k in range(LINE):
            part = group[96 * k : 96 * k + 96, :].astype(F32)
            at = (side * LINE + k) * OUT_BLK
            for p in range(4):
                for tp in range(2):
                    hid[p, tp, at : at + OUT_BLK, :] = part[OUT_BLK * p : OUT_BLK * (p + 1), 128 * tp : 128 * tp + 128]
    acts = []
    for p in range(4):
        halves = []
        for tp in range(2):
            h = hid[p, tp]
            scale = lax.rsqrt(jnp.sum(h * h, axis=0, keepdims=True) * (1.0 / C2) + 1e-6)
            halves.append(silu(h * scale * gmid_ref[...]).astype(BF16))
        acts.append(halves)
    for b in range(3):
        for tp in range(2):
            for px in range(2):
                src = jnp.concatenate([acts[2 * py + px][tp] for py in range(2)], axis=1)
                rows = dot_nt(pick[b], src).astype(BF16)
                for half in range(2):
                    lhs[2 * tp + half, px, :, C2 * b : C2 * b + C2] = rows[128 * half : 128 * half + 128]
    lane = iota((1, 8, 128), 2)
    limit = limit_ref[...]
    below = [lane < 128 - 32 * i for i in range(4)]
    def multiply(t):
        if t == 0:
            both = jnp.dot(lhs[0:2].reshape(512, 3 * C2), w_all[...], preferred_element_type=F32)
            prod[0:2] = both.reshape(2, 2, 128, 1152)
        elif t > 1:
            at = 384 * (t - 1)
            prod[t, :, :, at:] = jnp.dot(
                lhs[t].reshape(256, 3 * C2), w_all[:, at:], preferred_element_type=F32
            ).reshape(2, 128, 1152 - at)

    def combine(t):
        sums = []
        for px in range(2):
            row = []
            for e in range(3):
                total = None
                for a in range(3):
                    s = t + a - 2
                    if s < 0:
                        continue
                    at = 128 * (3 * a + e)
                    term = prod[s, px, :, at : at + 128].reshape(WL, 8, 128)
                    total = term if total is None else total + term
                row.append(total)
            sums.append(row)
        zero = jnp.zeros((1, 8, 128), F32)
        after = jnp.concatenate([sums[0][2][1:], zero], axis=0)
        before = jnp.concatenate([zero, sums[1][0][:-1]], axis=0)
        outs = [
            before + sums[0][1] + sums[0][2],
            sums[0][0] + sums[0][1] + sums[1][2],
            sums[0][0] + sums[1][1] + sums[1][2],
            sums[1][0] + sums[1][1] + after,
        ]
        vals = []
        for i, o in enumerate(outs):
            scale = lax.rsqrt(jnp.sum(o * o, axis=2, keepdims=True) * (1.0 / C3) + 1e-6)
            v = jnp.where(t < limit, silu(o * scale * gout_ref[...]), 0.0)
            vals.append(pltpu.roll(v, 128 - 32 * i, 2) if i else v)
        tiles = [
            jnp.where(lane < 96, vals[0], vals[1]),
            jnp.where(lane < 64, vals[1], vals[2]),
            jnp.where(lane < 32, vals[2], vals[3]),
        ]
        for x in range(WL):
            both = jnp.concatenate([tile[x] for tile in tiles], axis=1)
            out_ref[0, t, :, 384 * x : 384 * x + 384] = both.astype(BF16)

    copies = [pltpu.make_async_copy(out_ref.at[:, t], out_hbm.at[:, t], sems.at[t]) for t in range(FMAX)]
    multiply(0)
    multiply(2)
    combine(0)
    copies[0].start()
    multiply(3)
    combine(1)
    copies[1].start()
    combine(2)
    copies[2].start()
    combine(3)
    copies[3].start()
    for copy in copies:
        copy.wait()


def finish(*rest):
    return pl.pallas_call(
        out_kernel,
        out_shape=jax.ShapeDtypeStruct((1, FMAX, 4 * RL, 4 * WL * C3), BF16),
        in_specs=[VMEM()] * len(rest),
        out_specs=HBM(),
        scratch_shapes=[
            pltpu.VMEM((4, 2, C2, 128), F32),
            pltpu.VMEM((4, 2, 128, 3 * C2), BF16),
            pltpu.VMEM((4, 2, 128, 1152), F32),
            pltpu.VMEM((1, FMAX, 4 * RL, 4 * WL * C3), BF16),
            pltpu.SemaphoreType.DMA((FMAX,)),
        ],
        compiler_params=pltpu.CompilerParams(vmem_limit_bytes=48 << 20),
        cost_estimate=cost(4.8),
        name="finish",
    )(*rest)


def along_z(value, step):
    return lax.ppermute(value, "grp", [(g, (g + PLANE * step) % (LINE * PLANE)) for g in range(LINE * PLANE)])


def in_plane(value, flip):
    return lax.ppermute(value, "grp", [(g, g ^ flip) for g in range(LINE * PLANE)])


def near_chip(value):
    pairs = [(2 * g + c, 2 * (g ^ (1 + c)) + c) for g in range(LINE * PLANE) for c in range(2)]
    return lax.ppermute(value, ("grp", "row"), pairs)


def other_core(value):
    return lax.ppermute(value, "row", [(0, 1), (1, 0)])


def per_device_fast(latents, frames, offsets, assign, w_in, w_mid, w_out, gain_in, gain_mid, gain_out):
    core = lax.axis_index("row")
    w_in = w_in.transpose(1, 0, 2).reshape(27 * ZC, C1)
    *pieces, w_in, fills = pack(offsets, assign, jnp.transpose(w_mid, (1, 0, 2)), latents, w_in, frames)
    pieces = [pieces[0]] + [along_z(pieces[k], k) for k in range(1, LINE)]
    parts = join(pieces)
    parts = [parts[0]] + [in_plane(parts[d], d) for d in range(1, PLANE)]
    full = w_out.reshape(MID_SH, 3, 3, 3, C3).transpose(2, 0, 1, 3, 4).reshape(3, MID_SH, 9 * C3)
    half = lax.dynamic_slice_in_dim(full, core * 6, 6, axis=1)
    full = jnp.pad(full, ((0, 0), (0, 16 - MID_SH), (0, WOUT_LANES - 9 * C3))).reshape(48, WOUT_LANES)
    half = jnp.pad(half, ((0, 0), (0, 2), (0, WOUT_LANES - 9 * C3))).reshape(24, WOUT_LANES)
    plane = regroup(half, near_chip(full), in_plane(half, 3))
    own = [plane] + [along_z(plane, k) for k in range(1, LINE)]
    hidden = mid(fills, parts, w_in, gain_in[None, :])
    own, _ = lax.optimization_barrier((own, hidden[0]))
    raw, order, pick, gmid, gout, limit = prep(frames, assign, gain_mid[None, :], gain_out[None, :], own)
    w_last = wide(raw, other_core(raw), order)
    hidden = stack([hidden[0]] + [along_z(hidden[k], k) for k in range(1, LINE)], 30)
    return finish(hidden, other_core(hidden), w_last, pick, gmid, gout, limit)


def solution(mesh):
    fast = mesh.shape["grp"] == LINE * PLANE and mesh.shape["row"] == 2
    placed = (
        P("grp", None),
        P(),
        P(),
        P(),
        P(),
        P("grp", None, None),
        P("grp", None, None),
        P(),
        P(),
        P(),
    )
    return jax.shard_map(
        per_device_fast if fast else per_device_general,
        mesh=mesh,
        in_specs=placed,
        out_specs=P("grp", None, "row", None),
        check_vma=False,
    )
```

```python
import functools

import jax
import jax.numpy as jnp
from jax import lax
from jax.experimental import pallas as pl
from jax.experimental.pallas import tpu as pltpu
from jax.sharding import PartitionSpec as P

RL = 2
WL = 16
FMAX = 4


def extended_2(cells, sides, width):
    for axis, dim in sides:
        count = lax.axis_size(axis)
        ends = count - 1
        head = lax.slice_in_dim(cells, 0, width, axis=dim)
        tail = lax.slice_in_dim(cells, cells.shape[dim] - width, cells.shape[dim], axis=dim)
        cells = jnp.concatenate(
            [
                lax.ppermute(tail, axis, [(i, (i + 1) % count) for i in range(ends)]),
                cells,
                lax.ppermute(head, axis, [((i + 1) % count, i) for i in range(ends)]),
            ],
            axis=dim,
        )
    return cells


def rms_silu(hidden, gain):
    mean_sq = jnp.mean(hidden * hidden, axis=-1, keepdims=True)
    scaled = hidden * lax.rsqrt(mean_sq + 1e-06) * gain
    return jax.nn.silu(scaled)


def causal_conv(extended, weight):
    count_t = extended.shape[0]
    count_r = extended.shape[1] - 2
    count_c = extended.shape[2]
    width_in = extended.shape[3]
    width_out = weight.shape[2]
    padded = jnp.pad(extended, ((2, 0), (0, 0), (1, 1), (0, 0)))
    total = jnp.zeros((count_t * count_r * count_c, width_out), jnp.float32)
    for time_tap in range(3):
        for row_tap in range(3):
            for col_tap in range(3):
                window = padded[
                    time_tap : time_tap + count_t,
                    row_tap : row_tap + count_r,
                    col_tap : col_tap + count_c,
                ]
                window = window.reshape(count_t * count_r * count_c, width_in)
                tap_index = 9 * time_tap + 3 * row_tap + col_tap
                total = total + jnp.dot(
                    window, weight[:, tap_index, :], preferred_element_type=jnp.float32
                )
    return total.reshape(count_t, count_r, count_c, width_out)


def upsample(values):
    return jnp.repeat(jnp.repeat(values, 2, axis=1), 2, axis=2)


def per_device_general(latents, frames, offsets, assign, w_in, w_mid, w_out, gain_in, gain_mid, gain_out):
    groups = lax.axis_size("grp")
    row_count = lax.axis_size("row")
    row_index = lax.axis_index("row")
    group_index = lax.axis_index("grp")
    channels = w_in.shape[0]
    cap_vals = latents.shape[1] // groups
    cap_tokens = cap_vals // channels
    span_len = cap_tokens // FMAX
    flat = latents[0]
    slot_ids = jnp.arange(cap_vals, dtype=jnp.int32)

    def select_span(request):
        start = offsets[request] * channels
        block = lax.dynamic_slice_in_dim(flat, start, cap_vals)
        keep = slot_ids < frames[request] * span_len * channels
        return jnp.where(keep, block, jnp.zeros((), block.dtype))

    outgoing = jax.vmap(select_span)(assign)
    incoming = lax.all_to_all(outgoing, "grp", split_axis=0, concat_axis=0, tiled=True)
    table = incoming.reshape(groups * cap_tokens, channels)
    request = assign[group_index]
    count = frames[request]
    fill_len = count * span_len
    image_rows = RL * row_count
    frame_ids = jnp.arange(FMAX, dtype=jnp.int32)[:, None, None]
    row_ids = row_index * RL + jnp.arange(RL, dtype=jnp.int32)[None, :, None]
    col_ids = jnp.arange(WL, dtype=jnp.int32)[None, None, :]
    position = (frame_ids * image_rows + row_ids) * WL + col_ids
    shard = jnp.minimum(position // fill_len, groups - 1)
    within = position % fill_len
    tokens = table[shard * cap_tokens + within]
    valid = (frame_ids < count)[..., None]
    latent_in = jnp.where(valid, tokens, jnp.zeros((), tokens.dtype))
    full_mid, full_out = (
        lax.all_gather(w_mid, "grp", axis=0, tiled=True),
        lax.all_gather(w_out, "grp", axis=0, tiled=True),
    )
    latent_ext = extended_2(latent_in, (("row", 1),), 1)
    act_in = rms_silu(causal_conv(latent_ext, w_in), gain_in).astype(jnp.bfloat16)
    mid_ext = extended_2(upsample(act_in), (("row", 1),), 1)
    act_mid = rms_silu(causal_conv(mid_ext, full_mid), gain_mid).astype(jnp.bfloat16)
    out_ext = extended_2(upsample(act_mid), (("row", 1),), 1)
    final = rms_silu(causal_conv(out_ext, full_out), gain_out)
    final = jnp.where(valid, final, jnp.zeros((), jnp.float32)).astype(jnp.bfloat16)
    return final.reshape(1, FMAX, 4 * RL, 4 * WL * final.shape[3])


LINE = 4
PLANE = 4
ZC, C1, C2, C3 = 16, 384, 192, 96
TOK = 16
IN_SH = C1 // 16
MID_SH = C2 // 16
OUT_BLK = C2 // (2 * LINE)
PIECE_ROWS = 80
USED = 9 * (C2 // (2 * LINE))
SPARE = 256 - USED
W_ROWS = 3 * IN_SH
B_ROWS = LINE * W_ROWS
WOUT_LANES = 896
HALF_CH = C2 // 2
F32, BF16 = jnp.float32, jnp.bfloat16
VMEM = functools.partial(pl.BlockSpec, memory_space=pltpu.VMEM)
SMEM = functools.partial(pl.BlockSpec, memory_space=pltpu.SMEM)
HBM = functools.partial(pl.BlockSpec, memory_space=pltpu.HBM)


def in_hbm(*values):
    return [pltpu.with_memory_space_constraint(v, pltpu.HBM) for v in values]


def cost(us):
    return pl.CostEstimate(flops=int(us * 1.15e9), bytes_accessed=0, transcendentals=0)


def iota(shape, dim):
    return lax.broadcasted_iota(jnp.int32, shape, dim)


def place():
    group = lax.axis_index("grp")
    return lax.div(group, PLANE), lax.rem(group, PLANE), lax.axis_index("row")


def silu(v):
    return v / (1.0 + jnp.exp(-v))


def dot_nt(lhs, rhs):
    return lax.dot_general(lhs, rhs, (((1,), (1,)), ((), ())), preferred_element_type=F32)


def hidden_lanes(table, part):
    moved = pltpu.roll(table, (USED - SPARE * part) % 256, 1)
    return jnp.where(iota(table.shape, 1) >= USED, moved, 0.0)


def found_lanes(rows, parts):
    table = jnp.zeros((TOK, 256), F32)
    for part in range(parts):
        moved = pltpu.roll(rows[TOK * part : TOK * (part + 1)], (SPARE * part - USED) % 256, 1)
        lane = iota((TOK, 256), 1)
        table = jnp.where((lane >= SPARE * part) & (lane < SPARE * (part + 1)), moved, table)
    return table


def pack_kernel(offsets_hbm, assign_hbm, w_hbm, lat_hbm, win_hbm, frames_hbm, *refs):
    outs, w1, fills, (frames, wf, lf, pf, tab, lat_rows, w_ref, lat_ref, offsets, assign, sems) = refs[:LINE], refs[LINE], refs[LINE + 1], refs[LINE + 2 :]
    parts = [pl.ds(9 * a, 9) for a in range(3)]
    moves = [(w_hbm.at[p], w_ref.at[p]) for p in parts]
    moves = [(offsets_hbm, offsets), (assign_hbm, assign), (lat_hbm, lat_ref)] + moves
    moves += [(win_hbm, w1.at[0 : 27 * ZC]), (frames_hbm, frames)]
    copies = [pltpu.make_async_copy(src, dst, sems.at[i]) for i, (src, dst) in enumerate(moves)]
    for copy in copies:
        copy.start()
    z, q, c = place()
    lf[32:40, :] = jnp.zeros((8, 128), F32)
    w1[27 * ZC :, :] = jnp.zeros((512 - 27 * ZC, C1), BF16)
    for k in range(LINE):
        pf[k, W_ROWS:, :] = jnp.zeros((PIECE_ROWS - W_ROWS, 256), F32)
    lane1 = iota((1, 128), 1)
    for copy in copies[:3]:
        copy.wait()
    lat = lat_ref[...].astype(F32)
    for j in range(32):
        lf[j : j + 1, :] = lat[:, 128 * j : 128 * j + 128]
    for g in range(16):
        off = offsets[assign[g]]
        row, rem = lax.div(off, 8), lax.rem(off, 8)
        x = pltpu.roll(lf[pl.ds(row, 8), :], lax.rem(128 - ZC * rem, 128), 1)
        keep = lane1 < 128 - ZC * rem
        tab[g : g + 1, 0:128] = jnp.where(keep, x[0:1], x[1:2])
        tab[g : g + 1, 128:256] = jnp.where(keep, x[1:2], x[2:3])
    table = tab[...]
    for part in range(4):
        lat_rows[TOK * part : TOK * (part + 1), :] = hidden_lanes(table, part)
    lat_rows[4 * TOK : W_ROWS, :] = jnp.zeros((W_ROWS - 4 * TOK, 256), F32)
    low, high = pltpu.roll(table, 256 - 4 * SPARE, 1)[:8], pltpu.roll(table, 512 - 8 * SPARE, 1)[8:]
    lat_rows[W_ROWS:, :] = jnp.where(iota((8, 256), 1) < 256 - 4 * SPARE, low, high)
    for a in range(3):
        copies[3 + a].wait()
        wf[9 * a : 9 * a + 9, :, :C2] = w_ref[9 * a : 9 * a + 9].astype(F32)
    lane = iota((IN_SH, 128), 1)

    def choose(core):
        for line in range(LINE):
            start = (2 * line + core) * OUT_BLK
            tile, into = start // 128, start % 128
            for b in range(3):
                acc = [jnp.zeros((IN_SH, 128), F32)] * 2
                for j in range(9):
                    tap = 9 * (j // 3) + 3 * b + j % 3
                    x = wf[tap, :, 128 * tile : 128 * tile + 128]
                    if into + OUT_BLK > 128:
                        x = jnp.where(lane >= into, x, wf[tap, :, 128 : 256])
                    at, to = OUT_BLK * j // 128, OUT_BLK * j % 128
                    moved = pltpu.roll(x, (to - into) % 128, 1)
                    acc[at] = jnp.where((lane >= to) & (lane < to + OUT_BLK), moved, acc[at])
                    if to + OUT_BLK > 128:
                        acc[at + 1] = jnp.where(lane < to + OUT_BLK - 128, moved, acc[at + 1])
                for half in range(2):
                    pf[line, IN_SH * b : IN_SH * (b + 1), 128 * half : 128 * half + 128] = acc[half]

    for core in range(2):
        pl.when(c == core)(functools.partial(choose, core))
    for k in range(LINE):
        outs[k][...] = (pf[lax.rem(z + k, LINE)] + lat_rows[...]).astype(BF16)
    copies[6].wait()
    copies[7].wait()
    for i in range(LINE):
        fill = frames[assign[lax.rem(z + i, LINE) * PLANE + q]] * (TOK // FMAX)
        fills[i : i + 1, :] = jnp.full((1, 128), fill, jnp.int32).astype(F32)


def pack(offsets, assign, w_mid, latents, w_in, frames):
    piece = jax.ShapeDtypeStruct((PIECE_ROWS, 256), BF16)
    return pl.pallas_call(
        pack_kernel,
        out_shape=[piece] * LINE + [jax.ShapeDtypeStruct((512, C1), BF16), jax.ShapeDtypeStruct((LINE, 128), F32)],
        in_specs=[HBM()] * 6,
        out_specs=[VMEM()] * (LINE + 2),
        scratch_shapes=[
            pltpu.SMEM(frames.shape, jnp.int32),
            pltpu.VMEM((27, IN_SH, 256), F32),
            pltpu.VMEM((40, 128), F32),
            pltpu.VMEM((LINE, PIECE_ROWS, 256), F32),
            pltpu.VMEM((TOK, 256), F32),
            pltpu.VMEM((PIECE_ROWS, 256), F32),
            pltpu.VMEM((27, IN_SH, C2), BF16),
            pltpu.VMEM(latents.shape, BF16),
            pltpu.SMEM(offsets.shape, jnp.int32),
            pltpu.SMEM(assign.shape, jnp.int32),
            pltpu.SemaphoreType.DMA((8,)),
        ],
        cost_estimate=cost(2),
        compiler_params=pltpu.CompilerParams(vmem_limit_bytes=32 << 20),
        name="pack",
    )(*in_hbm(offsets, assign, w_mid, latents, w_in, frames))


def join_kernel(*refs):
    pieces, outs, (pf, bf, tab) = dict(zip((0, 1, 3, 2), refs[:LINE])), refs[LINE : LINE + PLANE], refs[LINE + PLANE :]
    _, q, _ = place()
    lane = iota((8, 256), 1)
    for k in range(LINE):
        whole = pieces[k][...].astype(F32)
        bf[W_ROWS * k : W_ROWS * (k + 1), :] = whole[:W_ROWS]
        table, rest = found_lanes(whole, 4), whole[W_ROWS:]
        low, high = pltpu.roll(rest, 4 * SPARE, 1), pltpu.roll(rest, 8 * SPARE - 256, 1)
        pf[TOK * k : TOK * k + 8, :] = jnp.where(lane >= 4 * SPARE, low, table[:8])
        pf[TOK * k + 8 : TOK * (k + 1), :] = jnp.where(lane >= 4 * SPARE, high, table[8:])
    for d in range(PLANE):
        for k in range(LINE):
            for line in range(LINE):
                at = LINE * k + line
                tab[at : at + 1, :] = pf[pl.ds(TOK * k + PLANE * line + (q ^ d), 1), :]
        table = tab[...]
        keep = iota((TOK, 256), 1) < USED
        for part in range(7):
            rows = slice(TOK * part, TOK * (part + 1))
            bf[rows, :] = jnp.where(keep, bf[rows, :], hidden_lanes(table, part))
        outs[d][...] = bf[...].astype(BF16)


def join(pieces):
    out = jax.ShapeDtypeStruct((B_ROWS, 256), BF16)
    return pl.pallas_call(
        join_kernel,
        out_shape=[out] * PLANE,
        in_specs=[VMEM()] * LINE,
        out_specs=[VMEM()] * PLANE,
        scratch_shapes=[
            pltpu.VMEM((LINE * TOK, 256), F32),
            pltpu.VMEM((B_ROWS, 256), F32),
            pltpu.VMEM((TOK, 256), F32),
        ],
        compiler_params=pltpu.CompilerParams(vmem_limit_bytes=32 << 20),
        cost_estimate=cost(5),
        name="join",
    )(*(pieces[k] for k in (0, 1, 3, 2)))


def mid_kernel(fills, w1, gain_ref, *refs):
    parts, outs = refs[:PLANE], refs[PLANE : PLANE + LINE]
    lt, xs, tokens, shifted, act, wf = refs[PLANE + LINE :]
    z, q, _ = place()
    for d in range(PLANE):
        part = parts[d][...].astype(F32)
        lt[...] = found_lanes(part, 7)
        for k in range(LINE):
            shard = lax.rem(z - k + LINE, LINE) * PLANE + (q ^ d)
            for b in range(3):
                at = W_ROWS * k + IN_SH * b
                wf[b, pl.ds(pl.multiple_of(shard * IN_SH, 8), IN_SH), :] = part[at : at + IN_SH]
            for i in range(LINE):
                xs[i, pl.ds(shard, 1), :] = lt[pl.ds(LINE * k + lax.rem(z + i, LINE), 1), :]
    repeat = (iota((256, 128), 0) % ZC == iota((256, 128), 1) % ZC).astype(F32).astype(BF16)
    pos16, shard16 = iota((256, 16), 0).astype(F32), iota((256, 16), 1).astype(F32)
    pos, token = iota((256, 256), 0).astype(F32), (iota((256, 256), 1) // ZC).astype(F32)
    lane, col = iota((256, 128), 1), iota((256, 128), 0) % WL
    inner_l, inner_r = col > 0, col < WL - 1
    block = lane // ZC
    tap_col = [(block + r) % 3 for r in range(3)]
    lane1 = iota((1, 128), 1)
    zero_rows = jnp.zeros((2, 6, WL, 128), BF16)
    zero_cols = jnp.zeros((4, 1, WL, 128), BF16)
    for i in range(LINE):
        fill = fills[i : i + 1, 0:16]
        start = fill * shard16
        hit = (pos16 >= start) & (pos16 < start + fill)
        first = jnp.sum(jnp.where(hit, start, 0.0), axis=1, keepdims=True)
        rows = jnp.dot(hit.astype(F32).astype(BF16), xs[i].astype(BF16), preferred_element_type=F32)
        own = jnp.where(pos - first == token, rows, 0.0).astype(BF16)
        tokens[i, 8:264, :] = jnp.dot(own, repeat, preferred_element_type=F32)
        here = tokens[i, 8:264, :]
        left = jnp.where(inner_l, tokens[i, 7:263, :], 0.0)
        right = jnp.where(inner_r, tokens[i, 9:265, :], 0.0)
        for r in range(3):
            v = jnp.where(tap_col[r] == 0, left, jnp.where(tap_col[r] == 1, here, right)).astype(BF16)
            shifted[i, r, 0:2] = zero_rows
            shifted[i, r, 2:6, 0:1] = zero_cols
            shifted[i, r, 2:6, 5:6] = zero_cols
            shifted[i, r, 2:6, 1:5] = v.reshape(4, 4, WL, 128)
    for i in range(LINE):
        tiles = []
        for j in range(4):
            tile = None
            for tap in range(8 * j // 3, min(8 * j + 7, 26) // 3 + 1):
                a, b = divmod(tap, 3)
                lo, hi = max(3 * tap - 8 * j, 0) * ZC, min(3 * tap + 3 - 8 * j, 8) * ZC
                keep = ((lane1 >= lo) & (lane1 < hi)).astype(F32).astype(BF16)
                term = shifted[i, 8 * j % 3, a : a + 4, b : b + 4].reshape(256, 128) * keep
                tile = term if tile is None else tile + term
            tiles.append(tile)
        h = jnp.dot(jnp.concatenate(tiles, axis=1), w1[...], preferred_element_type=F32)
        scale = lax.rsqrt(jnp.mean(h * h, axis=1, keepdims=True) + 1e-6)
        out = silu(h * scale * gain_ref[...]).astype(BF16)
        for tp in range(2):
            act[512 * tp + 128 * i : 512 * tp + 128 * i + 128, :] = out[128 * tp : 128 * tp + 128]
    lane = iota((OUT_BLK, 128), 1)
    second, row, column = lane >= 64, lane // WL % 4, lane % WL
    sums = [[[] for _ in range(2)] for _ in range(LINE)]
    for b in range(3):
        turned = wf[b].T.astype(BF16)
        prods = [dot_nt(turned[0:224], act[0:512, :]), dot_nt(turned[64:224], act[512:1024, :])]

        def tile(i, tp, a, e):
            at = OUT_BLK * (3 * a + e) - 64 * tp
            return prods[tp][at : at + OUT_BLK, 128 * i : 128 * i + 128]

        for i in range(LINE):
            for e in range(3):
                early, late = (pltpu.roll(tile(i, tp, 1, e), 64, 1) for tp in range(2))
                sums[i][0].append(tile(i, 0, 2, e) + jnp.where(second, early, 0.0))
                sums[i][1].append(tile(i, 1, 2, e) + jnp.where(second, late, early) + tile(i, 0, 0, e))
    for i in range(LINE):
        for tp in range(2):
            halves = [[], []]
            for b in range(3):
                e0, e1, e2 = sums[i][tp][3 * b : 3 * b + 3]
                halves[0].append(jnp.where(column > 0, pltpu.roll(e0, 1, 1), 0.0) + e1 + e2)
                halves[1].append(e0 + e1 + jnp.where(column < WL - 1, pltpu.roll(e2, 127, 1), 0.0))
            phases = [None] * 4
            for px in range(2):
                b0, b1, b2 = halves[px]
                phases[px] = jnp.where(row > 0, pltpu.roll(b0, WL, 1), 0.0) + b1 + b2
                phases[2 + px] = b0 + b1 + jnp.where(row < 3, pltpu.roll(b2, 128 - WL, 1), 0.0)
            outs[i][:, 128 * tp : 128 * tp + 128] = jnp.concatenate(phases, axis=0).astype(BF16)


def mid(fills, parts, w_in, gain_in):
    out = jax.ShapeDtypeStruct((4 * OUT_BLK, 256), BF16)
    return pl.pallas_call(
        mid_kernel,
        out_shape=[out] * LINE,
        in_specs=[VMEM()] * (PLANE + 3),
        out_specs=[VMEM()] * LINE,
        scratch_shapes=[
            pltpu.VMEM((LINE * LINE, 256), F32),
            pltpu.VMEM((LINE, 16, 256), F32),
            pltpu.VMEM((LINE, 288, 128), F32),
            pltpu.VMEM((LINE, 3, 6, 6, WL, 128), BF16),
            pltpu.VMEM((LINE * 256, C1), BF16),
            pltpu.VMEM((3, C1, 256), F32),
        ],
        compiler_params=pltpu.CompilerParams(vmem_limit_bytes=48 << 20),
        cost_estimate=cost(5),
        name="mid",
    )(fills, w_in, gain_in, *parts)


def regroup_kernel(half, near, far, out, rows):
    for b in range(3):
        at = OUT_BLK * b
        rows[at : at + 6, :] = half[8 * b : 8 * b + 6, :].astype(F32)
        rows[at + 6 : at + 18, :] = near[16 * b : 16 * b + 16, :].astype(F32)[:MID_SH]
        rows[at + 18 : at + 24, :] = far[8 * b : 8 * b + 6, :].astype(F32)
    out[...] = rows[...].astype(BF16)


def regroup(half, near, far):
    return pl.pallas_call(
        regroup_kernel,
        out_shape=jax.ShapeDtypeStruct((3 * OUT_BLK, WOUT_LANES), BF16),
        in_specs=[VMEM()] * 3,
        out_specs=VMEM(),
        scratch_shapes=[pltpu.VMEM((3 * OUT_BLK, WOUT_LANES), F32)],
        cost_estimate=cost(5),
        compiler_params=pltpu.CompilerParams(vmem_limit_bytes=32 << 20),
        name="regroup",
    )(half, near, far)


def prep_kernel(frames_hbm, assign_hbm, gmid_hbm, gout_hbm, *refs):
    parts, (raw, order_out, pick_out, gmid_out, gout_out, limit_out) = refs[:LINE], refs[LINE : LINE + 6]
    gmid_ref, gout_ref, frames, assign, sems = refs[LINE + 6 :]
    moves = [(gmid_hbm, gmid_ref), (gout_hbm, gout_ref), (frames_hbm, frames), (assign_hbm, assign)]
    loads = [pltpu.make_async_copy(src, dst, sems.at[i]) for i, (src, dst) in enumerate(moves)]
    for load in loads:
        load.start()
    z, q, c = place()
    for k in range(LINE):
        raw[3 * OUT_BLK * k : 3 * OUT_BLK * (k + 1), :] = parts[k][...]
    row, channel = iota((C2, C2), 0), iota((C2, C2), 1)
    side, step, in_shard = row // HALF_CH, row % HALF_CH // OUT_BLK, row % MID_SH
    flip = q ^ (2 * (c ^ side) + row % OUT_BLK // MID_SH)
    near = (flip == 1) | (flip == 2)
    holder = jnp.where(near, flip - 1, in_shard // 6)
    slot = jnp.where(near, 6 + in_shard, 6 * flip + in_shard % 6)
    held = (c ^ holder) * HALF_CH + step * OUT_BLK + slot
    order_out[...] = (channel == held).astype(F32).astype(BF16)
    r, l = iota((256, 256), 0), iota((256, 256), 1)
    same = (r // 8) == ((l // 64) % 2) * WL + l % WL
    mid_row = 2 * ((l // WL) % 4) + l // 128
    for b in range(3):
        pick_out[b] = (same & (mid_row == (c * 8 + r % 8 + b - 1) >> 1)).astype(F32).astype(BF16)
    for load in loads:
        load.wait()
    wanted = (2 * ((z - step) & (LINE - 1)) + (c ^ side)) * OUT_BLK + row % OUT_BLK
    column = jnp.sum(jnp.where(channel == wanted, gmid_ref[...], 0.0), axis=1, keepdims=True)
    gmid_out[...] = jnp.broadcast_to(column, (C2, 128))
    gout_out[...] = jnp.zeros((1, 128), F32)
    gout_out[:, :C3] = gout_ref[...]
    limit_out[...] = jnp.full((1, 128), frames[assign[z * PLANE + q]], jnp.int32).astype(F32)


def prep(frames, assign, gain_mid, gain_out, parts):
    return pl.pallas_call(
        prep_kernel,
        out_shape=[
            jax.ShapeDtypeStruct((LINE * 3 * OUT_BLK, WOUT_LANES), BF16),
            jax.ShapeDtypeStruct((C2, C2), BF16),
            jax.ShapeDtypeStruct((3, 256, 256), BF16),
            jax.ShapeDtypeStruct((C2, 128), F32),
            jax.ShapeDtypeStruct((1, 128), F32),
            jax.ShapeDtypeStruct((1, 128), F32),
        ],
        in_specs=[HBM()] * 4 + [VMEM()] * LINE,
        out_specs=[VMEM()] * 6,
        scratch_shapes=[
            pltpu.VMEM(gain_mid.shape, F32),
            pltpu.VMEM(gain_out.shape, F32),
            pltpu.SMEM(frames.shape, jnp.int32),
            pltpu.SMEM(assign.shape, jnp.int32),
            pltpu.SemaphoreType.DMA((4,)),
        ],
        cost_estimate=cost(0.01),
        compiler_params=pltpu.CompilerParams(vmem_limit_bytes=32 << 20),
        name="prep",
    )(*in_hbm(frames, assign, gain_mid, gain_out), *parts)


def wide_kernel(own, other, order, out, wf):
    wf[:, :, :, C3:] = jnp.zeros((3, 9, C2, 128 - C3), F32)
    for source, raw in enumerate((own, other)):
        for k in range(LINE):
            part = raw[72 * k : 72 * k + 72, :].astype(F32)
            at = (source * LINE + k) * OUT_BLK
            for j in range(9):
                tap = part[:, C3 * j : C3 * (j + 1)]
                for b in range(3):
                    wf[b, j, at : at + OUT_BLK, :C3] = tap[OUT_BLK * b : OUT_BLK * (b + 1)]
    for b in range(3):
        for j in range(9):
            moved = jnp.dot(order[...], wf[b, j].astype(BF16), preferred_element_type=F32)
            out[C2 * b : C2 * (b + 1), 128 * j : 128 * (j + 1)] = moved.astype(BF16)


def wide(own, other, order):
    return pl.pallas_call(
        wide_kernel,
        out_shape=jax.ShapeDtypeStruct((3 * C2, 1152), BF16),
        in_specs=[VMEM()] * 3,
        out_specs=VMEM(),
        scratch_shapes=[pltpu.VMEM((3, 9, C2, 128), F32)],
        cost_estimate=cost(0.01),
        compiler_params=pltpu.CompilerParams(vmem_limit_bytes=48 << 20),
        name="wide",
    )(own, other, order)


def stack_kernel(*refs):
    rows = refs[0].shape[0]
    for i, ref in enumerate(refs[:-1]):
        refs[-1][rows * i : rows * (i + 1), :] = ref[...]


def stack(parts, us=5):
    rows, lanes = parts[0].shape
    return pl.pallas_call(
        stack_kernel,
        out_shape=jax.ShapeDtypeStruct((len(parts) * rows, lanes), BF16),
        in_specs=[VMEM()] * len(parts),
        out_specs=VMEM(),
        cost_estimate=cost(us),
        compiler_params=pltpu.CompilerParams(vmem_limit_bytes=32 << 20),
        name="stack",
    )(*parts)


def out_kernel(own, other, w_all, pick, gmid_ref, gout_ref, limit_ref, out_hbm, hid, lhs, prod, out_ref, sems):
    for side, group in enumerate((own, other)):
        for k in range(LINE):
            part = group[96 * k : 96 * k + 96, :].astype(F32)
            at = (side * LINE + k) * OUT_BLK
            for p in range(4):
                for tp in range(2):
                    hid[p, tp, at : at + OUT_BLK, :] = part[OUT_BLK * p : OUT_BLK * (p + 1), 128 * tp : 128 * tp + 128]
    acts = []
    for p in range(4):
        halves = []
        for tp in range(2):
            h = hid[p, tp]
            scale = lax.rsqrt(jnp.sum(h * h, axis=0, keepdims=True) * (1.0 / C2) + 1e-6)
            halves.append(silu(h * scale * gmid_ref[...]).astype(BF16))
        acts.append(halves)
    for b in range(3):
        for tp in range(2):
            for px in range(2):
                src = jnp.concatenate([acts[2 * py + px][tp] for py in range(2)], axis=1)
                rows = dot_nt(pick[b], src).astype(BF16)
                for half in range(2):
                    lhs[2 * tp + half, px, :, C2 * b : C2 * b + C2] = rows[128 * half : 128 * half + 128]
    lane = iota((1, 8, 128), 2)
    limit = limit_ref[...]
    below = [lane < 128 - 32 * i for i in range(4)]
    def multiply(t):
        if t == 0:
            both = jnp.dot(lhs[0:2].reshape(512, 3 * C2), w_all[...], preferred_element_type=F32)
            prod[0:2] = both.reshape(2, 2, 128, 1152)
        elif t > 1:
            at = 384 * (t - 1)
            prod[t, :, :, at:] = jnp.dot(
                lhs[t].reshape(256, 3 * C2), w_all[:, at:], preferred_element_type=F32
            ).reshape(2, 128, 1152 - at)

    def combine(t):
        sums = []
        for px in range(2):
            row = []
            for e in range(3):
                total = None
                for a in range(3):
                    s = t + a - 2
                    if s < 0:
                        continue
                    at = 128 * (3 * a + e)
                    term = prod[s, px, :, at : at + 128].reshape(WL, 8, 128)
                    total = term if total is None else total + term
                row.append(total)
            sums.append(row)
        zero = jnp.zeros((1, 8, 128), F32)
        after = jnp.concatenate([sums[0][2][1:], zero], axis=0)
        before = jnp.concatenate([zero, sums[1][0][:-1]], axis=0)
        outs = [
            before + sums[0][1] + sums[0][2],
            sums[0][0] + sums[0][1] + sums[1][2],
            sums[0][0] + sums[1][1] + sums[1][2],
            sums[1][0] + sums[1][1] + after,
        ]
        vals = []
        for i, o in enumerate(outs):
            scale = lax.rsqrt(jnp.sum(o * o, axis=2, keepdims=True) * (1.0 / C3) + 1e-6)
            v = jnp.where(t < limit, silu(o * scale * gout_ref[...]), 0.0)
            vals.append(pltpu.roll(v, 128 - 32 * i, 2) if i else v)
        tiles = [
            jnp.where(lane < 96, vals[0], vals[1]),
            jnp.where(lane < 64, vals[1], vals[2]),
            jnp.where(lane < 32, vals[2], vals[3]),
        ]
        for x in range(WL):
            both = jnp.concatenate([tile[x] for tile in tiles], axis=1)
            out_ref[0, t, :, 384 * x : 384 * x + 384] = both.astype(BF16)

    copies = [pltpu.make_async_copy(out_ref.at[:, t], out_hbm.at[:, t], sems.at[t]) for t in range(FMAX)]
    multiply(0)
    multiply(2)
    combine(0)
    copies[0].start()
    multiply(3)
    combine(1)
    copies[1].start()
    combine(2)
    copies[2].start()
    combine(3)
    copies[3].start()
    for copy in copies:
        copy.wait()


def finish(*rest):
    return pl.pallas_call(
        out_kernel,
        out_shape=jax.ShapeDtypeStruct((1, FMAX, 4 * RL, 4 * WL * C3), BF16),
        in_specs=[VMEM()] * len(rest),
        out_specs=HBM(),
        scratch_shapes=[
            pltpu.VMEM((4, 2, C2, 128), F32),
            pltpu.VMEM((4, 2, 128, 3 * C2), BF16),
            pltpu.VMEM((4, 2, 128, 1152), F32),
            pltpu.VMEM((1, FMAX, 4 * RL, 4 * WL * C3), BF16),
            pltpu.SemaphoreType.DMA((FMAX,)),
        ],
        compiler_params=pltpu.CompilerParams(vmem_limit_bytes=48 << 20),
        cost_estimate=cost(4.8),
        name="finish",
    )(*rest)


def along_z(value, step):
    return lax.ppermute(value, "grp", [(g, (g + PLANE * step) % (LINE * PLANE)) for g in range(LINE * PLANE)])


def in_plane(value, flip):
    return lax.ppermute(value, "grp", [(g, g ^ flip) for g in range(LINE * PLANE)])


def near_chip(value):
    pairs = [(2 * g + c, 2 * (g ^ (1 + c)) + c) for g in range(LINE * PLANE) for c in range(2)]
    return lax.ppermute(value, ("grp", "row"), pairs)


def other_core(value):
    return lax.ppermute(value, "row", [(0, 1), (1, 0)])


def per_device_fast(latents, frames, offsets, assign, w_in, w_mid, w_out, gain_in, gain_mid, gain_out):
    core = lax.axis_index("row")
    w_in = w_in.transpose(1, 0, 2).reshape(27 * ZC, C1)
    *pieces, w_in, fills = pack(offsets, assign, jnp.transpose(w_mid, (1, 0, 2)), latents, w_in, frames)
    pieces = [pieces[0]] + [along_z(pieces[k], k) for k in range(1, LINE)]
    parts = join(pieces)
    parts = [parts[0]] + [in_plane(parts[d], d) for d in range(1, PLANE)]
    full = w_out.reshape(MID_SH, 3, 3, 3, C3).transpose(2, 0, 1, 3, 4).reshape(3, MID_SH, 9 * C3)
    half = lax.dynamic_slice_in_dim(full, core * 6, 6, axis=1)
    full = jnp.pad(full, ((0, 0), (0, 16 - MID_SH), (0, WOUT_LANES - 9 * C3))).reshape(48, WOUT_LANES)
    half = jnp.pad(half, ((0, 0), (0, 2), (0, WOUT_LANES - 9 * C3))).reshape(24, WOUT_LANES)
    plane = regroup(half, near_chip(full), in_plane(half, 3))
    own = [plane] + [along_z(plane, k) for k in range(1, LINE)]
    hidden = mid(fills, parts, w_in, gain_in[None, :])
    own, _ = lax.optimization_barrier((own, hidden[0]))
    raw, order, pick, gmid, gout, limit = prep(frames, assign, gain_mid[None, :], gain_out[None, :], own)
    w_last = wide(raw, other_core(raw), order)
    hidden = stack([hidden[0]] + [along_z(hidden[k], k) for k in range(1, LINE)], 30)
    return finish(hidden, other_core(hidden), w_last, pick, gmid, gout, limit)


def solution(mesh):
    fast = mesh.shape["grp"] == LINE * PLANE and mesh.shape["row"] == 2
    placed = (
        P("grp", None),
        P(),
        P(),
        P(),
        P(),
        P("grp", None, None),
        P("grp", None, None),
        P(),
        P(),
        P(),
    )
    return jax.shard_map(
        per_device_fast if fast else per_device_general,
        mesh=mesh,
        in_specs=placed,
        out_specs=P("grp", None, "row", None),
        check_vma=False,
    )
```
